32 devices in a mesh: dp: 4 (over z), chan: 2 (over y), hid: 4 (over x, core).
Axes of the slice: x: 2, y: 2, z: 4, core: 2. Of those that a mesh axis runs over, the one named last changes fastest.
Arguments:
- patches: bfloat16 [96, 196, 768], P(('dp', 'hid'), None, 'chan'), may hold values from -6 to 6
- cotangent: bfloat16 [96, 196, 768], P(('dp', 'hid'), None, 'chan'), may hold values from -6 to 6
- live_images: int32 [16], P(('dp', 'hid')), may hold values from 3 to 6, as said below
- first_gain: bfloat16 [768], P('chan'), may hold values from 0.099609375 to 1.8984375
- first_shift: bfloat16 [768], P('chan'), may hold values from -2 to 2
- token_up: bfloat16 [196, 384], replicated, may hold values from -0.4375 to 0.4375
- token_up_bias: bfloat16 [384], replicated, may hold values from -3 to 3
- token_down: bfloat16 [384, 196], replicated, may hold values from -0.3125 to 0.3125
- token_down_bias: bfloat16 [196], replicated, may hold values from -2 to 2
- second_gain: bfloat16 [768], P('chan'), may hold values from 0.099609375 to 1.8984375
- second_shift: bfloat16 [768], P('chan'), may hold values from -2 to 2
- chan_up: bfloat16 [768, 3072], P(None, 'hid'), may hold values from -0.21875 to 0.21875
- chan_up_bias: bfloat16 [3072], P('hid'), may hold values from -3 to 3
- chan_down: bfloat16 [3072, 768], P('hid', 'chan'), may hold values from -0.109375 to 0.109375
- chan_down_bias: bfloat16 [768], P('chan'), may hold values from -2 to 2
Outputs:
- mixed: bfloat16 [96, 196, 768], P(('dp', 'hid'), None, 'chan')
- input_grad: bfloat16 [96, 196, 768], P(('dp', 'hid'), None, 'chan')
- grad_first_gain: float32 [768], P('chan')
- grad_first_shift: float32 [768], P('chan')
- grad_token_up: float32 [196, 384], replicated
- grad_token_up_bias: float32 [384], replicated
- grad_token_down: float32 [384, 196], replicated
- grad_token_down_bias: float32 [196], replicated
- grad_second_gain: float32 [768], P('chan')
- grad_second_shift: float32 [768], P('chan')
- grad_chan_up: float32 [768, 3072], P(None, 'hid')
- grad_chan_up_bias: float32 [3072], P('hid')
- grad_chan_down: float32 [3072, 768], P('hid', 'chan')
- grad_chan_down_bias: float32 [768], P('chan')
The draws below stay inside these ranges and needn't reach their ends.
Inputs may be any that keep to these rules, and one draw needn't show every extreme that they name: Each group holds live_images[g] real images in its first slots, the rest are padding; some group is full and some holds exactly 3 images.
All inputs are finite; a program needn't handle non-finite values.
Results may differ from the reference program's by a relative error of at most 0.0065.
Values may be sent and summed in bfloat16 or wider, within the bound.
A program may use at most 192 MiB of HBM per device.

```python
import jax
import jax.numpy as jnp
from jax import lax

D = 768
S = 196
DS = 384
FF = 3072
IMG_DEV = 6
GROUPS = 16
IMAGES = 96


def draw_live_images(key, part):
    key = jax.random.fold_in(key, 11)
    first, second = jax.random.split(key)
    least = max(1, IMG_DEV // 2)
    counts = jax.random.randint(first, (GROUPS,), least, IMG_DEV + 1)
    picks = jax.random.permutation(second, GROUPS)
    counts = counts.at[picks[0]].set(IMG_DEV).at[picks[1]].set(least)
    return counts.astype(jnp.int32)


def level_of(key, extent, pieces, smallest, top_value):
    def one(position, parts):
        draws = jax.random.uniform(jax.random.fold_in(jax.random.fold_in(key, 6), position), (parts,), jnp.float32, smallest / len(pieces), top_value / len(pieces))
        return jnp.repeat(jnp.exp(draws), extent[position] // parts).reshape((-1,) + (1,) * (len(extent) - position - 1))

    loudness = one(*pieces[0])
    for cut in pieces[1:]:
        loudness = loudness * one(*cut)
    return loudness


def bell_draw(rng, extent, width, most, pieces=(), kind=jnp.bfloat16):
    level = level_of(rng, extent, pieces, -0.22, 0.18) if pieces else 1.0
    array = jax.random.normal(rng, extent, jnp.float32) * width * level
    return jnp.minimum(jnp.maximum(array, -most), most).astype(kind)


def setup_inputs(seed: int = 0) -> dict:
    splits = jax.random.split(jax.random.key(seed), 16)
    return {
        "patches": bell_draw(splits[0], (IMAGES, S, D), 1.0, 6.0, ((0, 16), (2, 2))),
        "cotangent": bell_draw(splits[1], (IMAGES, S, D), 1.0, 6.0, ((0, 16), (2, 2))),
        "live_images": draw_live_images(jax.random.fold_in(splits[15], 71), 0),
        "first_gain": jnp.clip(1.0 + 0.18 * jax.random.normal(splits[3], (D,), jnp.float32), 0.099609375, 1.8984375).astype(jnp.bfloat16),
        "first_shift": bell_draw(splits[4], (D,), 0.3, 2.0, ((0, 2),)),
        "token_up": bell_draw(splits[5], (S, DS), S ** -0.5, 0.4375),
        "token_up_bias": bell_draw(splits[6], (DS,), 0.5, 3.0),
        "token_down": bell_draw(splits[7], (DS, S), DS ** -0.5, 0.3125),
        "token_down_bias": bell_draw(splits[8], (S,), 0.3, 2.0),
        "second_gain": jnp.clip(1.0 + 0.18 * jax.random.normal(splits[9], (D,), jnp.float32), 0.099609375, 1.8984375).astype(jnp.bfloat16),
        "second_shift": bell_draw(splits[10], (D,), 0.3, 2.0, ((0, 2),)),
        "chan_up": bell_draw(splits[11], (D, FF), D ** -0.5, 0.21875, ((1, 4),)),
        "chan_up_bias": bell_draw(splits[12], (FF,), 0.5, 3.0, ((0, 4),)),
        "chan_down": bell_draw(splits[13], (FF, D), FF ** -0.5, 0.109375, ((0, 4), (1, 2))),
        "chan_down_bias": bell_draw(splits[14], (D,), 0.3, 2.0, ((0, 2),)),
    }


EPS = 1e-06
HIGH = lax.Precision.HIGHEST

@jax.custom_vjp
def low(v):
    return lax.optimization_barrier(v.astype(jnp.bfloat16)).astype(jnp.float32)

@jax.custom_vjp
def low_back(v):
    return v

def low_keep(v):
    return (low(v), None)

def low_pass(kept, grad):
    return (grad,)

def back_keep(v):
    return (v, None)

def back_low(kept, grad):
    return (low(grad),)
low.defvjp(low_keep, low_pass)
low_back.defvjp(back_keep, back_low)

def layer_norm(values, gain, shift):
    mean = lax.optimization_barrier(jnp.mean(values, -1, keepdims=True))
    spread = lax.optimization_barrier(jnp.mean(values * values, -1, keepdims=True)) - mean * mean
    return (values - mean) * lax.rsqrt(spread + EPS) * gain + shift

def block_forward(block, keep, params):
    first_gain, first_shift, token_up, token_up_bias, token_down, token_down_bias, second_gain, second_shift, chan_up, chan_up_bias, chan_down, chan_down_bias = params
    token_in = low(layer_norm(block, first_gain, first_shift))
    token_pre = low_back(jnp.einsum('bpc,pk->bkc', token_in, token_up, precision=HIGH) + token_up_bias[None, :, None])
    token_hidden = low(jax.nn.gelu(token_pre))
    token_out = low_back(jnp.einsum('bkc,kp->bpc', token_hidden, token_down, precision=HIGH) + token_down_bias[None, :, None])
    mixed_once = block + token_out
    chan_in = low(layer_norm(mixed_once, second_gain, second_shift))
    chan_pre = low_back(jnp.einsum('bpc,cf->bpf', chan_in, chan_up, precision=HIGH) + chan_up_bias)
    chan_hidden = low(jax.nn.gelu(chan_pre))
    chan_out = low_back(jnp.einsum('bpf,fc->bpc', chan_hidden, chan_down, precision=HIGH) + chan_down_bias)
    return keep[:, None, None] * (mixed_once + chan_out)

def reference(patches, cotangent, live_images, first_gain, first_shift, token_up, token_up_bias, token_down, token_down_bias, second_gain, second_shift, chan_up, chan_up_bias, chan_down, chan_down_bias):
    params = tuple((p.astype(jnp.float32) for p in (first_gain, first_shift, token_up, token_up_bias, token_down, token_down_bias, second_gain, second_shift, chan_up, chan_up_bias, chan_down, chan_down_bias)))
    keep_all = (jnp.arange(IMG_DEV, dtype=jnp.int32)[None, :] < live_images[:, None]).astype(jnp.float32)
    blocks = patches.astype(jnp.float32).reshape(GROUPS, IMG_DEV, S, D)
    backs = cotangent.astype(jnp.float32).reshape(GROUPS, IMG_DEV, S, D)

    def step(totals, item):
        block, back_in, keep = item
        result, pullback = jax.vjp(lambda b, *p: block_forward(b, keep, p), block, *params)
        grads = pullback(back_in)
        return (tuple((t + g for t, g in zip(totals, grads[1:]))), (result, grads[0]))
    start_totals = tuple((jnp.zeros(p.shape, jnp.float32) for p in params))
    totals, (results, input_grads) = lax.scan(step, start_totals, (blocks, backs, keep_all))
    mixed = results.reshape(IMAGES, S, D).astype(jnp.bfloat16)
    input_grad = input_grads.reshape(IMAGES, S, D).astype(jnp.bfloat16)
    return (mixed, input_grad, totals[0], totals[1], totals[2], totals[3], totals[4], totals[5], totals[6], totals[7], totals[8], totals[9], totals[10], totals[11])
```

```python
import functools

import jax
import jax.numpy as jnp
from jax import lax
from jax.experimental import pallas as pl
from jax.experimental.pallas import tpu as pltpu
from jax.sharding import PartitionSpec as P

EPS = 1e-06
BF = jnp.bfloat16
F32 = jnp.float32
MESH = pl.DeviceIdType.MESH
TANH_A = 0.7978845608028654
TANH_B = TANH_A * 0.044715


def nn(left, right):
    return lax.dot_general(left, right, (((1,), (0,)), ((), ())), preferred_element_type=F32)


def nt(left, right):
    return lax.dot_general(left, right, (((1,), (1,)), ((), ())), preferred_element_type=F32)


def tn(left, right):
    return lax.dot_general(left, right, (((0,), (0,)), ((), ())), preferred_element_type=F32)


def gelu_pair(v):
    square = v * v
    tanh = jnp.tanh(v * (TANH_A + TANH_B * square))
    half = 0.5 + 0.5 * tanh
    value = v * half
    slope = half + value * (1.0 - tanh) * (TANH_A + 3.0 * TANH_B * square)
    return value, slope


def pad_rows(count):
    return -(-count // 16) * 16


class Sizes:
    def __init__(self, mesh_shape, patches, chan_up, token_up):
        self.dp = mesh_shape["dp"]
        self.chan = mesh_shape["chan"]
        self.hid = mesh_shape["hid"]
        self.xs = self.hid // 2
        self.images, self.s, self.l = patches
        self.ps = pad_rows(self.s + 1)
        self.d = 2 * self.l
        self.own = self.images // 2
        self.f = chan_up[1]
        self.ds = token_up[1]
        self.chunks = self.f // self.l
        self.plane = self.chan * self.hid
        groups = 3 + self.hid * self.chunks
        unit = 16 * self.plane
        self.vec_row = 2 * self.ps
        self.small = -(-(self.vec_row + 8 * groups) // unit) * unit
        self.groups = (self.small - self.vec_row) // 8
        self.piece = self.small // self.plane
        self.levels = self.dp.bit_length() - 1
        self.seg = 2 * self.l // self.dp
        assert self.chan == 2 and self.hid % 2 == 0 and self.images % 2 == 0
        assert 1 << self.levels == self.dp and self.f % self.l == 0 and self.ds == self.l


def kernel(
    o,
    live_ref, patches_ref, cot_ref, ut_ref, up_ref, dn_ref, dt_ref, tdb_ref, vec_ref, bias_ref, chan_up_ref, chan_down_ref,
    mixed_out, grad_out, gup_out, gdn_out, small_out,
    pat, cot, cot_in, stats, stats_in, means, tin, th, tslope, msend, mrecv, rows_m, rows_n, inv2, vec_in,
    xs_all, gs_all, w_up, w_dn, w_b, hid_s, pg_s, out_acc, ng_acc, xch_send, ng_in, out_in,
    blow, bl_send, mo_send, scaled, gacc, vecs,
    gb, rx, ry, tot, fin, rz, small_send, small_in, small_z,
    loc_sem, send_sem, recv_sem,
):
    z = lax.axis_index("dp")
    y = lax.axis_index("chan")
    h = lax.axis_index("hid")
    c = h % 2
    x = h // 2
    S, PS, L, OWN, IM, F = o.s, o.ps, o.l, o.own, o.images, o.f
    width = float(o.d)

    def dev(zz=None, yy=None, xx=None, cc=None):
        zz = z if zz is None else zz
        yy = y if yy is None else yy
        xx = x if xx is None else xx
        cc = c if cc is None else cc
        return (zz, yy, xx * 2 + cc)

    partner = dev(yy=1 - y)
    sibling = dev(cc=1 - c)
    counter = [0]

    def take(count=1):
        base = counter[0]
        counter[0] += count
        return base

    def remote(src, dst, device, index=None):
        index = take() if index is None else index
        return pltpu.make_async_remote_copy(
            src_ref=src, dst_ref=dst, send_sem=send_sem.at[index], recv_sem=recv_sem.at[index],
            device_id=device, device_id_type=MESH,
        )

    loads = []

    def load(src, dst):
        copy = pltpu.make_async_copy(src, dst, loc_sem.at[len(loads)])
        loads.append(copy)
        copy.start()
        return copy

    load_pat = load(patches_ref, pat)
    load_cot = load(cot_ref, cot)
    load_up0 = load(chan_up_ref.at[pl.ds(pl.multiple_of(y * L, L), L)], w_up.at[0, pl.ds(0, L)])
    load_up1 = load(chan_up_ref.at[pl.ds(pl.multiple_of((1 - y) * L, L), L)], w_up.at[0, pl.ds(L, L)])
    load_dn = load(chan_down_ref, w_dn.at[0, :, pl.ds(0, L)])
    load_b = load(bias_ref, w_b.at[0])

    pad = PS - S
    pad_row = lax.broadcasted_iota(jnp.int32, (pad, L), 0)
    one_row = jnp.where(pad_row == 0, 1.0, 0.0).astype(BF)
    for j in range(IM):
        tin[j, S:PS, :] = one_row
    xs_all[...] = jnp.zeros(xs_all.shape, BF)
    gs_all[...] = jnp.zeros(gs_all.shape, BF)
    rows_n[...] = jnp.zeros(rows_n.shape, F32)
    rows_m[...] = jnp.zeros(rows_m.shape, F32)
    inv2[...] = jnp.zeros(inv2.shape, F32)
    stats[...] = jnp.zeros(stats.shape, F32)
    msend[...] = jnp.zeros(msend.shape, BF)
    mo_send[...] = jnp.zeros(mo_send.shape, BF)
    vecs[...] = jnp.zeros(vecs.shape, F32)
    gacc[...] = jnp.zeros(gacc.shape, F32)

    barrier = pltpu.get_barrier_semaphore()
    here = y * o.hid + h
    for step in range(1, o.plane):
        there = (here + step) % o.plane
        pl.semaphore_signal(barrier, inc=1, device_id=(z, there // o.hid, there % o.hid), device_id_type=MESH)
    for step in range(1, o.dp):
        pl.semaphore_signal(barrier, inc=1, device_id=((z + step) % o.dp, y, h), device_id_type=MESH)
    pl.semaphore_wait(barrier, o.plane - 1 + o.dp - 1)

    lane = lax.broadcasted_iota(jnp.int32, (S, 128), 1)
    load_pat.wait()

    def sums_of(j, acc):
        v = pat[j].astype(F32)
        acc = jnp.where(lane == j, jnp.sum(v, -1, keepdims=True), acc)
        return jnp.where(lane == j + 64, jnp.sum(v * v, -1, keepdims=True), acc)

    stats[0, :S, :] = lax.fori_loop(0, IM, sums_of, jnp.zeros((S, 128), F32))
    copy_stats = remote(stats.at[0], stats_in.at[0], partner)
    copy_stats.start()
    copy_vec = remote(vec_ref, vec_in, partner)
    copy_vec.start()

    copy_dn = [None] * o.xs
    copy_dn2 = [None] * o.xs
    copy_up = [None] * o.xs
    copy_up2 = [None] * o.xs
    copy_b = [None] * o.xs
    mine_rows = pl.ds(pl.multiple_of(y * L, L), L)
    other_rows = pl.ds(pl.multiple_of((1 - y) * L, L), L)
    copy_dn2[0] = remote(chan_down_ref, w_dn.at[0, :, pl.ds(L, L)], partner)
    copy_dn2[0].start()
    copy_cot = remote(cot_ref.at[pl.ds((1 - y) * OWN, OWN)], cot_in, partner)
    copy_cot.start()
    for step in range(1, o.xs):
        there = (x + step) % o.xs
        copy_b[step] = remote(bias_ref, w_b.at[step], dev(xx=there))
        copy_up[step] = remote(chan_up_ref.at[mine_rows], w_up.at[step, pl.ds(0, L)], dev(xx=there))
        copy_up2[step] = remote(chan_up_ref.at[other_rows], w_up.at[step, pl.ds(L, L)], dev(xx=there))
        copy_dn[step] = remote(chan_down_ref, w_dn.at[step, :, pl.ds(0, L)], dev(xx=there))
        copy_dn2[step] = remote(chan_down_ref, w_dn.at[step, :, pl.ds(L, L)], dev(xx=there, yy=1 - y))
        for copy in (copy_b, copy_up, copy_up2, copy_dn, copy_dn2):
            copy[step].start()

    copy_stats.wait()
    total = (stats[0] + stats_in[0]) * (1.0 / width)
    inv = lax.rsqrt(pltpu.roll(total, 64, 1) - total * total + EPS)
    wide_lane = lax.broadcasted_iota(jnp.int32, (PS, 128), 1)
    means[...] = jnp.where(wide_lane < 64, total, pltpu.roll(inv, 64, 1))

    def column(ref_rows, j):
        return jnp.sum(jnp.where(lane == j, ref_rows, 0.0), -1, keepdims=True)

    first_gain = vec_ref[0:1, :]
    first_shift = vec_ref[1:2, :]

    def first_norm(j):
        table = means[:S, :]
        inv_one = column(table, j + 64)
        return (pat[j].astype(F32) - column(table, j)) * inv_one, inv_one

    def token_forward(j):
        normed, _ = first_norm(j)
        tin[j, :S, :] = (normed * first_gain + first_shift).astype(BF)
        value, slope = gelu_pair(nn(ut_ref[...], tin[j]))
        th[j] = value.astype(BF)
        tslope[j] = slope.astype(BF)
        back = nn(dt_ref[...], th[j])
        return pat[j].astype(F32) + back[:S] + tdb_ref[:S, :]

    mixed_sems = take(OWN)

    def copy_mixed(i):
        return remote(msend.at[i], mrecv.at[i], partner, mixed_sems + i)

    @pl.loop(0, OWN)
    def _(i):
        msend[i, :S, :] = token_forward((1 - y) * OWN + i).astype(BF)
        copy_mixed(i).start()

    @pl.loop(0, OWN)
    def _(i):
        rows_m[i, :S, :L] = token_forward(y * OWN + i)

    load_cot.wait()
    copy_cot.wait()
    live = live_ref[0]

    def keep_of(j):
        return jnp.where(j < live, 1.0, 0.0).astype(F32)

    @pl.loop(0, OWN)
    def _(i):
        keep = keep_of(y * OWN + i)
        gs_all[c, i, :S, :L] = (cot[y * OWN + i].astype(F32) * keep).astype(BF)
        gs_all[c, i, :S, L:] = (cot_in[i].astype(F32) * keep).astype(BF)

    copy_gs = remote(gs_all.at[c], gs_all.at[c], sibling)
    copy_gs.start()

    copy_vec.wait()
    both = [jnp.concatenate([vec_ref[k:k + 1, :], vec_in[k:k + 1, :]], axis=1) for k in range(2, 5)]
    second_gain, second_shift, down_bias = both
    row_sems = take(OWN)

    def copy_rows(i):
        return remote(xs_all.at[c, i], xs_all.at[c, i], sibling, row_sems + i)

    @pl.loop(0, OWN)
    def _(i):
        copy_mixed(i).wait()
        rows_m[i, :S, L:] = mrecv[i, :S, :].astype(F32)
        v = rows_m[i, :S, :]
        mean = jnp.sum(v, -1, keepdims=True) * (1.0 / width)
        spread = jnp.sum(v * v, -1, keepdims=True) * (1.0 / width) - mean * mean
        inv_two = lax.rsqrt(spread + EPS)
        normed = (v - mean) * inv_two
        inv2[i, :S, :] = inv_two
        rows_n[i, :S, :] = normed
        xs_all[c, i, :S, :] = (normed * second_gain + second_shift).astype(BF)
        copy_rows(i).start()

    rows = OWN * PS
    load_up0.wait()
    load_up1.wait()
    load_dn.wait()
    load_b.wait()
    copy_gs.wait()

    @pl.loop(0, OWN)
    def _(i):
        copy_rows(i).wait()

    order = [0] + list(range(1, o.xs))
    copy_gx = {}
    first = True
    for step in order:
        if step:
            copy_b[step].wait()
            copy_up[step].wait()
            copy_up2[step].wait()
            copy_dn[step].wait()
        copy_dn2[step].wait()
        for part in range(o.chunks):
            cols = pl.ds(part * L, L)

            def side(cc, total, first=first, step=step, cols=cols):
                xin = xs_all[cc].reshape(rows, o.d)
                gin = gs_all[cc].reshape(rows, o.d)
                value, slope = gelu_pair(nn(xin, w_up[step, :, cols]) + w_b[step, 0:1, cols])
                hidden = value.astype(BF)
                hid_s[cc] = hidden
                down = w_dn[step, cols, :]
                add_out = nn(hidden, down)
                pre = (nt(gin, down) * slope).astype(BF)
                pg_s[cc] = pre
                add_ng = nt(pre, w_up[step, :, cols])
                if first:
                    out_acc[cc] = add_out
                    ng_acc[cc] = add_ng
                else:
                    out_acc[cc] += add_out
                    ng_acc[cc] += add_ng
                return total + jnp.sum(pre.astype(F32), 0, keepdims=True)

            up_bias_grad = lax.fori_loop(0, 2, side, jnp.zeros((1, L), F32))
            owner = ((x + o.xs - step) % o.xs * 2 + c) * o.chunks + part
            vecs[3 + owner, 0:1, :] = up_bias_grad
            first = False
            for half in range(2):
                lanes = pl.ds(half * L, L)
                xin = xs_all[:, :, :, lanes].reshape(2 * rows, L)
                gin = gs_all[:, :, :, lanes].reshape(2 * rows, L)
                gb[step, part, half, 0] = tn(xin, pg_s[...].reshape(2 * rows, L)).astype(BF)
                gb[step, part, half, 1] = tn(hid_s[...].reshape(2 * rows, L), gin).astype(BF)
            if step:
                copy = remote(gb.at[step, part], rx.at[step - 1, part], dev(xx=(x + o.xs - step) % o.xs))
                copy.start()
                copy_gx[step, part] = copy

    xch_send[0] = ng_acc[1 - c].astype(BF)
    copy_ng = remote(xch_send.at[0], ng_in, sibling)
    copy_ng.start()
    xch_send[1] = out_acc[1 - c].astype(BF)
    copy_out = remote(xch_send.at[1], out_in, sibling)
    copy_out.start()

    res_sems = take(OWN)

    def copy_res(i):
        return remote(bl_send.at[i], blow.at[y * OWN + i], partner, res_sems + i)

    copy_ng.wait()

    def residual(i, sums):
        block = pl.ds(pl.multiple_of(i * PS, 16), PS)
        ng = ng_acc[c, block, :] + ng_in[block, :].astype(F32)
        normed = rows_n[i]
        back = gs_all[c, i].astype(F32)
        sums = (
            sums[0] + jnp.sum(ng * normed, 0, keepdims=True),
            sums[1] + jnp.sum(ng, 0, keepdims=True),
            sums[2] + jnp.sum(back, 0, keepdims=True),
        )
        q = ng * second_gain
        m1 = jnp.sum(q, -1, keepdims=True) * (1.0 / width)
        m2 = jnp.sum(q * normed, -1, keepdims=True) * (1.0 / width)
        res = (back + inv2[i] * (q - m1 - normed * m2)).astype(BF)
        bl_send[i] = res[:, L:]
        copy_res(i).start()
        blow[y * OWN + i] = res[:, :L]
        return sums

    zero = jnp.zeros((1, o.d), F32)
    sums = lax.fori_loop(0, OWN, residual, (zero, zero, zero))
    for k in range(3):
        vecs[0, 1 + 2 * k:2 + 2 * k, :] = jnp.where(y == 0, sums[k][:, :L], sums[k][:, L:])
        vecs[0, 2 + 2 * k:3 + 2 * k, :] = jnp.where(y == 0, sums[k][:, L:], sums[k][:, :L])

    copy_out.wait()
    mixed_sems2 = take(OWN)

    def copy_mo(i):
        return remote(mo_send.at[i], mixed_out.at[y * OWN + i], partner, mixed_sems2 + i)

    @pl.loop(0, OWN)
    def _(i):
        block = pl.ds(pl.multiple_of(i * PS, 16), PS)
        branch = out_acc[c, block, :] + out_in[block, :].astype(F32) + down_bias
        result = (keep_of(y * OWN + i) * (rows_m[i] + branch)).astype(BF)
        mo_send[i] = result[:, L:]
        copy_mo(i).start()
        mixed_out[y * OWN + i] = result[:, :L]

    ones = jnp.ones((16, L), BF)

    def token_backward(j, carry):
        acc, sum_gain, sum_shift, sum_bias = carry
        low = blow[j]
        grad = (nn(dn_ref[...], low) * tslope[j].astype(F32)).astype(BF)
        gacc[0] += nt(tin[j], grad)
        gacc[1] += nt(low, th[j])
        sum_bias = sum_bias + nt(ones, low)
        back = nn(up_ref[...], grad)[:S]
        normed, _ = first_norm(j)
        sum_gain = sum_gain + jnp.sum(back * normed, 0, keepdims=True)
        sum_shift = sum_shift + jnp.sum(back, 0, keepdims=True)
        back = back * first_gain
        scaled[j, :S, :] = back
        acc = jnp.where(lane == j, jnp.sum(back, -1, keepdims=True), acc)
        acc = jnp.where(lane == j + 64, jnp.sum(back * normed, -1, keepdims=True), acc)
        return acc, sum_gain, sum_shift, sum_bias

    carry = (jnp.zeros((S, 128), F32), jnp.zeros((1, L), F32), jnp.zeros((1, L), F32), jnp.zeros((16, PS), F32))
    carry = lax.fori_loop(0, OWN, lambda i, t: token_backward(y * OWN + i, t), carry)

    def later(i, t):
        copy_res(i).wait()
        return token_backward((1 - y) * OWN + i, t)

    acc, sum_gain, sum_shift, sum_bias = lax.fori_loop(0, OWN, later, carry)
    stats[1, :S, :] = acc
    copy_stats2 = remote(stats.at[1], stats_in.at[1], partner)
    copy_stats2.start()
    vecs[0, 0:1, :PS] = sum_bias[0:1, :]
    vecs[1 + y, 0:1, :] = sum_gain
    vecs[1 + y, 1:2, :] = sum_shift

    def piece(k):
        return pl.ds(pl.multiple_of(k * o.piece, 16), o.piece)

    small_send[0:PS, :] = gacc[0].astype(BF)
    small_send[PS:2 * PS, :] = gacc[1].astype(BF)
    small_send[o.vec_row:, :] = vecs[...].reshape(8 * o.groups, L).astype(BF)
    copy_small = []
    for step in range(1, o.plane):
        there = (here + step) % o.plane
        copy = remote(small_send.at[piece(there)], small_in.at[step - 1], (z, there // o.hid, there % o.hid))
        copy.start()
        copy_small.append(copy)

    copy_stats2.wait()
    means2 = (stats[1, :S, :] + stats_in[1, :S, :]) * (1.0 / width)

    @pl.loop(0, IM)
    def _(j):
        normed, inv_one = first_norm(j)
        grad = scaled[j, :S, :] - column(means2, j) - normed * column(means2, j + 64)
        grad_out[j, :S, :] = (blow[j, :S, :].astype(F32) + inv_one * grad).astype(BF)
        grad_out[j, S:, :] = jnp.zeros((PS - S, L), BF)

    for copy in copy_small:
        copy.wait()
    mine = small_send[piece(here), :].astype(F32)
    for step in range(1, o.plane):
        mine = mine + small_in[step - 1].astype(F32)
    small_z[z] = mine.astype(BF)
    copy_z = []
    for step in range(1, o.dp):
        copy = remote(small_z.at[z], small_z.at[z], ((z + step) % o.dp, y, h))
        copy.start()
        copy_z.append(copy)

    copy_gy = []
    for part in range(o.chunks):
        for step in range(1, o.xs):
            copy_gx[step, part].wait()
        for half in range(2):
            for kind in range(2):
                mine = gb[0, part, half, kind].astype(F32)
                for step in range(1, o.xs):
                    mine = mine + rx[step - 1, part, half, kind].astype(F32)
                gb[0, part, half, kind] = mine.astype(BF)
        copy = remote(gb.at[0, part, 1], ry.at[part], partner)
        copy.start()
        copy_gy.append(copy)

    for copy in copy_z:
        copy.wait()
    mine = small_z[0].astype(F32)
    for k in range(1, o.dp):
        mine = mine + small_z[k].astype(F32)
    small_out[piece(here), :] = mine.astype(BF)
    copy_sf = []
    for step in range(1, o.plane):
        there = (here + step) % o.plane
        copy = remote(small_out.at[piece(here)], small_out.at[piece(here)], (z, there // o.hid, there % o.hid))
        copy.start()
        copy_sf.append(copy)

    half_seg = o.dp // 2
    for part in range(o.chunks):
        copy_gy[part].wait()
        for kind in range(2):
            mine = gb[0, part, 0, kind].astype(F32) + ry[part, kind].astype(F32)
            for k in range(half_seg):
                tot[part, kind * half_seg + k] = mine[k * o.seg:(k + 1) * o.seg].astype(BF)
    start, count, used = 0, o.dp, 0
    spans = []
    for level in range(o.levels):
        bit = (z // (1 << level)) % 2
        peer = dev(zz=z + (1 - 2 * bit) * (1 << level))
        count //= 2
        keep_at, send_at = start + bit * count, start + (1 - bit) * count
        copies = []
        for part in range(o.chunks):
            copy = remote(tot.at[part, pl.ds(send_at, count)], rz.at[part, pl.ds(used, count)], peer)
            copy.start()
            copies.append(copy)
        for part in range(o.chunks):
            copies[part].wait()
            mine = tot[part, pl.ds(keep_at, count)].astype(F32) + rz[part, pl.ds(used, count)].astype(F32)
            (fin if count == 1 else tot)[part, pl.ds(keep_at, count)] = mine.astype(BF)
        spans.append((keep_at, count, peer))
        start = keep_at
        used += count
    for keep_at, count, peer in reversed(spans):
        copies = []
        for part in range(o.chunks):
            span = fin.at[part, pl.ds(keep_at, count)]
            copy = remote(span, span, peer)
            copy.start()
            copies.append(copy)
        for copy in copies:
            copy.wait()
    copies = []
    for part in range(o.chunks):
        copy = remote(fin.at[part, pl.ds(0, half_seg)], gup_out.at[part, y], partner)
        copy.start()
        copies.append(copy)
        gup_out[part, y] = fin[part, :half_seg]
        gdn_out[part] = fin[part, half_seg:]

    @pl.loop(0, OWN)
    def _(i):
        copy_mo(i).wait()

    for copy in copies + copy_sf:
        copy.wait()


def block_call(o, live, patches, cot, ut, up, dn, dt, tdb, vec, bias, chan_up, chan_down):
    I, S, PS, L, OWN, D, X, C = o.images, o.s, o.ps, o.l, o.own, o.d, o.xs, o.chunks
    half_seg = o.dp // 2
    any_spec = pl.BlockSpec(memory_space=pl.ANY)
    vmem = pl.BlockSpec(memory_space=pltpu.VMEM)
    rows = OWN * PS
    copies = 2 + 1 + 1 + 5 * (X - 1) + 3 * OWN + 1 + (X - 1) * C + 2 + OWN + 1
    copies += 2 * (o.plane - 1) + o.dp - 1 + C + 2 * o.levels * C + C + 8
    outs = [
        jax.ShapeDtypeStruct((I, PS, L), BF),
        jax.ShapeDtypeStruct((I, PS, L), BF),
        jax.ShapeDtypeStruct((C, 2, half_seg, o.seg, L), BF),
        jax.ShapeDtypeStruct((C, half_seg, o.seg, L), BF),
        jax.ShapeDtypeStruct((o.small, L), BF),
    ]
    scratch = [
        ((I, S, L), BF), ((I, S, L), BF), ((OWN, S, L), BF),
        ((2, PS, 128), F32), ((2, PS, 128), F32), ((PS, 128), F32),
        ((I, PS, L), BF), ((I, o.ds, L), BF), ((I, o.ds, L), BF),
        ((OWN, PS, L), BF), ((OWN, PS, L), BF),
        ((OWN, PS, D), F32), ((OWN, PS, D), F32), ((OWN, PS, 1), F32), ((8, L), F32),
        ((2, OWN, PS, D), BF), ((2, OWN, PS, D), BF),
        ((X, D, o.f), BF), ((X, o.f, D), BF), ((X, 8, o.f), F32),
        ((2, rows, L), BF), ((2, rows, L), BF), ((2, rows, D), F32), ((2, rows, D), F32),
        ((2, rows, D), BF), ((rows, D), BF), ((rows, D), BF),
        ((I, PS, L), BF), ((OWN, PS, L), BF), ((OWN, PS, L), BF), ((I, PS, L), F32),
        ((2, PS, L), F32), ((o.groups, 8, L), F32),
        ((X, C, 2, 2, L, L), BF), ((X - 1, C, 2, 2, L, L), BF), ((C, 2, L, L), BF),
        ((C, o.dp, o.seg, L), BF), ((C, o.dp, o.seg, L), BF), ((C, o.dp - 1, o.seg, L), BF),
        ((o.small, L), BF), ((o.plane - 1, o.piece, L), BF), ((o.dp, o.piece, L), BF),
    ]
    return pl.pallas_call(
        functools.partial(kernel, o),
        out_shape=outs,
        in_specs=[pl.BlockSpec(memory_space=pltpu.SMEM), any_spec, any_spec] + [vmem] * 7 + [any_spec] * 2,
        out_specs=[vmem] * 5,
        scratch_shapes=[pltpu.VMEM(shape, kind) for shape, kind in scratch]
        + [pltpu.SemaphoreType.DMA((8,)), pltpu.SemaphoreType.DMA((copies,)), pltpu.SemaphoreType.DMA((copies,))],
        compiler_params=pltpu.CompilerParams(
            collective_id=1, has_side_effects=True, vmem_limit_bytes=63 * 2**20
        ),
        name="mixer_block",
    )(live, patches, cot, ut, up, dn, dt, tdb, vec, bias, chan_up, chan_down)


def body(
    o,
    patches,
    cotangent,
    live_images,
    first_gain,
    first_shift,
    token_up,
    token_up_bias,
    token_down,
    token_down_bias,
    second_gain,
    second_shift,
    chan_up,
    chan_up_bias,
    chan_down,
    chan_down_bias,
):
    S, PS, L = o.s, o.ps, o.l
    rest = PS - S
    up = jnp.pad(token_up, ((0, rest), (0, 0)))
    ut = jnp.concatenate([token_up, token_up_bias[None], jnp.zeros((rest - 1, o.ds), BF)], 0).T
    dn = jnp.pad(token_down, ((0, 0), (0, rest)))
    dt = jnp.pad(token_down.T, ((0, rest), (0, 0)))
    tdb = jnp.pad(token_down_bias.astype(F32), (0, rest))[:, None]
    vec = jnp.stack([first_gain, first_shift, second_gain, second_shift, chan_down_bias] + [jnp.zeros((L,), BF)] * 3)
    bias = jnp.broadcast_to(chan_up_bias.astype(F32)[None], (8, o.f))
    mixed, grad, gup, gdn, small = block_call(
        o, live_images, patches, cotangent, ut, up, dn, dt, tdb, vec.astype(F32), bias, chan_up, chan_down
    )
    y = lax.axis_index("chan")
    h = lax.axis_index("hid")
    small = small.astype(F32)
    groups = small[o.vec_row:].reshape(o.groups, 8, L)

    def pick(at, row):
        return lax.dynamic_slice_in_dim(groups[:, row], at, 1, 0)[0]

    def pick_half(row):
        return lax.dynamic_slice_in_dim(groups[0], row + y, 1, 0)[0]

    return (
        mixed[:, :S],
        grad[:, :S],
        pick(1 + y, 0),
        pick(1 + y, 1),
        small[:S],
        small[S],
        small[PS:PS + S].T,
        groups[0, 0, :S],
        pick_half(1),
        pick_half(3),
        gup.reshape(o.chunks, 2, L, L).transpose(1, 2, 0, 3).reshape(o.d, o.f).astype(F32),
        lax.dynamic_slice_in_dim(groups[:, 0], 3 + h * o.chunks, o.chunks, 0).reshape(o.f),
        gdn.reshape(o.f, L).astype(F32),
        pick_half(5),
    )


def solution(mesh):
    in_specs = (
        P(("dp", "hid"), None, "chan"),
        P(("dp", "hid"), None, "chan"),
        P(("dp", "hid")),
        P("chan"),
        P("chan"),
        P(),
        P(),
        P(),
        P(),
        P("chan"),
        P("chan"),
        P(None, "hid"),
        P("hid"),
        P("hid", "chan"),
        P("chan"),
    )
    out_specs = (
        P(("dp", "hid"), None, "chan"),
        P(("dp", "hid"), None, "chan"),
        P("chan"),
        P("chan"),
        P(),
        P(),
        P(),
        P(),
        P("chan"),
        P("chan"),
        P(None, "hid"),
        P("hid"),
        P("hid", "chan"),
        P("chan"),
    )

    def whole(*args):
        shape = dict(mesh.shape)
        patches, token_up, chan_up = args[0].shape, args[5].shape, args[11].shape
        local = (patches[0] // (shape["dp"] * shape["hid"]), patches[1], patches[2] // shape["chan"])
        o = Sizes(shape, local, (chan_up[0], chan_up[1] // shape["hid"]), token_up)
        mapped = jax.shard_map(
            functools.partial(body, o), mesh=mesh, in_specs=in_specs, out_specs=out_specs, check_vma=False
        )
        return mapped(*args)

    return whole
```

```python
import functools

import jax
import jax.numpy as jnp
from jax import lax
from jax.experimental import pallas as pl
from jax.experimental.pallas import tpu as pltpu
from jax.sharding import PartitionSpec as P

EPS = 1e-06
BF = jnp.bfloat16
F32 = jnp.float32
MESH = pl.DeviceIdType.MESH
TANH_A = 0.7978845608028654
TANH_B = TANH_A * 0.044715


def nn(left, right):
    return lax.dot_general(left, right, (((1,), (0,)), ((), ())), preferred_element_type=F32)


def nt(left, right):
    return lax.dot_general(left, right, (((1,), (1,)), ((), ())), preferred_element_type=F32)


def tn(left, right):
    return lax.dot_general(left, right, (((0,), (0,)), ((), ())), preferred_element_type=F32)


def gelu_pair(v):
    square = v * v
    tanh = jnp.tanh(v * (TANH_A + TANH_B * square))
    half = 0.5 + 0.5 * tanh
    value = v * half
    slope = half + value * (1.0 - tanh) * (TANH_A + 3.0 * TANH_B * square)
    return value, slope


def pad_rows(count):
    return -(-count // 16) * 16


class Sizes:
    ways = (("xyz", "yxz"), ("zxy", "yxz"))
    plan = {
        ("M", 0, "grad"): ((0, 1),),
        ("O", 1, "side"): ((0, 0),),
        ("M", 1, "side"): ((0, 0), (0, 1), (1, 0)),
        ("M", 1, "grad"): ((1, 1), (1, 0)),
        ("residual",): ((0, 0), (0, 1)),
        ("token own",): ((1, 0),),
        ("token other",): ((0, 0), (0, 1), (1, 0), (1, 1)),
        ("norm",): ((0, 0), (0, 1), (1, 0), (1, 1)),
        ("end",): ("small", (0, 0), (0, 1), (1, 0), (1, 1)),
    }

    def __init__(self, mesh_shape, patches, chan_up, token_up):
        self.dp = mesh_shape["dp"]
        self.chan = mesh_shape["chan"]
        self.hid = mesh_shape["hid"]
        self.xs = self.hid // 2
        self.images, self.s, self.l = patches
        self.ps = pad_rows(self.s + 1)
        self.d = 2 * self.l
        self.own = self.images // 2
        self.f = chan_up[1]
        self.ds = token_up[1]
        self.chunks = self.f // self.l
        self.plane = self.chan * self.hid
        units = [(part, kind) for part in range(self.chunks) for kind in range(2)]
        self.firsts = [(part, kind) for part, kind in units if self.ways[part % 2][kind] == "zxy"]
        self.slots = [(part, kind, half) for part, kind in units for half in range(1 + ((part, kind) in self.firsts))]
        groups = 3 + self.hid * self.chunks
        unit = 16 * self.plane
        self.vec_row = 2 * self.ps
        self.small = -(-(self.vec_row + 8 * groups) // unit) * unit
        self.groups = (self.small - self.vec_row) // 8
        self.piece = self.small // self.plane
        self.levels = self.dp.bit_length() - 1
        self.seg = self.l // self.dp
        self.wide = -(-self.ps // 128) * 128
        assert self.images <= 8
        assert self.chan == 2 and self.hid % 2 == 0 and self.images % 2 == 0
        assert 1 << self.levels == self.dp and self.f % self.l == 0 and self.ds == self.l


def kernel(
    o,
    live_ref, patches_ref, cot_ref, ut_ref, up_ref, dn_ref, dt_ref, tdb_ref, vec_ref, bias_ref, chan_up_ref, chan_down_ref,
    mixed_out, grad_out, gup_out, gdn_out, small_out,
    pat, cot, cot_in, stats, stats_in, means, means2, tin, th, tslope, msend, mrecv, rows_m, rows_n, inv2, vec_in,
    xs_all, gs_all, w_up, w_dn, w_b, hid_s, pg_s, out_acc, ng_acc, xch_send, ng_in, out_in,
    blow, gacc, vecs,
    gm, gb, rx, yb, ry, ryo, zb, rz, rzo, fin_up, fin, small_send, small_in, small_z,
    loc_sem, send_sem, recv_sem,
):
    z = lax.axis_index("dp")
    y = lax.axis_index("chan")
    h = lax.axis_index("hid")
    c = h % 2
    x = h // 2
    S, PS, L, OWN, IM, X, C = o.s, o.ps, o.l, o.own, o.images, o.xs, o.chunks
    width = float(o.d)
    here = y * o.hid + h
    bit = z % 2
    half_l = L // 2

    def dev(zz=None, yy=None, xx=None, cc=None):
        zz = z if zz is None else zz
        yy = y if yy is None else yy
        xx = x if xx is None else xx
        cc = c if cc is None else cc
        return (zz, yy, xx * 2 + cc)

    partner = dev(yy=1 - y)
    sibling = dev(cc=1 - c)
    z_pair = dev(zz=z + 1 - 2 * bit)
    counter = [0]

    def take(count=1):
        base = counter[0]
        counter[0] += count
        return base

    def remote(src, dst, device, index=None):
        index = take() if index is None else index
        return pltpu.make_async_remote_copy(
            src_ref=src, dst_ref=dst, send_sem=send_sem.at[index], recv_sem=recv_sem.at[index],
            device_id=device, device_id_type=MESH,
        )

    def send(src, dst, device):
        copy = remote(src, dst, device)
        copy.start()
        return copy

    barrier = pltpu.get_barrier_semaphore()
    for step in range(1, o.plane):
        there = (here + step) % o.plane
        pl.semaphore_signal(barrier, inc=1, device_id=(z, there // o.hid, there % o.hid), device_id_type=MESH)
    for step in range(1, o.dp):
        pl.semaphore_signal(barrier, inc=1, device_id=((z + step) % o.dp, y, h), device_id_type=MESH)

    loads = []

    def load(src, dst):
        copy = pltpu.make_async_copy(src, dst, loc_sem.at[len(loads)])
        loads.append(copy)
        copy.start()
        return copy

    load_pat = load(patches_ref, pat)
    load_cot = load(cot_ref, cot)
    load_up0 = load(chan_up_ref.at[pl.ds(pl.multiple_of(y * L, L), L)], w_up.at[0, pl.ds(0, L)])
    load_up1 = load(chan_up_ref.at[pl.ds(pl.multiple_of((1 - y) * L, L), L)], w_up.at[0, pl.ds(L, L)])
    load_dn = load(chan_down_ref, w_dn.at[0, :, pl.ds(0, L)])
    load_b = load(bias_ref, w_b.at[0])

    pad = PS - S
    pad_row = lax.broadcasted_iota(jnp.int32, (pad, L), 0)
    one_row = jnp.where(pad_row == 0, 1.0, 0.0).astype(BF)
    for j in range(IM):
        tin[j, S:PS, :] = one_row
    for i in range(OWN):
        xs_all[c, i, S:PS, :] = jnp.zeros((pad, o.d), BF)
        gs_all[c, i, S:PS, :] = jnp.zeros((pad, o.d), BF)
        rows_n[i, S:PS, :] = jnp.zeros((pad, o.d), F32)
        rows_m[i, S:PS, :] = jnp.zeros((pad, o.d), F32)
        inv2[i, S:PS, :] = jnp.zeros((pad, 1), F32)
        msend[i, S:PS, :] = jnp.zeros((pad, L), BF)
    vecs[...] = jnp.zeros(vecs.shape, F32)
    gacc[...] = jnp.zeros(gacc.shape, F32)

    lane = lax.broadcasted_iota(jnp.int32, (S, 128), 1)
    load_pat.wait()

    def note(table, j, first, second):
        table = jnp.where(lane == j, first, table)
        return jnp.where(lane == j + 8, second, table)

    def across(table):
        rest = jnp.zeros((o.wide - S, 128), F32)
        return jnp.concatenate([table, rest], 0).T[:16]

    def along(table):
        return jnp.concatenate([table, jnp.zeros((112, o.wide), F32)], 0).T

    def sums_of(j, table):
        v = pat[j].astype(F32)
        return note(table, j, jnp.sum(v, -1, keepdims=True), jnp.sum(v * v, -1, keepdims=True))

    stats[0] = across(lax.fori_loop(0, IM, sums_of, jnp.zeros((S, 128), F32)))

    pl.semaphore_wait(barrier, o.plane - 1 + o.dp - 1)

    copy_stats = send(stats.at[0], stats_in.at[0], partner)
    copy_vec = send(vec_ref, vec_in, partner)
    near = pl.ds(bit * L, L)
    near_from = pl.ds(pl.multiple_of(((y + bit) % 2) * L, L), L)
    copy_b = {step: send(bias_ref, w_b.at[step], dev(xx=(x + step) % X)) for step in range(1, X)}
    copy_w = {}
    copy_f = {}

    def weight_spans(step, part):
        cols = pl.ds(part * L, L)
        rows_dn = pl.ds(pl.multiple_of(part * L + bit * half_l, 16), half_l)
        return (
            (chan_up_ref.at[near_from, cols], w_up.at[step, near, cols], y),
            (chan_down_ref.at[rows_dn], w_dn.at[step, rows_dn, pl.ds(0, L)], y),
            (chan_down_ref.at[rows_dn], w_dn.at[step, rows_dn, pl.ds(L, L)], 1 - y),
        )

    def fetch(part, which):
        for step in range(1, X):
            for n in which:
                src, dst, yy = weight_spans(step, part)[n]
                copy_w[step, part, n] = send(src, dst, dev(xx=(x + step) % X, yy=yy))

    def hand_on(part, which):
        for step in range(1, X):
            for n in which:
                dst = weight_spans(step, part)[n][1]
                copy_w[step, part, n].wait()
                copy_f[step, part, n] = send(dst, dst, z_pair)

    fetch(0, (0,))
    copy_cot = send(cot_ref.at[pl.ds((1 - y) * OWN, OWN)], cot_in, partner)
    fetch(0, (1, 2))

    copy_stats.wait()
    total = (stats[0] + stats_in[0]) * (1.0 / width)
    mean, square = total[:8], total[8:]
    means[...] = along(jnp.concatenate([mean, lax.rsqrt(square - mean * mean + EPS)], 0))

    def column(table, j):
        return jnp.sum(jnp.where(lane == j, table, 0.0), -1, keepdims=True)

    first_gain = vec_ref[0:1, :]
    first_shift = vec_ref[1:2, :]

    def first_norm(j):
        table = means[:S, :]
        inv_one = column(table, j + 8)
        return (pat[j].astype(F32) - column(table, j)) * inv_one, inv_one

    def token_forward(j):
        normed, _ = first_norm(j)
        tin[j, :S, :] = (normed * first_gain + first_shift).astype(BF)
        value, slope = gelu_pair(nn(ut_ref[...], tin[j]))
        th[j] = value.astype(BF)
        tslope[j] = slope.astype(BF)
        back = nn(dt_ref[...], th[j])
        return pat[j].astype(F32) + back[:S] + tdb_ref[:S, :]

    mixed_sems = take(OWN)

    def copy_mixed(i):
        return remote(msend.at[i], mrecv.at[i], partner, mixed_sems + i)

    @pl.loop(0, OWN)
    def _(i):
        msend[i, :S, :] = token_forward((1 - y) * OWN + i).astype(BF)
        copy_mixed(i).start()

    @pl.loop(0, OWN)
    def _(i):
        rows_m[i, :S, :L] = token_forward(y * OWN + i)

    hand_on(0, (0,))
    load_cot.wait()
    copy_cot.wait()
    live = live_ref[0]

    def keep_of(j):
        return jnp.where(j < live, 1.0, 0.0).astype(F32)

    @pl.loop(0, OWN)
    def _(i):
        keep = keep_of(y * OWN + i)
        gs_all[c, i, :S, :L] = (cot[y * OWN + i].astype(F32) * keep).astype(BF)
        gs_all[c, i, :S, L:] = (cot_in[i].astype(F32) * keep).astype(BF)

    copy_gs = send(gs_all.at[c], gs_all.at[c], sibling)
    hand_on(0, (1, 2))
    for part in range(1, C):
        fetch(part, (0, 1))

    copy_vec.wait()
    both = [jnp.concatenate([vec_ref[n:n + 1, :], vec_in[n:n + 1, :]], axis=1) for n in range(2, 5)]
    second_gain, second_shift, down_bias = both
    row_sems = take(OWN)

    def copy_rows(i):
        return remote(xs_all.at[c, i], xs_all.at[c, i], sibling, row_sems + i)

    @pl.loop(0, OWN)
    def _(i):
        copy_mixed(i).wait()
        rows_m[i, :S, L:] = mrecv[i, :S, :].astype(F32)
        v = rows_m[i, :S, :]
        mean = jnp.sum(v, -1, keepdims=True) * (1.0 / width)
        spread = jnp.sum(v * v, -1, keepdims=True) * (1.0 / width) - mean * mean
        inv_two = lax.rsqrt(spread + EPS)
        normed = (v - mean) * inv_two
        inv2[i, :S, :] = inv_two
        rows_n[i, :S, :] = normed
        xs_all[c, i, :S, :] = (normed * second_gain + second_shift).astype(BF)
        copy_rows(i).start()

    for part in range(1, C):
        fetch(part, (2,))
    copy_dn2 = {}

    def fetch_dn2(part):
        span = pl.ds(part * L, L)
        copy_dn2[part] = send(chan_down_ref.at[span], w_dn.at[0, span, pl.ds(L, L)], partner)

    fetch_dn2(0)
    load_up0.wait()
    load_up1.wait()
    load_dn.wait()
    load_b.wait()
    copy_gs.wait()
    for part in range(1, C):
        hand_on(part, (0, 1))

    @pl.loop(0, OWN)
    def _(i):
        copy_rows(i).wait()

    ready = {}

    def levels():
        start, count, used = 0, o.dp, 0
        for level in range(o.levels):
            side_bit = (z // (1 << level)) % 2
            peer = dev(zz=z + (1 - 2 * side_bit) * (1 << level))
            count //= 2
            yield start + side_bit * count, start + (1 - side_bit) * count, count, used, peer
            start = start + side_bit * count
            used += count

    def add(part, kind, half, span, *terms):
        mine = gm[part, kind, half, span]
        for term in terms:
            mine = mine + term.astype(F32)
        gm[part, kind, half, span] = mine

    everything = pl.ds(0, o.dp)

    def gather(part, kind):
        halves = 2 if kind == 0 else 1
        done = fin_up if kind == 0 else fin
        own = pl.ds(my_segment(), 1)
        done[part, 0, own] = gm[part, kind, 0, own].astype(BF)
        if kind == 0:
            copy = send(fin_up.at[part, 0, own], fin_up.at[part, 1, own], partner)
            yield
            copy.wait()
        for keep_at, _, count, _, peer in reversed(list(levels())):
            copies = []
            for half in range(halves):
                span = done.at[part, half, pl.ds(keep_at, count)]
                copies.append(send(span, span, peer))
            yield
            for copy in copies:
                copy.wait()
        if kind == 0:
            gup_out[part, y] = fin_up[part, 0]
            gup_out[part, 1 - y] = fin_up[part, 1]
        else:
            gdn_out[part] = fin[part, 0]

    def slot(part, kind, half):
        return o.slots.index((part, kind, half))

    def reduce_z(part, kind, halves):
        for keep_at, send_at, count, used, peer in levels():
            span = pl.ds(used, count)
            copies = []
            for half in range(halves):
                here_z = slot(part, kind, half)
                zb[here_z, span] = gm[part, kind, half, pl.ds(send_at, count)].astype(BF)
                copies.append(send(zb.at[here_z, span], rz.at[here_z, span], peer))
            yield
            for half in range(halves):
                copies[half].wait()
                add(part, kind, half, pl.ds(keep_at, count), rz[slot(part, kind, half), span])

    def my_segment():
        return list(levels())[-1][0]

    def chunk_xyz(part, kind):
        copies = [send(gb.at[n, part, kind], rx.at[n, part, kind], dev(xx=(x + X - 1 - n) % X)) for n in range(X - 1)]
        yield
        for n in range(X - 1):
            copies[n].wait()
        for half in (1, 0):
            add(part, kind, half, everything, *[rx[n, part, kind, half] for n in range(X - 1)])
            if half:
                yb[part, kind] = gm[part, kind, 1].astype(BF)
                copy = send(yb.at[part, kind], ry.at[part, kind], partner)
        yield
        copy.wait()
        add(part, kind, 0, everything, ry[part, kind])
        yield from reduce_z(part, kind, 1)
        yield from gather(part, kind)

    def chunk_yxz(part, kind):
        copies = [send(gb.at[n, part, kind, 1], ryo.at[n, part, kind], partner) for n in range(X - 1)]
        yield
        for n in range(X - 1):
            copies[n].wait()
            mine = gb[n, part, kind, 0].astype(F32) + ryo[n, part, kind].astype(F32)
            gb[n, part, kind, 0] = mine.astype(BF)
            copies[n] = send(gb.at[n, part, kind, 0], rx.at[n, part, kind, 0], dev(xx=(x + X - 1 - n) % X))
        yb[part, kind] = gm[part, kind, 1].astype(BF)
        copy = send(yb.at[part, kind], ry.at[part, kind], partner)
        yield
        copy.wait()
        for n in range(X - 1):
            copies[n].wait()
        add(part, kind, 0, everything, ry[part, kind], *[rx[n, part, kind, 0] for n in range(X - 1)])
        yield from reduce_z(part, kind, 1)
        yield from gather(part, kind)

    def chunk_zxy(part, kind):
        for keep_at, send_at, count, used, peer in levels():
            copies = {}
            span = pl.ds(used, count)
            for n in range(X - 1):
                for half in range(2):
                    src = gb.at[n, part, kind, half, pl.ds(send_at, count)]
                    copies[n, half] = send(src, rzo.at[n, o.firsts.index((part, kind)), half, span], peer)
            yield
            for n in range(X - 1):
                for half in range(2):
                    copies[n, half].wait()
                    keep = pl.ds(keep_at, count)
                    mine = gb[n, part, kind, half, keep].astype(F32) + rzo[n, o.firsts.index((part, kind)), half, span].astype(F32)
                    gb[n, part, kind, half, keep] = mine.astype(BF)
        at = pl.ds(my_segment(), 1)
        copies = []
        for n in range(X - 1):
            span = gb.at[n, part, kind, :, at]
            copies.append(send(span, rx.at[n, part, kind, :, at], dev(xx=(x + X - 1 - n) % X)))
        yield from reduce_z(part, kind, 2)
        for copy in copies:
            copy.wait()
        for half in (1, 0):
            add(part, kind, half, at, *[rx[n, part, kind, half, at] for n in range(X - 1)])
            if half:
                yb[part, kind, at] = gm[part, kind, 1, at].astype(BF)
                copy = send(yb.at[part, kind, at], ry.at[part, kind, at], partner)
        yield
        copy.wait()
        add(part, kind, 0, at, ry[part, kind, at])
        yield from gather(part, kind)

    pipes = {}

    def begin(part, kind):
        pipes[part, kind] = o.ways[part % len(o.ways)][kind]
        pipes[part, kind] = {"xyz": chunk_xyz, "yxz": chunk_yxz, "zxy": chunk_zxy}[pipes[part, kind]](part, kind)
        step_of((part, kind))

    def step_of(name):
        if name in pipes:
            try:
                next(pipes[name])
            except StopIteration:
                del pipes[name]

    def at(*point):
        for name in o.plan.get(point, ()):
            step_of(name)

    rows = OWN * PS
    first = True

    def weight_grad(kind, half):
        lanes = pl.ds(half * L, L)
        if kind == 0:
            grad = tn(xs_all[:, :, :, lanes].reshape(2 * rows, L), pg_s[...].reshape(2 * rows, L))
        else:
            grad = tn(hid_s[...].reshape(2 * rows, L), gs_all[:, :, :, lanes].reshape(2 * rows, L))
        return grad.reshape(o.dp, o.seg, L)

    for part in range(C):
        for step in list(range(1, X)) + [0]:
            if step:
                if part == 0:
                    copy_b[step].wait()
                for n in range(3):
                    copy_f[step, part, n].wait()
            else:
                copy_dn2[part].wait()
            cols = pl.ds(part * L, L)

            def side(cc, total, first=first, step=step, cols=cols):
                xin = xs_all[cc].reshape(rows, o.d)
                gin = gs_all[cc].reshape(rows, o.d)
                value, slope = gelu_pair(nn(xin, w_up[step, :, cols]) + w_b[step, 0:1, cols])
                hidden = value.astype(BF)
                hid_s[cc] = hidden
                down = w_dn[step, cols, :]
                add_out = nn(hidden, down)
                pre = (nt(gin, down) * slope).astype(BF)
                pg_s[cc] = pre
                add_ng = nt(pre, w_up[step, :, cols])
                if first:
                    out_acc[cc] = add_out
                    ng_acc[cc] = add_ng
                else:
                    out_acc[cc] += add_out
                    ng_acc[cc] += add_ng
                return total + jnp.sum(pre.astype(F32), 0, keepdims=True)

            up_bias_grad = lax.fori_loop(0, 2, side, jnp.zeros((1, L), F32))
            if step == 1:
                if part + 1 < C:
                    hand_on(part + 1, (2,))
                    fetch_dn2(part + 1)
            owner = ((x + X - step) % X * 2 + c) * C + part
            vecs[3 + owner, 0:1, :] = up_bias_grad
            first = False
            if step in (0, X - 1):
                at("M" if step == 0 else "O", part, "side")
            if step == 0 and part == C - 1:
                xch_send[0] = ng_acc[1 - c].astype(BF)
                copy_ng = send(xch_send.at[0], ng_in, sibling)
                xch_send[1] = out_acc[1 - c].astype(BF)
                copy_out = send(xch_send.at[1], out_in, sibling)
            for kind in range(2):
                for half in range(2):
                    if step:
                        gb[step - 1, part, kind, half] = weight_grad(kind, half).astype(BF)
                    else:
                        gm[part, kind, half] = weight_grad(kind, half)
                if step == X - 1:
                    begin(part, kind)
            if step in (0, X - 1):
                at("M" if step == 0 else "O", part, "grad")

    res_sems = take(OWN)

    def copy_res(i):
        return remote(mrecv.at[i], blow.at[y * OWN + i], partner, res_sems + i)

    copy_ng.wait()

    def residual(i, sums):
        block = pl.ds(pl.multiple_of(i * PS, 16), PS)
        ng = ng_acc[c, block, :] + ng_in[block, :].astype(F32)
        normed = rows_n[i]
        back = gs_all[c, i].astype(F32)
        sums = (
            sums[0] + jnp.sum(ng * normed, 0, keepdims=True),
            sums[1] + jnp.sum(ng, 0, keepdims=True),
            sums[2] + jnp.sum(back, 0, keepdims=True),
        )
        q = ng * second_gain
        m1 = jnp.sum(q, -1, keepdims=True) * (1.0 / width)
        m2 = jnp.sum(q * normed, -1, keepdims=True) * (1.0 / width)
        res = (back + inv2[i] * (q - m1 - normed * m2)).astype(BF)
        mrecv[i] = res[:, L:]
        copy_res(i).start()
        blow[y * OWN + i] = res[:, :L]
        return sums

    zero = jnp.zeros((1, o.d), F32)
    sums = lax.fori_loop(0, OWN, residual, (zero, zero, zero))
    for n in range(3):
        vecs[0, 1 + 2 * n:2 + 2 * n, :] = jnp.where(y == 0, sums[n][:, :L], sums[n][:, L:])
        vecs[0, 2 + 2 * n:3 + 2 * n, :] = jnp.where(y == 0, sums[n][:, L:], sums[n][:, :L])
    at("residual")

    ones = jnp.ones((16, L), BF)

    def scaled(j):
        return j // OWN, pl.ds(pl.multiple_of(j % OWN * PS, 16), PS), pl.ds(0, L)

    def token_backward(j, carry):
        table, sum_gain, sum_shift, sum_bias = carry
        low = blow[j]
        grad = (nn(dn_ref[...], low) * tslope[j].astype(F32)).astype(BF)
        gacc[0] += nt(tin[j], grad)
        gacc[1] += nt(low, th[j])
        sum_bias = sum_bias + nt(ones, low)
        back = nn(up_ref[...], grad)
        normed, _ = first_norm(j)
        sum_gain = sum_gain + jnp.sum(back[:S] * normed, 0, keepdims=True)
        sum_shift = sum_shift + jnp.sum(back[:S], 0, keepdims=True)
        back = back * first_gain
        ng_acc[scaled(j)] = back
        back = back[:S]
        table = note(table, j, jnp.sum(back, -1, keepdims=True), jnp.sum(back * normed, -1, keepdims=True))
        return table, sum_gain, sum_shift, sum_bias

    carry = (jnp.zeros((S, 128), F32), jnp.zeros((1, L), F32), jnp.zeros((1, L), F32), jnp.zeros((16, PS), F32))
    carry = lax.fori_loop(0, OWN, lambda i, t: token_backward(y * OWN + i, t), carry)
    at("token own")

    def later(i, t):
        copy_res(i).wait()
        return token_backward((1 - y) * OWN + i, t)

    table, sum_gain, sum_shift, sum_bias = lax.fori_loop(0, OWN, later, carry)
    stats[1] = across(table)
    copy_stats2 = send(stats.at[1], stats_in.at[1], partner)
    vecs[0, 0:1, :PS] = sum_bias[0:1, :]
    vecs[1 + y, 0:1, :] = sum_gain
    vecs[1 + y, 1:2, :] = sum_shift

    def piece(n):
        return pl.ds(pl.multiple_of(n * o.piece, 16), o.piece)

    def plane_peers():
        for step in range(1, o.plane):
            there = (here + step) % o.plane
            yield step, there, (z, there // o.hid, there % o.hid)

    small_send[0:PS, :] = gacc[0].astype(BF)
    small_send[PS:2 * PS, :] = gacc[1].astype(BF)
    small_send[o.vec_row:, :] = vecs[...].reshape(8 * o.groups, L).astype(BF)

    def reduce_small():
        copies = [send(small_send.at[piece(there)], small_in.at[n - 1], peer) for n, there, peer in plane_peers()]
        yield
        for copy in copies:
            copy.wait()
        mine = small_send[piece(here), :].astype(F32)
        for n in range(1, o.plane):
            mine = mine + small_in[n - 1].astype(F32)
        small_z[z] = mine.astype(BF)
        copies = [send(small_z.at[z], small_z.at[z], ((z + n) % o.dp, y, h)) for n in range(1, o.dp)]
        yield
        for copy in copies:
            copy.wait()
        mine = small_z[0].astype(F32)
        for n in range(1, o.dp):
            mine = mine + small_z[n].astype(F32)
        small_out[piece(here), :] = mine.astype(BF)
        copies = [send(small_out.at[piece(here)], small_out.at[piece(here)], peer) for _, _, peer in plane_peers()]
        yield
        for copy in copies:
            copy.wait()

    pipes["small"] = reduce_small()
    step_of("small")
    at("token other")

    copy_stats2.wait()
    means2[...] = along((stats[1] + stats_in[1]) * (1.0 / width))

    @pl.loop(0, IM)
    def _(j):
        normed, inv_one = first_norm(j)
        grad = ng_acc[scaled(j)][:S]
        grad = grad - column(means2[:S, :], j) - normed * column(means2[:S, :], j + 8)
        grad_out[j, :S, :] = (blow[j, :S, :].astype(F32) + inv_one * grad).astype(BF)
        grad_out[j, S:, :] = jnp.zeros((PS - S, L), BF)

    at("norm")

    copy_out.wait()
    mixed_sems2 = take(OWN)

    def copy_mo(i):
        return remote(msend.at[i], mixed_out.at[y * OWN + i], partner, mixed_sems2 + i)

    @pl.loop(0, OWN)
    def _(i):
        block = pl.ds(pl.multiple_of(i * PS, 16), PS)
        branch = out_acc[c, block, :] + out_in[block, :].astype(F32) + down_bias
        result = (keep_of(y * OWN + i) * (rows_m[i] + branch)).astype(BF)
        msend[i] = result[:, L:]
        copy_mo(i).start()
        mixed_out[y * OWN + i] = result[:, :L]

    at("end")
    while pipes:
        for name in list(pipes):
            step_of(name)

    @pl.loop(0, OWN)
    def _(i):
        copy_mo(i).wait()


def block_call(o, live, patches, cot, ut, up, dn, dt, tdb, vec, bias, chan_up, chan_down):
    I, S, PS, L, OWN, D, X, C = o.images, o.s, o.ps, o.l, o.own, o.d, o.xs, o.chunks
    any_spec = pl.BlockSpec(memory_space=pl.ANY)
    vmem = pl.BlockSpec(memory_space=pltpu.VMEM)
    rows = OWN * PS
    block = (o.dp, o.seg, L)
    less = (o.dp - 1, o.seg, L)
    copies = 16 + 4 * OWN + (X - 1) * (1 + 6 * C) + C + 2 * (o.plane - 1) + o.dp - 1
    copies += 2 * C * ((X - 1) * (2 + 2 * o.levels) + 4 * o.levels + 2) + C
    outs = [
        jax.ShapeDtypeStruct((I, PS, L), BF),
        jax.ShapeDtypeStruct((I, PS, L), BF),
        jax.ShapeDtypeStruct((C, 2, o.dp, o.seg, L), BF),
        jax.ShapeDtypeStruct((C, o.dp, o.seg, L), BF),
        jax.ShapeDtypeStruct((o.small, L), BF),
    ]
    scratch = [
        ((I, S, L), BF), ((I, S, L), BF), ((OWN, S, L), BF),
        ((2, 16, o.wide), F32), ((2, 16, o.wide), F32), ((o.wide, 128), F32), ((o.wide, 128), F32),
        ((I, PS, L), BF), ((I, o.ds, L), BF), ((I, o.ds, L), BF),
        ((OWN, PS, L), BF), ((OWN, PS, L), BF),
        ((OWN, PS, D), F32), ((OWN, PS, D), F32), ((OWN, PS, 1), F32), ((8, L), F32),
        ((2, OWN, PS, D), BF), ((2, OWN, PS, D), BF),
        ((X, D, o.f), BF), ((X, o.f, D), BF), ((X, 8, o.f), F32),
        ((2, rows, L), BF), ((2, rows, L), BF), ((2, rows, D), F32), ((2, rows, D), F32),
        ((2, rows, D), BF), ((rows, D), BF), ((rows, D), BF),
        ((I, PS, L), BF),
        ((2, PS, L), F32), ((o.groups, 8, L), F32),
        ((C, 2, 2) + block, F32), ((X - 1, C, 2, 2) + block, BF), ((X - 1, C, 2, 2) + block, BF),
        ((C, 2) + block, BF), ((C, 2) + block, BF), ((X - 1, C, 2) + block, BF),
        ((len(o.slots),) + less, BF), ((len(o.slots),) + less, BF),
        ((X - 1, max(1, len(o.firsts)), 2) + (less if o.firsts else (1, 16, 128)), BF),
        ((C, 2) + block, BF), ((C, 1) + block, BF),
        ((o.small, L), BF), ((o.plane - 1, o.piece, L), BF), ((o.dp, o.piece, L), BF),
    ]
    return pl.pallas_call(
        functools.partial(kernel, o),
        out_shape=outs,
        in_specs=[pl.BlockSpec(memory_space=pltpu.SMEM), any_spec, any_spec] + [vmem] * 7 + [any_spec] * 2,
        out_specs=[vmem] * 5,
        scratch_shapes=[pltpu.VMEM(shape, kind) for shape, kind in scratch]
        + [pltpu.SemaphoreType.DMA((8,)), pltpu.SemaphoreType.DMA((copies,)), pltpu.SemaphoreType.DMA((copies,))],
        compiler_params=pltpu.CompilerParams(
            collective_id=1, has_side_effects=True, vmem_limit_bytes=63 * 2**20
        ),
        name="mixer_block",
    )(live, patches, cot, ut, up, dn, dt, tdb, vec, bias, chan_up, chan_down)


def body(
    o,
    patches,
    cotangent,
    live_images,
    first_gain,
    first_shift,
    token_up,
    token_up_bias,
    token_down,
    token_down_bias,
    second_gain,
    second_shift,
    chan_up,
    chan_up_bias,
    chan_down,
    chan_down_bias,
):
    S, PS, L = o.s, o.ps, o.l
    rest = PS - S
    up = jnp.pad(token_up, ((0, rest), (0, 0)))
    ut = jnp.concatenate([token_up, token_up_bias[None], jnp.zeros((rest - 1, o.ds), BF)], 0).T
    dn = jnp.pad(token_down, ((0, 0), (0, rest)))
    dt = jnp.pad(token_down.T, ((0, rest), (0, 0)))
    tdb = jnp.pad(token_down_bias.astype(F32), (0, rest))[:, None]
    vec = jnp.stack([first_gain, first_shift, second_gain, second_shift, chan_down_bias] + [jnp.zeros((L,), BF)] * 3)
    bias = jnp.broadcast_to(chan_up_bias.astype(F32)[None], (8, o.f))
    mixed, grad, gup, gdn, small = block_call(
        o, live_images, patches, cotangent, ut, up, dn, dt, tdb, vec.astype(F32), bias, chan_up, chan_down
    )
    y = lax.axis_index("chan")
    h = lax.axis_index("hid")
    small = small.astype(F32)
    groups = small[o.vec_row:].reshape(o.groups, 8, L)

    def pick(at, row):
        return lax.dynamic_slice_in_dim(groups[:, row], at, 1, 0)[0]

    def pick_half(row):
        return lax.dynamic_slice_in_dim(groups[0], row + y, 1, 0)[0]

    return (
        mixed[:, :S],
        grad[:, :S],
        pick(1 + y, 0),
        pick(1 + y, 1),
        small[:S],
        small[S],
        small[PS:PS + S].T,
        groups[0, 0, :S],
        pick_half(1),
        pick_half(3),
        gup.reshape(o.chunks, 2, L, L).transpose(1, 2, 0, 3).reshape(o.d, o.f).astype(F32),
        lax.dynamic_slice_in_dim(groups[:, 0], 3 + h * o.chunks, o.chunks, 0).reshape(o.f),
        gdn.reshape(o.f, L).astype(F32),
        pick_half(5),
    )


def solution(mesh):
    in_specs = (
        P(("dp", "hid"), None, "chan"),
        P(("dp", "hid"), None, "chan"),
        P(("dp", "hid")),
        P("chan"),
        P("chan"),
        P(),
        P(),
        P(),
        P(),
        P("chan"),
        P("chan"),
        P(None, "hid"),
        P("hid"),
        P("hid", "chan"),
        P("chan"),
    )
    out_specs = (
        P(("dp", "hid"), None, "chan"),
        P(("dp", "hid"), None, "chan"),
        P("chan"),
        P("chan"),
        P(),
        P(),
        P(),
        P(),
        P("chan"),
        P("chan"),
        P(None, "hid"),
        P("hid"),
        P("hid", "chan"),
        P("chan"),
    )

    def whole(*args):
        shape = dict(mesh.shape)
        patches, token_up, chan_up = args[0].shape, args[5].shape, args[11].shape
        local = (patches[0] // (shape["dp"] * shape["hid"]), patches[1], patches[2] // shape["chan"])
        o = Sizes(shape, local, (chan_up[0], chan_up[1] // shape["hid"]), token_up)
        mapped = jax.shard_map(
            functools.partial(body, o), mesh=mesh, in_specs=in_specs, out_specs=out_specs, check_vma=False
        )
        return mapped(*args)

    return whole
```

```python
import functools

import jax
import jax.numpy as jnp
from jax import lax
from jax.experimental import pallas as pl
from jax.experimental.pallas import tpu as pltpu
from jax.sharding import PartitionSpec as P

EPS = 1e-06
BF = jnp.bfloat16
F32 = jnp.float32
MESH = pl.DeviceIdType.MESH
TANH_A = 0.7978845608028654
TANH_B = TANH_A * 0.044715


def nn(left, right):
    return lax.dot_general(left, right, (((1,), (0,)), ((), ())), preferred_element_type=F32)


def nt(left, right):
    return lax.dot_general(left, right, (((1,), (1,)), ((), ())), preferred_element_type=F32)


def tn(left, right):
    return lax.dot_general(left, right, (((0,), (0,)), ((), ())), preferred_element_type=F32)


def gelu_pair(v):
    square = v * v
    tanh = jnp.tanh(v * (TANH_A + TANH_B * square))
    half = 0.5 + 0.5 * tanh
    value = v * half
    slope = half + value * (1.0 - tanh) * (TANH_A + 3.0 * TANH_B * square)
    return value, slope


def pad_to(count, unit):
    return -(-count // unit) * unit


WAYS = {
    (0, 0): ("xyz", "n"),
    (0, 1): ("yxz", "g"),
    (1, 0): ("myxz", "n"),
    (1, 1): ("mzxy", "g"),
    (2, 0): ("xyz", "n"),
    (2, 1): ("xyz", "g"),
}
PLAN = {
    ("O", 0, 1): ((0, 0), (0, 1)),
    ("M", 1, 1): ((0, 1), (1, 0)),
    ("M", 2, 1): ((1, 1),),
    ("O", 1): ((0, 1),),
    ("O", 2, 0): ((1, 1), (1, 0), (2, 0), (0, 1), (0, 0), (1, 1)),
    ("O", 2, 1): ((2, 0), (1, 0), (0, 1)),
    ("rows",): ((1, 1),),
    ("residual",): ((2, 1), (2, 0)),
    ("outputs",): ("mixed", (2, 0)),
    ("own", 0): ((0, 0), (2, 0), (2, 1), (0, 0), (1, 0)),
    ("own", 1): ((1, 1), (0, 0)),
    ("own", 2): ((1, 0), (2, 0)),
    ("other", 1): ((1, 1), (0, 1), (1, 0), (0, 0), "small", (2, 0)),
    ("token other",): ((2, 1), (1, 0), (1, 1), "small", (2, 1), (0, 1)),
    ("norm",): ((0, 0), (1, 0), "small", (1, 1), (2, 1), (2, 1), (0, 1), (0, 0), (1, 1), "small", (1, 0), "small"),
    ("end",): ((2, 1), (2, 0)),
}


class Sizes:
    def __init__(self, mesh_shape, patches, chan_up, token_up):
        self.dp = mesh_shape["dp"]
        self.hid = mesh_shape["hid"]
        self.xs = self.hid // 2
        self.images, self.s, self.l = patches
        self.ps = pad_to(self.s + 1, 16)
        self.wide = pad_to(self.ps, 128)
        self.d = 2 * self.l
        self.own = self.images // 2
        self.f = chan_up[1]
        self.ds = token_up[1]
        self.levels = self.dp.bit_length() - 1
        third = self.f // 3
        self.fetches = ((0, third), (third, 2 * third)) if self.f % 768 == 0 else ((0, self.f),)
        self.parts = tuple((n, third) for n in range(0, self.f, third)) if self.f % 768 == 0 else self.fetches
        self.units = [(part, kind) for part in range(len(self.parts)) for kind in range(2)]
        self.ways = {unit: ("xyz", "n") for unit in self.units}
        self.plan = {("O",) + unit: (unit,) for unit in self.units}
        if (self.xs, len(self.parts), self.levels) == (2, 3, 2):
            self.ways, self.plan = WAYS, PLAN
        self.chan_first = [unit for unit in self.units if self.ways[unit][0] in ("yxz", "myxz")]
        self.dp_first = [unit for unit in self.units if self.ways[unit][0] in ("zxy", "mzxy")]
        self.plane = 2 * self.hid
        self.blocks = -(-self.f // self.l)
        self.vec_wide = max(self.f, self.l)
        groups = 3 + self.hid * self.blocks
        self.vec_row = 2 * self.ps
        self.small = pad_to(self.vec_row + 8 * groups, 64 * self.xs)
        self.groups = (self.small - self.vec_row) // 8
        self.piece = self.small // (4 * self.xs)
        assert mesh_shape["chan"] == 2 and self.hid % 2 == 0 and self.images % 2 == 0 and self.images <= 8
        assert 1 << self.levels == self.dp and self.f % self.l == 0 and self.ds == self.l


def kernel(o, *refs):
    names = iter(refs)

    def get(count):
        return [next(names) for _ in range(count)]

    P_ = len(o.parts)
    live_hbm, patches_ref, cot_ref, tup_hbm, tdn_hbm, chan_up_ref, chan_down_ref = get(7)
    vector_hbm = get(8)
    mixed_out, grad_out, small_hbm = get(3)
    up_hbm, dn_hbm = get(P_), get(P_)
    vector_v = get(8)
    live_ref, tup_ref, tdn_ref, vec_ref, small_out = get(5)
    fin_up, fin_dn = get(P_), get(P_)
    pat, cot, cot_in, stats, stats_in, means, means2, up_s, ut_s, dn_s, dt_s, tdb_s = get(12)
    tin, th, tslope, msend, mrecv, rows_m, rows_n, inv2, vec_in = get(9)
    xs_all, gs_all, w_up, w_dn, w_b, hid_s, pg_s, out_own, ng_own, stage, ng_in, out_in = get(12)
    blow, gacc, vecs, small_send, small_c, small_p, small_in, small_z = get(8)
    gm, gb, rx, yb, ry = get(P_), get(P_), get(P_), get(P_), get(P_)
    zb, rz = dict(zip(o.units, get(2 * P_))), dict(zip(o.units, get(2 * P_)))
    ryo = {unit: next(names) for unit in o.chan_first}
    rzo = {unit: next(names) for unit in o.dp_first}
    loc_sem, send_sem, recv_sem = get(3)

    z = lax.axis_index("dp")
    y = lax.axis_index("chan")
    h = lax.axis_index("hid")
    c = h % 2
    x = h // 2
    S, PS, L, OWN, IM, X, F, N = o.s, o.ps, o.l, o.own, o.images, o.xs, o.f, o.dp
    width = float(o.d)
    here = y * o.hid + h
    bit = z % 2

    def dev(zz=None, yy=None, xx=None, cc=None):
        zz = z if zz is None else zz
        yy = y if yy is None else yy
        xx = x if xx is None else xx
        cc = c if cc is None else cc
        return (zz, yy, xx * 2 + cc)

    partner = dev(yy=1 - y)
    sibling = dev(cc=1 - c)
    z_pair = dev(zz=z + 1 - 2 * bit)
    counter = [0]

    def take(count=1):
        base = counter[0]
        counter[0] += count
        return base

    def remote(src, dst, device, index=None):
        index = take() if index is None else index
        return pltpu.make_async_remote_copy(
            src_ref=src, dst_ref=dst, send_sem=send_sem.at[index], recv_sem=recv_sem.at[index],
            device_id=device, device_id_type=MESH,
        )

    def send(src, dst, device):
        copy = remote(src, dst, device)
        copy.start()
        return copy

    barrier = pltpu.get_barrier_semaphore()
    for step in range(1, o.plane):
        there = (here + step) % o.plane
        pl.semaphore_signal(barrier, inc=1, device_id=(z, there // o.hid, there % o.hid), device_id_type=MESH)
    for step in range(1, N):
        pl.semaphore_signal(barrier, inc=1, device_id=((z + step) % N, y, h), device_id_type=MESH)

    loads = []

    def load(src, dst):
        copy = pltpu.make_async_copy(src, dst, loc_sem.at[len(loads)])
        loads.append(copy)
        copy.start()
        return copy

    stores = []

    def store(src, dst):
        copy = pltpu.make_async_copy(src, dst, loc_sem.at[24 + len(stores)])
        copy.start()
        stores.append(copy)

    load_vectors = [load(src, dst) for src, dst in zip(vector_hbm, vector_v)]
    load_live = load(live_hbm, live_ref)
    load_token = [load(tup_hbm, tup_ref), load(tdn_hbm, tdn_ref)]
    load_pat = load(patches_ref, pat)
    load_cot = load(cot_ref.at[pl.ds(y * OWN, OWN)], cot)
    load_up0 = load(chan_up_ref.at[pl.ds(pl.multiple_of(y * L, L), L)], w_up.at[0, pl.ds(0, L)])
    load_up1 = load(chan_up_ref.at[pl.ds(pl.multiple_of((1 - y) * L, L), L)], w_up.at[0, pl.ds(L, L)])
    load_dn = load(chan_down_ref, w_dn.at[0, :, pl.ds(0, L)])

    pad = PS - S
    pad_row = lax.broadcasted_iota(jnp.int32, (pad, L), 0)
    one_row = jnp.where(pad_row == 0, 1.0, 0.0).astype(BF)
    for j in range(IM):
        tin[j, S:PS, :] = one_row
    for i in range(OWN):
        xs_all[c, i, S:PS, :] = jnp.zeros((pad, o.d), BF)
        gs_all[c, i, S:PS, :] = jnp.zeros((pad, o.d), BF)
        rows_n[i, S:PS, :] = jnp.zeros((pad, o.d), F32)
        rows_m[i, S:PS, :] = jnp.zeros((pad, o.d), BF)
        inv2[i, S:PS, :] = jnp.zeros((pad, 1), F32)
        msend[i, S:PS, :] = jnp.zeros((pad, L), BF)
    vecs[...] = jnp.zeros(vecs.shape, F32)
    gacc[...] = jnp.zeros(gacc.shape, F32)
    vec_ref[...] = jnp.zeros(vec_ref.shape, F32)
    for n, copy in enumerate(load_vectors):
        copy.wait()
        count = vector_v[n].shape[0]
        vec_ref[n:n + 1, :count] = vector_v[n][...].astype(F32).reshape(1, count)
    for copy in load_token:
        copy.wait()
    w_b[0, 0:1, :] = vec_ref[7:8, :]
    up_bias, down_bias_row = vec_ref[5:6, :L], vec_ref[6:7, :L]
    last = jnp.zeros((o.wide - S - 1, L), F32)
    up_full = jnp.concatenate([tup_ref[...].astype(F32), up_bias, last], 0)
    up_s[...] = up_full[:PS].astype(BF)
    ut_s[...] = up_full.T[:, :PS].astype(BF)
    dn_full = jnp.concatenate([tdn_ref[...].astype(F32), jnp.zeros((o.wide - S, L), F32)], 0)
    dn_s[...] = dn_full.T[:, :PS].astype(BF)
    dt_s[...] = dn_full[:PS].astype(BF)
    tdb_s[...] = jnp.concatenate([down_bias_row, jnp.zeros((127, L), F32)], 0).T[:PS]

    lane = lax.broadcasted_iota(jnp.int32, (S, 128), 1)
    load_pat.wait()

    def note(table, j, first, second):
        table = jnp.where(lane == j, first, table)
        return jnp.where(lane == j + 8, second, table)

    def across(table):
        rest = jnp.zeros((o.wide - S, 128), F32)
        return jnp.concatenate([table, rest], 0).T[:16]

    def along(table):
        return jnp.concatenate([table, jnp.zeros((112, o.wide), F32)], 0).T

    def sums_of(j, table):
        v = pat[j].astype(F32)
        return note(table, j, jnp.sum(v, -1, keepdims=True), jnp.sum(v * v, -1, keepdims=True))

    stats[0] = across(lax.fori_loop(0, IM, sums_of, jnp.zeros((S, 128), F32)))

    pl.semaphore_wait(barrier, o.plane - 1 + N - 1)

    copy_stats = send(stats.at[0], stats_in.at[0], partner)
    copy_vec = send(vec_ref, vec_in, partner)
    near = pl.ds(bit * L, L)
    near_from = pl.ds(pl.multiple_of(((y + bit) % 2) * L, L), L)
    copy_b = {step: send(w_b.at[0], w_b.at[step], dev(xx=(x + step) % X)) for step in range(1, X)}
    copy_w = {}
    copy_f = {}

    def weight_spans(step, part):
        start, size = o.fetches[part]
        cols = pl.ds(start, size)
        rows_dn = pl.ds(pl.multiple_of(start + bit * (size // 2), 16), size // 2)
        rows_own = pl.ds(start, size) if part else rows_dn
        return (
            (chan_up_ref.at[near_from, cols], w_up.at[step, near, cols], y),
            (chan_down_ref.at[rows_own], w_dn.at[step, rows_own, pl.ds(0, L)], y),
            (chan_down_ref.at[rows_dn], w_dn.at[step, rows_dn, pl.ds(L, L)], 1 - y),
        )

    def fetch(part, which):
        for step in range(1, X):
            for n in which if part < len(o.fetches) else ():
                src, dst, yy = weight_spans(step, part)[n]
                copy_w[step, part, n] = send(src, dst, dev(xx=(x + step) % X, yy=yy))

    def hand_on(part, which):
        for step in range(1, X):
            for n in which if part < len(o.fetches) else ():
                dst = weight_spans(step, part)[n][1]
                if part and n == 1:
                    copy_f[step, part, n] = copy_w[step, part, n]
                else:
                    copy_w[step, part, n].wait()
                    copy_f[step, part, n] = send(dst, dst, z_pair)

    quarter = F // 4
    bit2 = (z // 2) % 2
    z_far = dev(zz=z + 2 - 4 * bit2)

    def dn2_span(first, count):
        return pl.ds(pl.multiple_of(first * quarter, 16), count * quarter)

    dn2_mine = dn2_span(bit * 2 + bit2, 1)
    dn2_half = dn2_span(bit * 2, 2)
    copy_dn2 = [send(chan_down_ref.at[dn2_mine], w_dn.at[0, dn2_mine, pl.ds(L, L)], partner)]

    def dn2_on(span, peer):
        copy_dn2[-1].wait()
        ref = w_dn.at[0, span, pl.ds(L, L)]
        copy_dn2.append(send(ref, ref, peer))

    fetch(0, (0,))
    copy_cot = send(cot_ref.at[pl.ds((1 - y) * OWN, OWN)], cot_in, partner)
    fetch(0, (1, 2))

    copy_stats.wait()
    total = (stats[0] + stats_in[0]) * (1.0 / width)
    mean, square = total[:8], total[8:]
    means[...] = along(jnp.concatenate([mean, lax.rsqrt(square - mean * mean + EPS)], 0))
    fetch(1, (0,))

    def column(table, j):
        return jnp.sum(jnp.where(lane == j, table, 0.0), -1, keepdims=True)

    first_gain = vec_ref[0:1, :L]
    first_shift = vec_ref[1:2, :L]

    def first_norm(j):
        table = means[:S, :]
        inv_one = column(table, j + 8)
        return (pat[j].astype(F32) - column(table, j)) * inv_one, inv_one

    def token_forward(j):
        normed, _ = first_norm(j)
        tin[j, :S, :] = (normed * first_gain + first_shift).astype(BF)
        value, slope = gelu_pair(nn(ut_s[...], tin[j]))
        th[j] = value.astype(BF)
        tslope[j] = slope.astype(BF)
        back = nn(dt_s[...], th[j])
        return pat[j].astype(F32) + back[:S] + tdb_s[:S, 0:1]

    mixed_sems = take(OWN)

    def copy_mixed(i):
        return remote(msend.at[i], mrecv.at[i], partner, mixed_sems + i)

    @pl.loop(0, OWN)
    def _(i):
        msend[i, :S, :] = token_forward((1 - y) * OWN + i).astype(BF)
        copy_mixed(i).start()

    @pl.loop(0, OWN)
    def _(i):
        rows_n[i, :S, :L] = token_forward(y * OWN + i)

    dn2_on(dn2_mine, z_far)
    hand_on(0, (0,))
    fetch(1, (1,))
    hand_on(0, (1, 2))
    dn2_on(dn2_half, z_pair)
    load_cot.wait()
    copy_cot.wait()
    load_live.wait()
    live = live_ref[0]

    def keep_of(j):
        return jnp.where(j < live, 1.0, 0.0).astype(F32)

    @pl.loop(0, OWN)
    def _(i):
        keep = keep_of(y * OWN + i)
        gs_all[c, i, :S, :L] = (cot[i].astype(F32) * keep).astype(BF)
        gs_all[c, i, :S, L:] = (cot_in[i].astype(F32) * keep).astype(BF)

    copy_gs = send(gs_all.at[c], gs_all.at[c], sibling)
    hand_on(1, (0,))

    copy_vec.wait()
    both = [jnp.concatenate([vec_ref[n:n + 1, :L], vec_in[n:n + 1, :L]], axis=1) for n in range(2, 5)]
    second_gain, second_shift, down_bias = both
    row_sems = take(OWN)

    def copy_rows(i):
        return remote(xs_all.at[c, i], xs_all.at[c, i], sibling, row_sems + i)

    @pl.loop(0, OWN)
    def _(i):
        copy_mixed(i).wait()
        rows_n[i, :S, L:] = mrecv[i, :S, :].astype(F32)
        v = rows_n[i, :S, :]
        mean = jnp.sum(v, -1, keepdims=True) * (1.0 / width)
        spread = jnp.sum(v * v, -1, keepdims=True) * (1.0 / width) - mean * mean
        inv_two = lax.rsqrt(spread + EPS)
        normed = (v - mean) * inv_two
        rows_m[i, :S, :] = v.astype(BF)
        inv2[i, :S, :] = inv_two
        rows_n[i, :S, :] = normed
        xs_all[c, i, :S, :] = (normed * second_gain + second_shift).astype(BF)
        copy_rows(i).start()

    fetch(1, (2,))
    hand_on(1, (1,))
    load_up0.wait()
    load_up1.wait()
    load_dn.wait()
    copy_gs.wait()

    @pl.loop(0, OWN)
    def _(i):
        copy_rows(i).wait()

    def levels():
        start, count, used = 0, N, 0
        for level in range(o.levels):
            side_bit = (z // (1 << level)) % 2
            peer = dev(zz=z + (1 - 2 * side_bit) * (1 << level))
            count //= 2
            yield start + side_bit * count, start + (1 - side_bit) * count, count, used, peer
            start = start + side_bit * count
            used += count

    def my_segment():
        return list(levels())[-1][0]

    def add(part, kind, half, span, *terms):
        mine = gm[part][kind, half, span]
        for term in terms:
            mine = mine + term.astype(F32)
        gm[part][kind, half, span] = mine

    everything = pl.ds(0, N)
    low, high = pl.ds(0, N // 2), pl.ds(N // 2, N // 2)

    def finals(part, kind):
        if kind == 0:
            return [fin_up[part].at[0], fin_up[part].at[1]]
        return [fin_dn[part]]

    def reduce_rec(part, kind, halves):
        out, land = zb[part, kind], rz[part, kind]
        for keep_at, send_at, count, used, peer in levels():
            span = pl.ds(used, count)
            copies = []
            for half in range(halves):
                out[half, span] = gm[part][kind, half, pl.ds(send_at, count)].astype(BF)
                copies.append(send(out.at[half, span], land.at[half, span], peer))
            yield
            for half in range(halves):
                copies[half].wait()
                add(part, kind, half, pl.ds(keep_at, count), land[half, span])

    def gather_rec(part, kind):
        own = pl.ds(my_segment(), 1)
        done = finals(part, kind)
        early = kind == 0 and o.ways[part, kind][1] == "g"
        done[0][own] = gm[part][kind, 0, own].astype(BF)
        if early:
            copy = send(done[0].at[own], done[1].at[own], partner)
            yield
            copy.wait()
        for keep_at, _, count, _, peer in reversed(list(levels())):
            span = pl.ds(keep_at, count)
            copies = [send(ref.at[span], ref.at[span], peer) for ref in done[:1 + early]]
            yield
            for copy in copies:
                copy.wait()
        if kind == 0 and not early:
            copy = send(done[0], done[1], partner)
            yield
            copy.wait()

    def owner(n):
        return dev(xx=(x + X - 1 - n) % X)

    def start_x(part, kind):
        return [send(gb[part].at[n, kind], rx[part].at[n, kind], owner(n)) for n in range(X - 1)]

    def send_y(part, kind, span):
        yb[part][kind, span] = gm[part][kind, 1, span].astype(BF)
        return send(yb[part].at[kind, span], ry[part].at[kind, span], partner)

    def wait_all(copies):
        for copy in copies:
            copy.wait()

    def add_x(part, kind, half, span):
        add(part, kind, half, span, *[rx[part][n, kind, half, span] for n in range(X - 1)])

    def chunk_xyz(part, kind):
        copies = start_x(part, kind)
        yield
        wait_all(copies)
        add_x(part, kind, 1, everything)
        copy = send_y(part, kind, everything)
        add_x(part, kind, 0, everything)
        yield
        copy.wait()
        add(part, kind, 0, everything, ry[part][kind])
        yield from reduce_rec(part, kind, 1)
        yield from gather_rec(part, kind)

    def chunk_xzy(part, kind):
        copies = start_x(part, kind)
        yield
        wait_all(copies)
        add_x(part, kind, 1, everything)
        add_x(part, kind, 0, everything)
        yield from reduce_rec(part, kind, 2)
        own = pl.ds(my_segment(), 1)
        copy = send_y(part, kind, own)
        yield
        copy.wait()
        add(part, kind, 0, own, ry[part][kind, own])
        yield from gather_rec(part, kind)

    def start_yo(part, kind):
        return [send(gb[part].at[n, kind, 1], ryo[part, kind].at[n], partner) for n in range(X - 1)]

    def pass_yo(part, kind, copies):
        wait_all(copies)
        for n in range(X - 1):
            mine = gb[part][n, kind, 0].astype(F32) + ryo[part, kind][n].astype(F32)
            gb[part][n, kind, 0] = mine.astype(BF)
        return [send(gb[part].at[n, kind, 0], rx[part].at[n, kind, 0], owner(n)) for n in range(X - 1)]

    def end_yx(part, kind, copies, copy):
        copy.wait()
        wait_all(copies)
        add(part, kind, 0, everything, ry[part][kind], *[rx[part][n, kind, 0] for n in range(X - 1)])
        yield from reduce_rec(part, kind, 1)
        yield from gather_rec(part, kind)

    def chunk_yxz(part, kind):
        copies = start_yo(part, kind)
        yield
        copies = pass_yo(part, kind, copies)
        yield
        copy = send_y(part, kind, everything)
        yield
        yield from end_yx(part, kind, copies, copy)

    def chunk_myxz(part, kind):
        copy = send_y(part, kind, everything)
        yield
        copies = start_yo(part, kind)
        yield
        copies = pass_yo(part, kind, copies)
        yield
        yield from end_yx(part, kind, copies, copy)

    def reduce_others(part, kind):
        land = rzo[part, kind]
        for keep_at, send_at, count, used, peer in levels():
            copies = {}
            span = pl.ds(used, count)
            for n in range(X - 1):
                for half in range(2):
                    src = gb[part].at[n, kind, half, pl.ds(send_at, count)]
                    copies[n, half] = send(src, land.at[n, half, span], peer)
            yield
            for n in range(X - 1):
                for half in range(2):
                    copies[n, half].wait()
                    keep = pl.ds(keep_at, count)
                    mine = gb[part][n, kind, half, keep].astype(F32) + land[n, half, span].astype(F32)
                    gb[part][n, kind, half, keep] = mine.astype(BF)

    def segment_x(part, kind):
        own = pl.ds(my_segment(), 1)
        return [send(gb[part].at[n, kind, :, own], rx[part].at[n, kind, :, own], owner(n)) for n in range(X - 1)]

    def end_zx(part, kind, copies):
        own = pl.ds(my_segment(), 1)
        wait_all(copies)
        add_x(part, kind, 1, own)
        copy = send_y(part, kind, own)
        add_x(part, kind, 0, own)
        yield
        copy.wait()
        add(part, kind, 0, own, ry[part][kind, own])
        yield from gather_rec(part, kind)

    def chunk_zxy(part, kind):
        yield from reduce_others(part, kind)
        copies = segment_x(part, kind)
        yield
        yield from reduce_rec(part, kind, 2)
        yield from end_zx(part, kind, copies)

    def chunk_mzxy(part, kind):
        yield from reduce_rec(part, kind, 2)
        yield from reduce_others(part, kind)
        copies = segment_x(part, kind)
        yield
        yield from end_zx(part, kind, copies)

    chunk = {
        "xyz": chunk_xyz, "xzy": chunk_xzy, "yxz": chunk_yxz, "myxz": chunk_myxz, "zxy": chunk_zxy, "mzxy": chunk_mzxy
    }
    pipes = {unit: chunk[o.ways[unit][0]](*unit) for unit in o.units}

    def step_of(name):
        if name in pipes:
            try:
                next(pipes[name])
            except StopIteration:
                del pipes[name]
                if name == "small":
                    store(small_out, small_hbm)
                elif name != "mixed":
                    part, kind = name
                    store(*((fin_up[part], up_hbm[part]), (fin_dn[part], dn_hbm[part]))[kind])

    def at(*point):
        for name in o.plan.get(point, ()):
            step_of(name)

    rows = OWN * PS

    def inner(step, start, size):
        cols = pl.ds(start, size)

        def side(cc, sums):
            pre = nn(xs_all[cc].reshape(rows, o.d), w_up[step, :, cols]) + w_b[step, 0:1, cols]
            value, slope = gelu_pair(pre)
            hid_s[step, cc, :, cols] = value.astype(BF)
            grad = (nt(gs_all[cc].reshape(rows, o.d), w_dn[step, cols, :]) * slope).astype(BF)
            pg_s[step, cc, :, cols] = grad
            return sums + jnp.sum(grad.astype(F32), 0, keepdims=True)

        sums = lax.fori_loop(0, 2, side, jnp.zeros((1, size), F32))
        group = 3 + ((x + X - step) % X * 2 + c) * o.blocks
        for n in range(start, start + size, 128):
            block, lanes = n // L, n % L
            vecs[group + block, 0:1, lanes:lanes + 128] = sums[:, n - start:n - start + 128]

    def weight_grad(step, part, kind):
        start, size = o.parts[part]
        cols = pl.ds(start, size)
        left, right = (pg_s, xs_all) if kind == 0 else (hid_s, gs_all)
        grad = tn(left[step, :, :, cols].reshape(2 * rows, size), right[...].reshape(2 * rows, o.d))
        grad = grad.reshape(N, size // N, o.d)
        for half in range(2):
            block = grad[:, :, half * L:(half + 1) * L]
            if step:
                gb[part][step - 1, kind, half] = block.astype(BF)
            else:
                gm[part][kind, half] = block

    def other_slots(group):
        start, size = o.fetches[group]
        for step in range(1, X):
            if group == 0:
                copy_b[step].wait()
            for n in range(3):
                copy_f[step, group, n].wait()
            inner(step, start, size)
        at("O", group)
        for part in range(P_):
            if start <= o.parts[part][0] < start + size:
                for kind in range(2):
                    for step in range(1, X):
                        weight_grad(step, part, kind)
                    at("O", part, kind)

    other_slots(0)
    hand_on(1, (2,))
    copy_dn2[-1].wait()
    inner(0, 0, F)
    at("M")
    for part in range(P_):
        for kind in range(2):
            weight_grad(0, part, kind)
            at("M", part, kind)
    for group in range(1, len(o.fetches)):
        other_slots(group)
    at("O")

    def row_sums(kind, cc):
        left, right, dot = ((pg_s, w_up, nt), (hid_s, w_dn, nn))[kind]
        total = dot(left[0, cc], right[0])
        for step in range(1, X):
            total = total + dot(left[step, cc], right[step])
        return total

    stage[0] = row_sums(0, 1 - c).astype(BF)
    copy_ng = send(stage.at[0], ng_in, sibling)
    mine = row_sums(0, c)
    ng_own[0] = mine[:, :L]
    ng_own[1] = mine[:, L:]
    at("rows")

    res_sems = take(OWN)

    def copy_res(i):
        return remote(mrecv.at[i], blow.at[y * OWN + i], partner, res_sems + i)

    copy_ng.wait()

    def residual(i, sums):
        block = pl.ds(pl.multiple_of(i * PS, 16), PS)
        ng = jnp.concatenate([ng_own[0, block, :], ng_own[1, block, :]], 1) + ng_in[block, :].astype(F32)
        normed = rows_n[i]
        back = gs_all[c, i].astype(F32)
        sums = (
            sums[0] + jnp.sum(ng * normed, 0, keepdims=True),
            sums[1] + jnp.sum(ng, 0, keepdims=True),
            sums[2] + jnp.sum(back, 0, keepdims=True),
        )
        q = ng * second_gain
        m1 = jnp.sum(q, -1, keepdims=True) * (1.0 / width)
        m2 = jnp.sum(q * normed, -1, keepdims=True) * (1.0 / width)
        res = (back + inv2[i] * (q - m1 - normed * m2)).astype(BF)
        mrecv[i] = res[:, L:]
        copy_res(i).start()
        blow[y * OWN + i] = res[:, :L]
        return sums

    zero = jnp.zeros((1, o.d), F32)
    sums = lax.fori_loop(0, OWN, residual, (zero, zero, zero))
    for n in range(3):
        vecs[0, 1 + 2 * n:2 + 2 * n, :] = jnp.where(y == 0, sums[n][:, :L], sums[n][:, L:])
        vecs[0, 2 + 2 * n:3 + 2 * n, :] = jnp.where(y == 0, sums[n][:, L:], sums[n][:, :L])
    at("residual")

    stage[1] = row_sums(1, 1 - c).astype(BF)
    copy_out = send(stage.at[1], out_in, sibling)
    at("outputs 0")
    out_own[...] = row_sums(1, c)

    mixed_sems2 = take(OWN)

    def copy_mo(i):
        return remote(msend.at[i], mixed_out.at[y * OWN + i], partner, mixed_sems2 + i)

    def output_rows():
        copy_out.wait()

        @pl.loop(0, OWN)
        def _(i):
            block = pl.ds(pl.multiple_of(i * PS, 16), PS)
            branch = out_own[block, :] + out_in[block, :].astype(F32) + down_bias
            result = (keep_of(y * OWN + i) * (rows_m[i].astype(F32) + branch)).astype(BF)
            msend[i] = result[:, L:]
            copy_mo(i).start()
            xs_all[c, i, :, :L] = result[:, :L]

        store(xs_all.at[c, :, :, pl.ds(0, L)], mixed_out.at[pl.ds(y * OWN, OWN)])
        yield

    pipes["mixed"] = output_rows()
    at("outputs")

    ones = jnp.ones((16, L), BF)

    def scaled(j):
        return j // OWN, pl.ds(pl.multiple_of(j % OWN * PS, 16), PS)

    def token_backward(j, carry):
        table, sum_gain, sum_shift, sum_bias = carry
        low_grad = blow[j]
        grad = (nn(dn_s[...], low_grad) * tslope[j].astype(F32)).astype(BF)
        gacc[0] += nt(tin[j], grad)
        gacc[1] += nt(low_grad, th[j])
        sum_bias = sum_bias + nt(ones, low_grad)
        back = nn(up_s[...], grad)
        normed, _ = first_norm(j)
        sum_gain = sum_gain + jnp.sum(back[:S] * normed, 0, keepdims=True)
        sum_shift = sum_shift + jnp.sum(back[:S], 0, keepdims=True)
        back = back * first_gain
        ng_own[scaled(j)] = back
        back = back[:S]
        table = note(table, j, jnp.sum(back, -1, keepdims=True), jnp.sum(back * normed, -1, keepdims=True))
        return table, sum_gain, sum_shift, sum_bias

    carry = (jnp.zeros((S, 128), F32), jnp.zeros((1, L), F32), jnp.zeros((1, L), F32), jnp.zeros((16, PS), F32))
    for i in range(OWN):
        carry = token_backward(y * OWN + i, carry)
        at("own", i)

    for i in range(OWN):
        copy_res(i).wait()
        carry = token_backward((1 - y) * OWN + i, carry)
        if i < OWN - 1:
            at("other", i)
    table, sum_gain, sum_shift, sum_bias = carry
    stats[1] = across(table)
    copy_stats2 = send(stats.at[1], stats_in.at[1], partner)
    vecs[0, 0:1, :PS] = sum_bias[0:1, :]
    vecs[1 + y, 0:1, :] = sum_gain
    vecs[1 + y, 1:2, :] = sum_shift

    half_small = o.small // 2
    spot = y * X + x
    chips = 2 * X

    def chip_peers():
        for step in range(1, chips):
            there = (spot + step) % chips
            yield step, there, dev(yy=there // X, xx=there % X)

    def piece(n):
        return pl.ds(pl.multiple_of(n * o.piece, 16), o.piece)

    def share(cc):
        return pl.ds(pl.multiple_of(cc * half_small, 16), half_small)

    def out_piece(n):
        return pl.ds(pl.multiple_of(c * half_small + n * o.piece, 16), o.piece)

    small_send[0:PS, :] = gacc[0]
    small_send[PS:2 * PS, :] = gacc[1]
    small_send[o.vec_row:, :] = vecs[...].reshape(8 * o.groups, L)

    def reduce_small():
        copy = send(small_send.at[share(1 - c)], small_c, sibling)
        yield
        copy.wait()
        small_p[...] = (small_send[share(c), :] + small_c[...]).astype(BF)
        copies = [send(small_p.at[piece(there)], small_in.at[n - 1], peer) for n, there, peer in chip_peers()]
        yield
        for copy in copies:
            copy.wait()
        mine = small_p[piece(spot), :].astype(F32)
        for n in range(1, chips):
            mine = mine + small_in[n - 1].astype(F32)
        small_z[z] = mine.astype(BF)
        copies = [send(small_z.at[z], small_z.at[z], dev(zz=(z + n) % N)) for n in range(1, N)]
        yield
        for copy in copies:
            copy.wait()
        mine = small_z[0].astype(F32)
        for n in range(1, N):
            mine = mine + small_z[n].astype(F32)
        small_out[out_piece(spot), :] = mine.astype(BF)
        span = small_out.at[out_piece(spot)]
        copies = [send(span, span, peer) for _, _, peer in chip_peers()]
        yield
        for copy in copies:
            copy.wait()
        span = small_out.at[share(c)]
        copy = send(span, span, sibling)
        yield
        copy.wait()

    pipes["small"] = reduce_small()
    step_of("small")
    at("token other")

    copy_stats2.wait()
    means2[...] = along((stats[1] + stats_in[1]) * (1.0 / width))

    @pl.loop(0, IM)
    def _(j):
        normed, inv_one = first_norm(j)
        grad = ng_own[scaled(j)][:S]
        grad = grad - column(means2[:S, :], j) - normed * column(means2[:S, :], j + 8)
        blow[j, :S, :] = (blow[j, :S, :].astype(F32) + inv_one * grad).astype(BF)

    store(blow, grad_out)
    at("norm")

    while pipes:
        for name in list(pipes):
            step_of(name)

    @pl.loop(0, OWN)
    def _(i):
        copy_mo(i).wait()

    for copy in stores:
        copy.wait()


def block_call(o, matrices, vectors):
    I, S, PS, L, OWN, D, X, N, F = o.images, o.s, o.ps, o.l, o.own, o.d, o.xs, o.dp, o.f
    any_spec = pl.BlockSpec(memory_space=pl.ANY)
    rows = OWN * PS
    copies = 16 + 4 * OWN + (X - 1) * (1 + 6 * len(o.parts)) + 6 * X + N
    copies += len(o.units) * ((X - 1) * (3 + 2 * o.levels) + 5 * o.levels + 8)
    segs = [size // N for _, size in o.parts]
    outs = [
        jax.ShapeDtypeStruct((I, PS, L), BF),
        jax.ShapeDtypeStruct((I, PS, L), BF),
        jax.ShapeDtypeStruct((o.small, L), BF),
    ]
    outs += [jax.ShapeDtypeStruct((2, N, seg, L), BF) for seg in segs]
    outs += [jax.ShapeDtypeStruct((N, seg, L), BF) for seg in segs]
    scratch = [(vector.shape, BF) for vector in vectors]
    scratch += [None, ((S, L), BF), ((S, L), BF), ((8, o.vec_wide), F32), ((o.small, L), BF)]
    scratch += [((2, N, seg, L), BF) for seg in segs] + [((N, seg, L), BF) for seg in segs]
    scratch += [
        ((I, S, L), BF), ((OWN, S, L), BF), ((OWN, S, L), BF),
        ((2, 16, o.wide), F32), ((2, 16, o.wide), F32),
        ((o.wide, 128), F32), ((o.wide, 128), F32),
        ((PS, L), BF), ((L, PS), BF), ((L, PS), BF), ((PS, L), BF), ((PS, 128), F32),
        ((I, PS, L), BF), ((I, o.ds, L), BF), ((I, o.ds, L), BF),
        ((OWN, PS, L), BF), ((OWN, PS, L), BF),
        ((OWN, PS, D), BF), ((OWN, PS, D), F32), ((OWN, PS, 1), F32), ((8, o.vec_wide), F32),
        ((2, OWN, PS, D), BF), ((2, OWN, PS, D), BF),
        ((X, D, F), BF), ((X, F, D), BF), ((X, 8, o.vec_wide), F32),
        ((X, 2, rows, F), BF), ((X, 2, rows, F), BF),
        ((rows, D), F32), ((2, rows, L), F32), ((2, rows, D), BF),
        ((rows, D), BF), ((rows, D), BF),
        ((I, PS, L), BF), ((2, PS, L), F32), ((o.groups, 8, L), F32),
        ((o.small, L), F32), ((o.small // 2, L), F32), ((o.small // 2, L), BF),
        ((2 * X - 1, o.piece, L), BF), ((N, o.piece, L), BF),
    ]
    blocks = [(N, seg, L) for seg in segs]
    scratch += [((2, 2) + block, F32) for block in blocks]
    scratch += [((X - 1, 2, 2) + block, BF) for block in blocks] * 2
    scratch += [((2,) + block, BF) for block in blocks] * 2
    for _ in range(2):
        for unit in o.units:
            halves = 1 if o.ways[unit][0] in ("xyz", "yxz", "myxz") else 2
            scratch.append(((halves,) + blocks[unit[0]], BF))
    scratch += [((X - 1,) + blocks[unit[0]], BF) for unit in o.chan_first]
    scratch += [((X - 1, 2) + blocks[unit[0]], BF) for unit in o.dp_first]
    return pl.pallas_call(
        functools.partial(kernel, o),
        out_shape=outs,
        in_specs=[any_spec] * (len(matrices) + len(vectors)),
        out_specs=[any_spec] * len(outs),
        scratch_shapes=[pltpu.VMEM(*entry) if entry else pltpu.SMEM((1,), jnp.int32) for entry in scratch]
        + [pltpu.SemaphoreType.DMA((40,)), pltpu.SemaphoreType.DMA((copies,)), pltpu.SemaphoreType.DMA((copies,))],
        compiler_params=pltpu.CompilerParams(
            collective_id=1, has_side_effects=True, vmem_limit_bytes=63 * 2**20
        ),
        name="mixer_block",
    )(*matrices, *vectors)


def unpack(o, *refs):
    P_ = len(o.parts)
    names = iter(refs)

    def get(count):
        return [next(names) for _ in range(count)]

    inputs, outputs = get(3 + 2 * P_), get(14)
    inputs_v, outputs_v = get(3 + 2 * P_), get(14)
    in_sem, out_sem = get(2)
    S, PS, L = o.s, o.ps, o.l
    y = lax.axis_index("chan")
    h = lax.axis_index("hid")
    loads = [pltpu.make_async_copy(src, dst, in_sem.at[n]) for n, (src, dst) in enumerate(zip(inputs, inputs_v))]
    stores = [pltpu.make_async_copy(src, dst, out_sem.at[n]) for n, (src, dst) in enumerate(zip(outputs_v, outputs))]
    order = list(range(3, 3 + 2 * P_)) + [0, 1, 2]
    for n in order:
        loads[n].start()
    mixed_in, grad_in, small_in = inputs_v[:3]
    fin_up, fin_dn = inputs_v[3:3 + P_], inputs_v[3 + P_:]
    mixed, grad, fg, fs, tu, tub, td, tdb, sg, ss, cu, cub, cd, cdb = outputs_v
    for part, (start, size) in enumerate(o.parts):
        loads[3 + part].wait()
        for half in range(2):
            block = fin_up[part][half].astype(F32).reshape(size, L).T
            cu[pl.ds(pl.multiple_of((y + half) % 2 * L, L), L), start:start + size] = block
    stores[10].start()
    for part, (start, size) in enumerate(o.parts):
        loads[3 + P_ + part].wait()
        cd[start:start + size, :] = fin_dn[part][...].astype(F32).reshape(size, L)
    stores[12].start()
    loads[0].wait()
    mixed[...] = mixed_in[:, :S]
    stores[0].start()
    loads[1].wait()
    grad[...] = grad_in[:, :S]
    stores[1].start()
    loads[2].wait()
    small = small_in[...].astype(F32)
    tu[...] = small[:S]
    tub[...] = small[S:S + 1].reshape(L)
    td[...] = small[PS:PS + S]
    groups = small[o.vec_row:].reshape(o.groups, 8, L)
    tdb[...] = groups[0, 0:1, :S].reshape(S)
    for n, ref in enumerate((sg, ss, cdb)):
        ref[...] = jnp.where(y == 0, groups[0, 1 + 2 * n:2 + 2 * n], groups[0, 2 + 2 * n:3 + 2 * n]).reshape(L)
    for n, ref in enumerate((fg, fs)):
        ref[...] = jnp.where(y == 0, groups[1, n:n + 1], groups[2, n:n + 1]).reshape(L)
    totals = []
    for n in range(o.blocks):
        total = jnp.zeros((1, L), F32)
        for k in range(o.hid):
            total = jnp.where(h == k, groups[3 + k * o.blocks + n, 0:1], total)
        totals.append(total)
    cub[...] = jnp.concatenate(totals, 1).reshape(o.f)
    for n in (2, 3, 4, 5, 6, 7, 8, 9, 11, 13):
        stores[n].start()
    for copy in stores:
        copy.wait()


def body(
    o,
    patches,
    cotangent,
    live_images,
    first_gain,
    first_shift,
    token_up,
    token_up_bias,
    token_down,
    token_down_bias,
    second_gain,
    second_shift,
    chan_up,
    chan_up_bias,
    chan_down,
    chan_down_bias,
):
    S, L, D, F = o.s, o.l, o.d, o.f
    matrices = [live_images, patches, cotangent, token_up, token_down.T, chan_up, chan_down]
    vectors = [first_gain, first_shift, second_gain, second_shift, chan_down_bias, token_up_bias, token_down_bias]
    results = block_call(o, matrices, vectors + [chan_up_bias])
    any_spec = pl.BlockSpec(memory_space=pl.ANY)
    shapes = [
        (patches.shape, BF), (patches.shape, BF), ((L,), F32), ((L,), F32), ((S, L), F32), ((L,), F32),
        ((S, L), F32), ((S,), F32), ((L,), F32), ((L,), F32), ((D, F), F32), ((F,), F32), ((F, L), F32),
        ((L,), F32),
    ]
    outs = pl.pallas_call(
        functools.partial(unpack, o),
        out_shape=[jax.ShapeDtypeStruct(shape, kind) for shape, kind in shapes],
        in_specs=[any_spec] * len(results),
        out_specs=[any_spec] * len(shapes),
        scratch_shapes=[pltpu.VMEM(result.shape, BF) for result in results]
        + [pltpu.VMEM(shape, kind) for shape, kind in shapes]
        + [pltpu.SemaphoreType.DMA((len(results),)), pltpu.SemaphoreType.DMA((len(shapes),))],
        compiler_params=pltpu.CompilerParams(vmem_limit_bytes=63 * 2**20),
        name="unpack",
    )(*results)
    return tuple(out.T if n == 6 else out for n, out in enumerate(outs))


def solution(mesh):
    in_specs = (
        P(("dp", "hid"), None, "chan"),
        P(("dp", "hid"), None, "chan"),
        P(("dp", "hid")),
        P("chan"),
        P("chan"),
        P(),
        P(),
        P(),
        P(),
        P("chan"),
        P("chan"),
        P(None, "hid"),
        P("hid"),
        P("hid", "chan"),
        P("chan"),
    )
    out_specs = (
        P(("dp", "hid"), None, "chan"),
        P(("dp", "hid"), None, "chan"),
        P("chan"),
        P("chan"),
        P(),
        P(),
        P(),
        P(),
        P("chan"),
        P("chan"),
        P(None, "hid"),
        P("hid"),
        P("hid", "chan"),
        P("chan"),
    )

    def whole(*args):
        shape = dict(mesh.shape)
        patches, token_up, chan_up = args[0].shape, args[5].shape, args[11].shape
        local = (patches[0] // (shape["dp"] * shape["hid"]), patches[1], patches[2] // shape["chan"])
        o = Sizes(shape, local, (chan_up[0], chan_up[1] // shape["hid"]), token_up)
        mapped = jax.shard_map(
            functools.partial(body, o), mesh=mesh, in_specs=in_specs, out_specs=out_specs, check_vma=False
        )
        return mapped(*args)

    return whole
```

```python
import functools

import jax
import jax.numpy as jnp
from jax import lax
from jax.experimental import pallas as pl
from jax.experimental.pallas import tpu as pltpu
from jax.sharding import PartitionSpec as P

EPS = 1e-06
BF = jnp.bfloat16
F32 = jnp.float32
MESH = pl.DeviceIdType.MESH
TANH_A = 0.7978845608028654
TANH_B = TANH_A * 0.044715


def nn(left, right):
    return lax.dot_general(left, right, (((1,), (0,)), ((), ())), preferred_element_type=F32)


def nt(left, right):
    return lax.dot_general(left, right, (((1,), (1,)), ((), ())), preferred_element_type=F32)


def tn(left, right):
    return lax.dot_general(left, right, (((0,), (0,)), ((), ())), preferred_element_type=F32)


def gelu_pair(v):
    square = v * v
    tanh = jnp.tanh(v * (TANH_A + TANH_B * square))
    half = 0.5 + 0.5 * tanh
    value = v * half
    slope = half + value * (1.0 - tanh) * (TANH_A + 3.0 * TANH_B * square)
    return value, slope


def pad_to(count, unit):
    return -(-count // unit) * unit


WAYS = {
    (0, 0): ("yxz", "nr"),
    (0, 1): ("xyz", "gr"),
    (1, 0): ("myxz", "nr"),
    (1, 1): ("xyz", "gr"),
    (2, 0): ("mzxy", "nr"),
    (2, 1): ("xyz", "gr"),
}
PLAN = {
    ("O", 0, 1): ((0, 1), (0, 0)),
    ("M", 2, 0): ((2, 0), (1, 0)),
    ("O", 1): ((0, 0), (2, 0), (0, 0), (0, 1)),
    ("O", 1, 1): ((1, 0),),
    ("O", 2, 1): ((1, 1), (0, 0), (2, 0)),
    ("rows",): ((0, 0), (0, 1)),
    ("residual",): ((2, 0), (1, 0)),
    ("outputs",): ((1, 0),),
    ("own", 0): ((0, 0),),
    ("own", 1): ((2, 0), (1, 1), (1, 0), (2, 1)),
    ("own", 2): ((0, 0), (2, 0)),
    ("other", 0): ((0, 1), (0, 0), (1, 1), (2, 0)),
    ("other", 1): ((1, 0),),
    ("token other",): (
        (2, 1), (0, 1), "small", "mixed", (2, 0), (1, 1), (0, 1), (1, 0), (2, 1), "small", (1, 1), (2, 1),
        (2, 0), (1, 1), (0, 1), "small", (0, 0),
    ),
    ("norm",): ((1, 0), (2, 1), "small", (2, 1), (2, 0), (1, 1)),
    ("end",): ("small", (2, 1), (1, 0)),
}


class Sizes:
    def __init__(self, mesh_shape, patches, chan_up, token_up):
        self.dp = mesh_shape["dp"]
        self.hid = mesh_shape["hid"]
        self.xs = self.hid // 2
        self.images, self.s, self.l = patches
        self.ps = pad_to(self.s + 1, 16)
        self.wide = pad_to(self.ps, 128)
        self.d = 2 * self.l
        self.own = self.images // 2
        self.f = chan_up[1]
        self.ds = token_up[1]
        self.levels = self.dp.bit_length() - 1
        third = self.f // 3
        self.fetches = ((0, third), (third, 2 * third)) if self.f % 768 == 0 else ((0, self.f),)
        self.parts = tuple((n, third) for n in range(0, self.f, third)) if self.f % 768 == 0 else self.fetches
        self.units = [(part, kind) for part in range(len(self.parts)) for kind in range(2)]
        self.ways = {unit: ("xyz", "n") for unit in self.units}
        self.plan = {("O",) + unit: (unit,) for unit in self.units}
        if (self.xs, len(self.parts), self.levels) == (2, 3, 2):
            self.ways, self.plan = WAYS, PLAN
        self.chan_first = [unit for unit in self.units if self.ways[unit][0] in ("yxz", "myxz")]
        self.dp_first = [unit for unit in self.units if self.ways[unit][0] in ("zxy", "mzxy")]
        self.loads = 16
        self.plane = 2 * self.hid
        self.blocks = -(-self.f // self.l)
        self.vec_wide = max(self.f, self.l)
        groups = 3 + self.hid * self.blocks
        self.vec_row = 2 * self.ps
        self.small = pad_to(self.vec_row + 8 * groups, 64 * self.xs)
        self.groups = (self.small - self.vec_row) // 8
        self.piece = self.small // (4 * self.xs)
        assert self.own >= 3 and mesh_shape["chan"] == 2 and self.hid % 2 == 0 and self.images % 2 == 0 and self.images <= 8
        assert 1 << self.levels == self.dp and self.f % self.l == 0 and self.ds == self.l


def kernel(o, *refs):
    names = iter(refs)

    def get(count):
        return [next(names) for _ in range(count)]

    P_ = len(o.parts)
    live_hbm, patches_ref, cot_ref, tup_hbm, tdn_hbm, chan_up_ref, chan_down_ref = get(7)
    vector_hbm = get(8)
    mixed_out, grad_out, small_hbm = get(3)
    up_hbm, dn_hbm = get(P_), get(P_)
    vector_v = get(8)
    live_ref, tup_ref, tdn_ref, vec_ref, small_out = get(5)
    fin_up, fin_dn = get(P_), get(P_)
    pat, cot, cot_in, stats, stats_in, means, means2, up_s, ut_s, dn_s, dt_s, tdb_s = get(12)
    tin, th, tslope, msend, mrecv, rows_m, rows_n, inv2, vec_in = get(9)
    xs_all, gs_all, w_up, w_dn, w_b, hid_s, pg_s, out_own, ng_own, stage, ng_in, out_in = get(12)
    blow, gacc, vecs, small_send, small_c, small_p, small_in, small_z = get(8)
    (gm,) = get(1)
    gb, rx, yb, ry = get(P_), get(P_), get(P_), get(P_)
    zb, rz = dict(zip(o.units, get(2 * P_))), dict(zip(o.units, get(2 * P_)))
    ryo = {unit: next(names) for unit in o.chan_first}
    rzo = {unit: next(names) for unit in o.dp_first}
    loc_sem, send_sem, recv_sem = get(3)

    z = lax.axis_index("dp")
    y = lax.axis_index("chan")
    h = lax.axis_index("hid")
    c = h % 2
    x = h // 2
    S, PS, L, OWN, IM, X, F, N = o.s, o.ps, o.l, o.own, o.images, o.xs, o.f, o.dp
    width = float(o.d)
    here = y * o.hid + h
    bit = z % 2

    def dev(zz=None, yy=None, xx=None, cc=None):
        zz = z if zz is None else zz
        yy = y if yy is None else yy
        xx = x if xx is None else xx
        cc = c if cc is None else cc
        return (zz, yy, xx * 2 + cc)

    partner = dev(yy=1 - y)
    sibling = dev(cc=1 - c)
    z_pair = dev(zz=z + 1 - 2 * bit)
    counter = [0]

    def take(count=1):
        base = counter[0]
        counter[0] += count
        return base

    def remote(src, dst, device, index=None):
        index = take() if index is None else index
        return pltpu.make_async_remote_copy(
            src_ref=src, dst_ref=dst, send_sem=send_sem.at[index], recv_sem=recv_sem.at[index],
            device_id=device, device_id_type=MESH,
        )

    def send(src, dst, device):
        copy = remote(src, dst, device)
        copy.start()
        return copy

    barrier = pltpu.get_barrier_semaphore()
    for step in range(1, o.plane):
        there = (here + step) % o.plane
        pl.semaphore_signal(barrier, inc=1, device_id=(z, there // o.hid, there % o.hid), device_id_type=MESH)
    for step in range(1, N):
        pl.semaphore_signal(barrier, inc=1, device_id=((z + step) % N, y, h), device_id_type=MESH)

    loads = []

    def load(src, dst):
        copy = pltpu.make_async_copy(src, dst, loc_sem.at[len(loads)])
        loads.append(copy)
        copy.start()
        return copy

    stores = []

    def store(src, dst):
        copy = pltpu.make_async_copy(src, dst, loc_sem.at[o.loads + len(stores)])
        copy.start()
        stores.append(copy)

    load_vectors = [load(src, dst) for src, dst in zip(vector_hbm, vector_v)]
    load_live = load(live_hbm, live_ref)
    load_token = [load(tup_hbm, tup_ref), load(tdn_hbm, tdn_ref)]
    load_pat = load(patches_ref, pat)
    load_cot = load(cot_ref.at[pl.ds(y * OWN, OWN)], cot)
    load_up0 = load(chan_up_ref.at[pl.ds(pl.multiple_of(y * L, L), L)], w_up.at[0, pl.ds(0, L)])
    load_up1 = load(chan_up_ref.at[pl.ds(pl.multiple_of((1 - y) * L, L), L)], w_up.at[0, pl.ds(L, L)])
    load_dn = load(chan_down_ref, w_dn.at[0, :, pl.ds(0, L)])

    pad = PS - S
    pad_row = lax.broadcasted_iota(jnp.int32, (pad, L), 0)
    one_row = jnp.where(pad_row == 0, 1.0, 0.0).astype(BF)
    for j in range(IM):
        tin[j, S:PS, :] = one_row
    for i in range(OWN):
        xs_all[c, i, S:PS, :] = jnp.zeros((pad, o.d), BF)
        gs_all[c, i, S:PS, :] = jnp.zeros((pad, o.d), BF)
        rows_n[i, S:PS, :] = jnp.zeros((pad, o.d), F32)
        rows_m[i, S:PS, :] = jnp.zeros((pad, o.d), BF)
        inv2[i, S:PS, :] = jnp.zeros((pad, 1), F32)
    vecs[...] = jnp.zeros(vecs.shape, F32)
    gacc[...] = jnp.zeros(gacc.shape, F32)
    vec_ref[...] = jnp.zeros(vec_ref.shape, F32)
    for n, copy in enumerate(load_vectors):
        copy.wait()
        count = vector_v[n].shape[0]
        vec_ref[n:n + 1, :count] = vector_v[n][...].astype(F32).reshape(1, count)
    for copy in load_token:
        copy.wait()
    w_b[0, 0:1, :] = vec_ref[7:8, :]
    up_bias, down_bias_row = vec_ref[5:6, :L], vec_ref[6:7, :L]
    last = jnp.zeros((o.wide - S - 1, L), F32)
    up_full = jnp.concatenate([tup_ref[...].astype(F32), up_bias, last], 0)
    up_s[...] = up_full[:PS].astype(BF)
    ut_s[...] = up_full.T[:, :PS].astype(BF)
    dn_full = jnp.concatenate([tdn_ref[...].astype(F32), jnp.zeros((o.wide - S, L), F32)], 0)
    dn_s[...] = dn_full.T[:, :PS].astype(BF)
    dt_s[...] = dn_full[:PS].astype(BF)
    tdb_s[...] = jnp.concatenate([down_bias_row, jnp.zeros((127, L), F32)], 0).T[:PS]

    lane = lax.broadcasted_iota(jnp.int32, (S, 128), 1)
    load_pat.wait()

    def note(table, j, first, second):
        table = jnp.where(lane == j, first, table)
        return jnp.where(lane == j + 8, second, table)

    def across(table):
        rest = jnp.zeros((o.wide - S, 128), F32)
        return jnp.concatenate([table, rest], 0).T[:16]

    def along(table):
        return jnp.concatenate([table, jnp.zeros((112, o.wide), F32)], 0).T

    def sums_of(j, table):
        v = pat[j].astype(F32)
        return note(table, j, jnp.sum(v, -1, keepdims=True), jnp.sum(v * v, -1, keepdims=True))

    stats[0] = across(lax.fori_loop(0, IM, sums_of, jnp.zeros((S, 128), F32)))

    pl.semaphore_wait(barrier, o.plane - 1 + N - 1)

    copy_stats = send(stats.at[0], stats_in.at[0], partner)
    copy_vec = send(vec_ref, vec_in, partner)
    near = pl.ds(bit * L, L)
    near_from = pl.ds(pl.multiple_of(((y + bit) % 2) * L, L), L)
    copy_b = {step: send(w_b.at[0], w_b.at[step], dev(xx=(x + step) % X)) for step in range(1, X)}
    copy_w = {}
    copy_f = {}

    def weight_rows(part):
        start, size = o.fetches[part]
        return pl.ds(pl.multiple_of(start + bit * (size // 2), 16), size // 2)

    def weight_spans(step, part):
        start, size = o.fetches[part]
        cols, rows_dn = pl.ds(start, size), weight_rows(part)
        rows_own = pl.ds(start, size) if part else rows_dn
        return (
            (chan_up_ref.at[near_from, cols], w_up.at[step, near, cols], y),
            (chan_down_ref.at[rows_own], w_dn.at[step, rows_own, pl.ds(0, L)], y),
            (chan_down_ref.at[rows_dn], w_dn.at[step, rows_dn, pl.ds(L, L)], 1 - y),
        )

    def fetch(part, which):
        for step in range(1, X):
            for n in which if part < len(o.fetches) else ():
                src, dst, yy = weight_spans(step, part)[n]
                if part and n == 2:
                    src, yy = w_dn.at[0, weight_rows(part), pl.ds(L, L)], y
                copy_w[step, part, n] = send(src, dst, dev(xx=(x + step) % X, yy=yy))

    def hand_on(part, which):
        for step in range(1, X):
            for n in which if part < len(o.fetches) else ():
                dst = weight_spans(step, part)[n][1]
                if part and n == 1:
                    copy_f[step, part, n] = copy_w[step, part, n]
                else:
                    copy_w[step, part, n].wait()
                    copy_f[step, part, n] = send(dst, dst, z_pair)

    def want(group, which):
        for step in range(1, X):
            for n in which:
                copy_f[step, group, n].wait()

    quarter = F // 4
    bit2 = (z // 2) % 2
    z_far = dev(zz=z + 2 - 4 * bit2)

    def dn2_span(first, count):
        return pl.ds(pl.multiple_of(first * quarter, 16), count * quarter)

    dn2_mine = dn2_span(bit * 2 + bit2, 1)
    dn2_half = dn2_span(bit * 2, 2)
    copy_dn2 = [send(chan_down_ref.at[dn2_mine], w_dn.at[0, dn2_mine, pl.ds(L, L)], partner)]

    def dn2_on(span, peer):
        copy_dn2[-1].wait()
        ref = w_dn.at[0, span, pl.ds(L, L)]
        copy_dn2.append(send(ref, ref, peer))

    fetch(0, (0,))
    cot_sems = take(OWN)

    def copy_cot(i):
        return remote(cot_ref.at[(1 - y) * OWN + i], cot_in.at[i], partner, cot_sems + i)

    fetch(0, (1, 2))
    copy_cot(0).start()

    copy_stats.wait()
    total = (stats[0] + stats_in[0]) * (1.0 / width)
    mean, square = total[:8], total[8:]
    means[...] = along(jnp.concatenate([mean, lax.rsqrt(square - mean * mean + EPS)], 0))
    fetch(1, (0,))

    def column(table, j):
        return jnp.sum(jnp.where(lane == j, table, 0.0), -1, keepdims=True)

    first_gain = vec_ref[0:1, :L]
    first_shift = vec_ref[1:2, :L]

    def first_norm(j):
        table = means[:S, :]
        inv_one = column(table, j + 8)
        return (pat[j].astype(F32) - column(table, j)) * inv_one, inv_one

    def token_forward(j):
        normed, _ = first_norm(j)
        tin[j, :S, :] = (normed * first_gain + first_shift).astype(BF)
        value, slope = gelu_pair(nn(ut_s[...], tin[j]))
        th[j] = value.astype(BF)
        tslope[j] = slope.astype(BF)
        back = nn(dt_s[...], th[j])
        return pat[j].astype(F32) + back[:S] + tdb_s[:S, 0:1]

    mixed_sems = take(OWN)

    def copy_mixed(i):
        return remote(msend.at[i], mrecv.at[i], partner, mixed_sems + i)

    @pl.loop(0, OWN)
    def _(i):
        msend[i] = token_forward((1 - y) * OWN + i).astype(BF)
        copy_mixed(i).start()

    copy_cot(1).start()
    dn2_on(dn2_mine, z_far)
    hand_on(0, (0,))

    @pl.loop(0, OWN)
    def _(i):
        rows_n[i, :S, :L] = token_forward(y * OWN + i)

    hand_on(0, (1, 2))
    fetch(1, (1,))
    dn2_on(dn2_half, z_pair)
    copy_vec.wait()
    both = [jnp.concatenate([vec_ref[n:n + 1, :L], vec_in[n:n + 1, :L]], axis=1) for n in range(2, 5)]
    second_gain, second_shift, down_bias = both
    row_sems = take(OWN)

    def copy_rows(i):
        return remote(xs_all.at[c, i], xs_all.at[c, i], sibling, row_sems + i)

    def second_norm(i):
        copy_mixed(i).wait()
        rows_n[i, :S, L:] = mrecv[i].astype(F32)
        v = rows_n[i, :S, :]
        mean = jnp.sum(v, -1, keepdims=True) * (1.0 / width)
        spread = jnp.sum(v * v, -1, keepdims=True) * (1.0 / width) - mean * mean
        inv_two = lax.rsqrt(spread + EPS)
        normed = (v - mean) * inv_two
        rows_m[i, :S, :] = v.astype(BF)
        inv2[i, :S, :] = inv_two
        rows_n[i, :S, :] = normed
        xs_all[c, i, :S, :] = (normed * second_gain + second_shift).astype(BF)
        copy_rows(i).start()

    load_cot.wait()
    load_live.wait()
    live = live_ref[0]
    gs_sems = take(OWN)

    def keep_of(j):
        return jnp.where(j < live, 1.0, 0.0).astype(F32)

    def copy_gs(i):
        return remote(gs_all.at[c, i], gs_all.at[c, i], sibling, gs_sems + i)

    def out_grads(i):
        copy_cot(i).wait()
        keep = keep_of(y * OWN + i)
        gs_all[c, i, :S, :L] = (cot[i].astype(F32) * keep).astype(BF)
        gs_all[c, i, :S, L:] = (cot_in[i].astype(F32) * keep).astype(BF)
        copy_gs(i).start()

    rows = OWN * PS

    def inner(step, start, size, i, sums):
        cols, block = pl.ds(start, size), pl.ds(pl.multiple_of(i * PS, 16), PS)
        pre = nn(xs_all[:, i].reshape(2 * PS, o.d), w_up[step, :, cols]) + w_b[step, 0:1, cols]
        value, slope = gelu_pair(pre)
        hid_s[step, :, block, cols] = value.astype(BF).reshape(2, PS, size)
        grad = (nt(gs_all[:, i].reshape(2 * PS, o.d), w_dn[step, cols, :]) * slope).astype(BF)
        pg_s[step, :, block, cols] = grad.reshape(2, PS, size)
        return sums + jnp.sum(grad.astype(F32), 0, keepdims=True)

    def bias_sums(step, start, size, sums):
        group = 3 + ((x + X - step) % X * 2 + c) * o.blocks
        for n in range(start, start + size, 128):
            block, lanes = n // L, n % L
            vecs[group + block, 0:1, lanes:lanes + 128] = sums[:, n - start:n - start + 128]

    def own_hidden(cc, i):
        block = pl.ds(pl.multiple_of(i * PS, 16), PS)
        value, slope = gelu_pair(nn(xs_all[cc, i], w_up[0]) + w_b[0, 0:1, :])
        hid_s[0, cc, block, :] = value.astype(BF)
        for n in range(o.blocks):
            first = ((cc * o.blocks + n) * OWN + i) * PS
            gm[pl.ds(pl.multiple_of(first, 16), PS), :] = slope[:, n * L:(n + 1) * L]

    def own_back(i, sums):
        block = pl.ds(pl.multiple_of(i * PS, 16), PS)
        grad = nt(gs_all[:, i].reshape(2 * PS, o.d), w_dn[0])
        for cc in range(2):
            slopes = []
            for n in range(o.blocks):
                first = ((cc * o.blocks + n) * OWN + i) * PS
                slopes.append(gm[pl.ds(pl.multiple_of(first, 16), PS), :])
            mine = (grad[cc * PS:(cc + 1) * PS] * jnp.concatenate(slopes, 1)).astype(BF)
            pg_s[0, cc, block, :] = mine
            sums = sums + jnp.sum(mine.astype(F32), 0, keepdims=True)
        return sums

    def own_forward(i):
        own_hidden(c, i)
        copy_rows(i).wait()
        own_hidden(1 - c, i)

    def other_slots_first(i):
        for step in range(1, X):
            sums_o[step] = inner(step, start0, size0, i, sums_o[step])

    start0, size0 = o.fetches[0]
    sums_o = [jnp.zeros((1, size0), F32)] * X
    sums_m = jnp.zeros((1, F), F32)
    load_up0.wait()
    load_up1.wait()
    load_dn.wait()
    second_norm(0)
    copy_cot(2).start()
    own_forward(0)
    out_grads(0)
    second_norm(1)
    hand_on(1, (0, 1))
    own_forward(1)
    for i in range(2, OWN):
        second_norm(i)
        own_forward(i)
    want(0, (0, 1, 2))
    for step in range(1, X):
        copy_b[step].wait()
    copy_gs(0).wait()
    other_slots_first(0)
    out_grads(1)
    copy_dn2[-1].wait()
    fetch(1, (2,))
    sums_m = own_back(0, sums_m)
    copy_gs(1).wait()
    other_slots_first(1)
    for i in range(2, OWN):
        out_grads(i)
        sums_m = own_back(i - 1, sums_m)
        copy_gs(i).wait()
        other_slots_first(i)
    for step in range(1, X):
        bias_sums(step, start0, size0, sums_o[step])

    def levels():
        start, count, used = 0, N, 0
        for level in range(o.levels):
            side_bit = (z // (1 << level)) % 2
            peer = dev(zz=z + (1 - 2 * side_bit) * (1 << level))
            count //= 2
            yield start + side_bit * count, start + (1 - side_bit) * count, count, used, peer
            start = start + side_bit * count
            used += count

    def my_segment():
        return list(levels())[-1][0]

    def gm_rows(part, kind, half, span):
        start, size = o.parts[part]
        seg = size // N
        first = 4 * start + (2 * kind + half) * size
        return pl.ds(pl.multiple_of(first + span.start * seg, 8), span.size * seg)

    def gm_get(part, kind, half, span):
        seg = o.parts[part][1] // N
        return gm[gm_rows(part, kind, half, span), :].reshape(span.size, seg, L)

    def gm_set(part, kind, half, span, value):
        gm[gm_rows(part, kind, half, span), :] = value.reshape(-1, L)

    def add(part, kind, half, span, *terms):
        mine = gm_get(part, kind, half, span)
        for term in terms:
            mine = mine + term.astype(F32)
        gm_set(part, kind, half, span, mine)

    everything = pl.ds(0, N)
    low, high = pl.ds(0, N // 2), pl.ds(N // 2, N // 2)

    def finals(part, kind):
        if kind == 0:
            return [fin_up[part].at[0], fin_up[part].at[1]]
        return [fin_dn[part]]

    def reduce_rec(part, kind, halves):
        out, land = zb[part, kind], rz[part, kind]
        for keep_at, send_at, count, used, peer in levels():
            span = pl.ds(used, count)
            copies = []
            for half in range(halves):
                out[half, span] = gm_get(part, kind, half, pl.ds(send_at, count)).astype(BF)
                copies.append(send(out.at[half, span], land.at[half, span], peer))
            yield
            for half in range(halves):
                copies[half].wait()
                add(part, kind, half, pl.ds(keep_at, count), land[half, span])

    def gather_rec(part, kind):
        own = pl.ds(my_segment(), 1)
        done = finals(part, kind)
        early = kind == 0 and o.ways[part, kind][1] == "g"
        done[0][own] = gm_get(part, kind, 0, own).astype(BF)
        if early:
            copy = send(done[0].at[own], done[1].at[own], partner)
            yield
            copy.wait()
        for keep_at, _, count, _, peer in reversed(list(levels())):
            span = pl.ds(keep_at, count)
            copies = [send(ref.at[span], ref.at[span], peer) for ref in done[:1 + early]]
            yield
            for copy in copies:
                copy.wait()
        if kind == 0 and not early:
            copy = send(done[0], done[1], partner)
            yield
            copy.wait()

    def owner(n):
        return dev(xx=(x + X - 1 - n) % X)

    def start_x(part, kind):
        return [send(gb[part].at[n, kind], rx[part].at[n, kind], owner(n)) for n in range(X - 1)]

    def send_y(part, kind, span):
        yb[part][kind, span] = gm_get(part, kind, 1, span).astype(BF)
        return send(yb[part].at[kind, span], ry[part].at[kind, span], partner)

    def wait_all(copies):
        for copy in copies:
            copy.wait()

    def add_x(part, kind, half, span):
        add(part, kind, half, span, *[rx[part][n, kind, half, span] for n in range(X - 1)])

    def chunk_xyz(part, kind):
        copies = start_x(part, kind)
        yield
        wait_all(copies)
        add_x(part, kind, 1, everything)
        copy = send_y(part, kind, everything)
        add_x(part, kind, 0, everything)
        yield
        copy.wait()
        add(part, kind, 0, everything, ry[part][kind])
        yield from reduce_rec(part, kind, 1)
        yield from gather_rec(part, kind)

    def chunk_xzy(part, kind):
        copies = start_x(part, kind)
        yield
        wait_all(copies)
        add_x(part, kind, 1, everything)
        add_x(part, kind, 0, everything)
        yield from reduce_rec(part, kind, 2)
        own = pl.ds(my_segment(), 1)
        copy = send_y(part, kind, own)
        yield
        copy.wait()
        add(part, kind, 0, own, ry[part][kind, own])
        yield from gather_rec(part, kind)

    def start_yo(part, kind):
        return [send(gb[part].at[n, kind, 1], ryo[part, kind].at[n], partner) for n in range(X - 1)]

    def pass_yo(part, kind, copies):
        wait_all(copies)
        for n in range(X - 1):
            mine = gb[part][n, kind, 0].astype(F32) + ryo[part, kind][n].astype(F32)
            gb[part][n, kind, 0] = mine.astype(BF)
        return [send(gb[part].at[n, kind, 0], rx[part].at[n, kind, 0], owner(n)) for n in range(X - 1)]

    def end_yx(part, kind, copies, copy):
        copy.wait()
        wait_all(copies)
        add(part, kind, 0, everything, ry[part][kind], *[rx[part][n, kind, 0] for n in range(X - 1)])
        yield from reduce_rec(part, kind, 1)
        yield from gather_rec(part, kind)

    def chunk_yxz(part, kind):
        copies = start_yo(part, kind)
        yield
        copies = pass_yo(part, kind, copies)
        yield
        copy = send_y(part, kind, everything)
        yield
        yield from end_yx(part, kind, copies, copy)

    def chunk_myxz(part, kind):
        copy = send_y(part, kind, everything)
        yield
        copies = start_yo(part, kind)
        yield
        copies = pass_yo(part, kind, copies)
        yield
        yield from end_yx(part, kind, copies, copy)

    def reduce_others(part, kind):
        land = rzo[part, kind]
        for keep_at, send_at, count, used, peer in levels():
            copies = {}
            span = pl.ds(used, count)
            for n in range(X - 1):
                for half in range(2):
                    src = gb[part].at[n, kind, half, pl.ds(send_at, count)]
                    copies[n, half] = send(src, land.at[n, half, span], peer)
            yield
            for n in range(X - 1):
                for half in range(2):
                    copies[n, half].wait()
                    keep = pl.ds(keep_at, count)
                    mine = gb[part][n, kind, half, keep].astype(F32) + land[n, half, span].astype(F32)
                    gb[part][n, kind, half, keep] = mine.astype(BF)

    def segment_x(part, kind):
        own = pl.ds(my_segment(), 1)
        return [send(gb[part].at[n, kind, :, own], rx[part].at[n, kind, :, own], owner(n)) for n in range(X - 1)]

    def end_zx(part, kind, copies):
        own = pl.ds(my_segment(), 1)
        wait_all(copies)
        add_x(part, kind, 1, own)
        copy = send_y(part, kind, own)
        add_x(part, kind, 0, own)
        yield
        copy.wait()
        add(part, kind, 0, own, ry[part][kind, own])
        yield from gather_rec(part, kind)

    def chunk_zxy(part, kind):
        yield from reduce_others(part, kind)
        copies = segment_x(part, kind)
        yield
        yield from reduce_rec(part, kind, 2)
        yield from end_zx(part, kind, copies)

    def chunk_mzxy(part, kind):
        yield from reduce_rec(part, kind, 2)
        yield from reduce_others(part, kind)
        copies = segment_x(part, kind)
        yield
        yield from end_zx(part, kind, copies)

    chunk = {
        "xyz": chunk_xyz, "xzy": chunk_xzy, "yxz": chunk_yxz, "myxz": chunk_myxz, "zxy": chunk_zxy, "mzxy": chunk_mzxy
    }
    pipes = {unit: chunk[o.ways[unit][0]](*unit) for unit in o.units}

    def step_of(name):
        if name in pipes:
            try:
                next(pipes[name])
            except StopIteration:
                del pipes[name]
                if name == "small":
                    store(small_out, small_hbm)
                elif name != "mixed":
                    part, kind = name
                    store(*((fin_up[part], up_hbm[part]), (fin_dn[part], dn_hbm[part]))[kind])

    def at(*point):
        for name in o.plan.get(point, ()):
            step_of(name)

    def weight_grad(step, part, kind):
        start, size = o.parts[part]
        cols = pl.ds(start, size)
        left, right = (pg_s, xs_all) if kind == 0 else (hid_s, gs_all)
        grad = tn(left[step, :, :, cols].reshape(2 * rows, size), right[...].reshape(2 * rows, o.d))
        grad = grad.reshape(N, size // N, o.d)
        for half in range(2):
            block = grad[:, :, half * L:(half + 1) * L]
            if step:
                gb[part][step - 1, kind, half] = block.astype(BF)
            else:
                gm_set(part, kind, half, everything, block)

    def other_slots(group):
        start, size = o.fetches[group]
        if group:
            want(group, (0, 1, 2))
            for step in range(1, X):
                sums = lax.fori_loop(
                    0, OWN, lambda i, t, step=step: inner(step, start, size, i, t), jnp.zeros((1, size), F32)
                )
                bias_sums(step, start, size, sums)
        at("O", group)
        for part in range(P_):
            if start <= o.parts[part][0] < start + size:
                for kind in range(2):
                    for step in range(1, X):
                        weight_grad(step, part, kind)
                    if part + kind == 0:
                        hand_on(1, (2,))
                    at("O", part, kind)

    other_slots(0)
    sums_m = own_back(OWN - 1, sums_m)
    bias_sums(0, 0, F, sums_m)
    at("M")
    for part in range(P_):
        for kind in range(2):
            weight_grad(0, part, kind)
            at("M", part, kind)
    for group in range(1, len(o.fetches)):
        other_slots(group)
    at("O")

    def row_sums(kind, cc):
        left, right, dot = ((pg_s, w_up, nt), (hid_s, w_dn, nn))[kind]
        total = dot(left[0, cc], right[0])
        for step in range(1, X):
            total = total + dot(left[step, cc], right[step])
        return total

    stage[0] = row_sums(0, 1 - c).astype(BF)
    copy_ng = send(stage.at[0], ng_in, sibling)
    mine = row_sums(0, c)
    ng_own[0] = mine[:, :L]
    ng_own[1] = mine[:, L:]
    at("rows")

    res_sems = take(OWN)

    def copy_res(i):
        return remote(mrecv.at[i], blow.at[y * OWN + i], partner, res_sems + i)

    copy_ng.wait()

    def residual(i, sums):
        block = pl.ds(pl.multiple_of(i * PS, 16), PS)
        ng = jnp.concatenate([ng_own[0, block, :], ng_own[1, block, :]], 1) + ng_in[block, :].astype(F32)
        normed = rows_n[i]
        back = gs_all[c, i].astype(F32)
        sums = (
            sums[0] + jnp.sum(ng * normed, 0, keepdims=True),
            sums[1] + jnp.sum(ng, 0, keepdims=True),
            sums[2] + jnp.sum(back, 0, keepdims=True),
        )
        q = ng * second_gain
        m1 = jnp.sum(q, -1, keepdims=True) * (1.0 / width)
        m2 = jnp.sum(q * normed, -1, keepdims=True) * (1.0 / width)
        res = (back + inv2[i] * (q - m1 - normed * m2)).astype(BF)
        mrecv[i] = res[:S, L:]
        copy_res(i).start()
        blow[y * OWN + i] = res[:S, :L]
        return sums

    zero = jnp.zeros((1, o.d), F32)
    sums = lax.fori_loop(0, OWN, residual, (zero, zero, zero))
    for n in range(3):
        vecs[0, 1 + 2 * n:2 + 2 * n, :] = jnp.where(y == 0, sums[n][:, :L], sums[n][:, L:])
        vecs[0, 2 + 2 * n:3 + 2 * n, :] = jnp.where(y == 0, sums[n][:, L:], sums[n][:, :L])
    at("residual")

    stage[1] = row_sums(1, 1 - c).astype(BF)
    copy_out = send(stage.at[1], out_in, sibling)
    at("outputs 0")
    out_own[...] = row_sums(1, c)

    copy_mo = remote(msend, mixed_out.at[pl.ds(y * OWN, OWN)], partner)

    def output_rows():
        copy_out.wait()

        @pl.loop(0, OWN)
        def _(i):
            block = pl.ds(pl.multiple_of(i * PS, 16), PS)
            branch = out_own[block, :] + out_in[block, :].astype(F32) + down_bias
            result = (keep_of(y * OWN + i) * (rows_m[i].astype(F32) + branch)).astype(BF)
            msend[i] = result[:S, L:]
            cot[i] = result[:S, :L]

        copy_mo.start()
        store(cot, mixed_out.at[pl.ds(y * OWN, OWN)])
        yield

    pipes["mixed"] = output_rows()
    at("outputs")

    ones = jnp.ones((16, L), BF)

    def scaled(j):
        return j // OWN, pl.ds(pl.multiple_of(j % OWN * PS, 16), PS)

    def token_backward(j, carry):
        table, sum_gain, sum_shift, sum_bias = carry
        low_grad = blow[j]
        grad = (nn(dn_s[:, :S], low_grad) * tslope[j].astype(F32)).astype(BF)
        gacc[0] += nt(tin[j], grad)
        gacc[1, :S, :] += nt(low_grad, th[j])
        sum_bias = sum_bias + nt(ones, low_grad)
        back = nn(up_s[...], grad)
        normed, _ = first_norm(j)
        sum_gain = sum_gain + jnp.sum(back[:S] * normed, 0, keepdims=True)
        sum_shift = sum_shift + jnp.sum(back[:S], 0, keepdims=True)
        back = back * first_gain
        ng_own[scaled(j)] = back
        back = back[:S]
        table = note(table, j, jnp.sum(back, -1, keepdims=True), jnp.sum(back * normed, -1, keepdims=True))
        return table, sum_gain, sum_shift, sum_bias

    carry = (jnp.zeros((S, 128), F32), jnp.zeros((1, L), F32), jnp.zeros((1, L), F32), jnp.zeros((16, S), F32))
    for i in range(OWN):
        carry = token_backward(y * OWN + i, carry)
        at("own", i)

    for i in range(OWN):
        copy_res(i).wait()
        carry = token_backward((1 - y) * OWN + i, carry)
        if i < OWN - 1:
            at("other", i)
    table, sum_gain, sum_shift, sum_bias = carry
    stats[1] = across(table)
    copy_stats2 = send(stats.at[1], stats_in.at[1], partner)
    vecs[0, 0:1, :S] = sum_bias[0:1, :]
    vecs[1 + y, 0:1, :] = sum_gain
    vecs[1 + y, 1:2, :] = sum_shift

    half_small = o.small // 2
    spot = y * X + x
    chips = 2 * X

    def chip_peers():
        for step in range(1, chips):
            there = (spot + step) % chips
            yield step, there, dev(yy=there // X, xx=there % X)

    def piece(n):
        return pl.ds(pl.multiple_of(n * o.piece, 16), o.piece)

    def share(cc):
        return pl.ds(pl.multiple_of(cc * half_small, 16), half_small)

    def out_piece(n):
        return pl.ds(pl.multiple_of(c * half_small + n * o.piece, 16), o.piece)

    small_send[0:PS, :] = gacc[0]
    small_send[PS:2 * PS, :] = gacc[1]
    small_send[o.vec_row:, :] = vecs[...].reshape(8 * o.groups, L)

    def reduce_small():
        copy = send(small_send.at[share(1 - c)], small_c, sibling)
        yield
        copy.wait()
        small_p[...] = (small_send[share(c), :] + small_c[...]).astype(BF)
        copies = [send(small_p.at[piece(there)], small_in.at[n - 1], peer) for n, there, peer in chip_peers()]
        yield
        for copy in copies:
            copy.wait()
        mine = small_p[piece(spot), :].astype(F32)
        for n in range(1, chips):
            mine = mine + small_in[n - 1].astype(F32)
        small_z[z] = mine.astype(BF)
        copies = [send(small_z.at[z], small_z.at[z], dev(zz=(z + n) % N)) for n in range(1, N)]
        yield
        for copy in copies:
            copy.wait()
        mine = small_z[0].astype(F32)
        for n in range(1, N):
            mine = mine + small_z[n].astype(F32)
        small_out[out_piece(spot), :] = mine.astype(BF)
        span = small_out.at[out_piece(spot)]
        copies = [send(span, span, peer) for _, _, peer in chip_peers()]
        yield
        for copy in copies:
            copy.wait()
        span = small_out.at[share(c)]
        copy = send(span, span, sibling)
        yield
        copy.wait()

    pipes["small"] = reduce_small()
    step_of("small")
    at("token other")

    copy_stats2.wait()
    means2[...] = along((stats[1] + stats_in[1]) * (1.0 / width))

    @pl.loop(0, IM)
    def _(j):
        normed, inv_one = first_norm(j)
        grad = ng_own[scaled(j)][:S]
        grad = grad - column(means2[:S, :], j) - normed * column(means2[:S, :], j + 8)
        blow[j] = (blow[j].astype(F32) + inv_one * grad).astype(BF)

    store(blow, grad_out)
    at("norm")

    while pipes:
        for name in list(pipes):
            step_of(name)

    copy_mo.wait()
    for copy in stores:
        copy.wait()


def block_call(o, matrices, vectors):
    I, S, PS, L, OWN, D, X, N, F = o.images, o.s, o.ps, o.l, o.own, o.d, o.xs, o.dp, o.f
    any_spec = pl.BlockSpec(memory_space=pl.ANY)
    rows = OWN * PS
    groups = len(o.fetches)
    copies = 2 + 4 + 5 * OWN + (X - 1) * (1 + 3 * groups + 3 + 2 * (groups - 1)) + 3 + 4 * X + N - 1
    for unit in o.units:
        way, order = o.ways[unit]
        early = unit[1] == 0 and order == "g"
        copies += o.levels * (1 + early) + (unit[1] == 0) + 1 + o.levels
        if way in ("zxy", "mzxy", "xzy"):
            copies += o.levels
        copies += (X - 1) * {"xyz": 1, "xzy": 1, "yxz": 2, "myxz": 2}.get(way, 2 * o.levels + 1)
    segs = [size // N for _, size in o.parts]
    outs = [
        jax.ShapeDtypeStruct((I, S, L), BF),
        jax.ShapeDtypeStruct((I, S, L), BF),
        jax.ShapeDtypeStruct((o.small, L), BF),
    ]
    outs += [jax.ShapeDtypeStruct((2, N, seg, L), BF) for seg in segs]
    outs += [jax.ShapeDtypeStruct((N, seg, L), BF) for seg in segs]
    scratch = [(vector.shape, BF) for vector in vectors]
    scratch += [None, ((S, L), BF), ((S, L), BF), ((8, o.vec_wide), F32), ((o.small, L), BF)]
    scratch += [((2, N, seg, L), BF) for seg in segs] + [((N, seg, L), BF) for seg in segs]
    scratch += [
        ((I, S, L), BF), ((OWN, S, L), BF), ((OWN, S, L), BF),
        ((2, 16, o.wide), F32), ((2, 16, o.wide), F32),
        ((o.wide, 128), F32), ((o.wide, 128), F32),
        ((PS, L), BF), ((L, PS), BF), ((L, PS), BF), ((PS, L), BF), ((PS, 128), F32),
        ((I, PS, L), BF), ((I, o.ds, L), BF), ((I, o.ds, L), BF),
        ((OWN, S, L), BF), ((OWN, S, L), BF),
        ((OWN, PS, D), BF), ((OWN, PS, D), F32), ((OWN, PS, 1), F32), ((8, o.vec_wide), F32),
        ((2, OWN, PS, D), BF), ((2, OWN, PS, D), BF),
        ((X, D, F), BF), ((X, F, D), BF), ((X, 8, o.vec_wide), F32),
        ((X, 2, rows, F), BF), ((X, 2, rows, F), BF),
        ((rows, D), F32), ((2, rows, L), F32), ((2, rows, D), BF),
        ((rows, D), BF), ((rows, D), BF),
        ((I, S, L), BF), ((2, PS, L), F32), ((o.groups, 8, L), F32),
        ((o.small, L), F32), ((o.small // 2, L), F32), ((o.small // 2, L), BF),
        ((2 * X - 1, o.piece, L), BF), ((N, o.piece, L), BF),
    ]
    blocks = [(N, seg, L) for seg in segs]
    scratch += [((4 * F, L), F32)]
    scratch += [((X - 1, 2, 2) + block, BF) for block in blocks] * 2
    scratch += [((2,) + block, BF) for block in blocks] * 2
    for _ in range(2):
        for unit in o.units:
            halves = 1 if o.ways[unit][0] in ("xyz", "yxz", "myxz") else 2
            scratch.append(((halves,) + blocks[unit[0]], BF))
    scratch += [((X - 1,) + blocks[unit[0]], BF) for unit in o.chan_first]
    scratch += [((X - 1, 2) + blocks[unit[0]], BF) for unit in o.dp_first]
    return pl.pallas_call(
        functools.partial(kernel, o),
        out_shape=outs,
        in_specs=[any_spec] * (len(matrices) + len(vectors)),
        out_specs=[any_spec] * len(outs),
        scratch_shapes=[pltpu.VMEM(*entry) if entry else pltpu.SMEM((1,), jnp.int32) for entry in scratch]
        + [pltpu.SemaphoreType.DMA((o.loads + 3 + len(o.units),)), pltpu.SemaphoreType.DMA((copies,)), pltpu.SemaphoreType.DMA((copies,))],
        compiler_params=pltpu.CompilerParams(
            collective_id=1, has_side_effects=True, vmem_limit_bytes=63 * 2**20
        ),
        name="mixer_block",
    )(*matrices, *vectors)


def unpack(o, *refs):
    P_ = len(o.parts)
    names = iter(refs)

    def get(count):
        return [next(names) for _ in range(count)]

    inputs, outputs = get(3 + 2 * P_), get(14)
    inputs_v, outputs_v = get(3 + 2 * P_), get(12)
    in_sem, out_sem = get(2)
    S, PS, L = o.s, o.ps, o.l
    y = lax.axis_index("chan")
    h = lax.axis_index("hid")
    loads = [pltpu.make_async_copy(src, dst, in_sem.at[n]) for n, (src, dst) in enumerate(zip(inputs, inputs_v))]
    outputs_v = inputs_v[:2] + outputs_v
    stores = [pltpu.make_async_copy(src, dst, out_sem.at[n]) for n, (src, dst) in enumerate(zip(outputs_v, outputs))]
    for load in loads[3:] + loads[:3]:
        load.start()
    small_in = inputs_v[2]
    fin_up, fin_dn = inputs_v[3:3 + P_], inputs_v[3 + P_:]
    _, _, fg, fs, tu, tub, td, tdb, sg, ss, cu, cub, cd, cdb = outputs_v
    for part, (start, size) in enumerate(o.parts):
        loads[3 + part].wait()
        for half in range(2):
            block = fin_up[part][half].astype(F32).reshape(size, L).T
            cu[pl.ds(pl.multiple_of((y + half) % 2 * L, L), L), start:start + size] = block
    stores[10].start()
    for part, (start, size) in enumerate(o.parts):
        loads[3 + P_ + part].wait()
        cd[start:start + size, :] = fin_dn[part][...].astype(F32).reshape(size, L)
    stores[12].start()
    for n in range(2):
        loads[n].wait()
        stores[n].start()
    loads[2].wait()
    small = small_in[...].astype(F32)
    tu[...] = small[:S]
    tub[...] = small[S:S + 1].reshape(L)
    td[...] = small[PS:PS + S]
    groups = small[o.vec_row:].reshape(o.groups, 8, L)
    tdb[...] = groups[0, 0:1, :S].reshape(S)
    for n, ref in enumerate((sg, ss, cdb)):
        ref[...] = jnp.where(y == 0, groups[0, 1 + 2 * n:2 + 2 * n], groups[0, 2 + 2 * n:3 + 2 * n]).reshape(L)
    for n, ref in enumerate((fg, fs)):
        ref[...] = jnp.where(y == 0, groups[1, n:n + 1], groups[2, n:n + 1]).reshape(L)
    totals = []
    for n in range(o.blocks):
        total = jnp.zeros((1, L), F32)
        for k in range(o.hid):
            total = jnp.where(h == k, groups[3 + k * o.blocks + n, 0:1], total)
        totals.append(total)
    cub[...] = jnp.concatenate(totals, 1).reshape(o.f)
    for n in (2, 3, 4, 5, 6, 7, 8, 9, 11, 13):
        stores[n].start()
    for copy in stores:
        copy.wait()


def body(
    o,
    patches,
    cotangent,
    live_images,
    first_gain,
    first_shift,
    token_up,
    token_up_bias,
    token_down,
    token_down_bias,
    second_gain,
    second_shift,
    chan_up,
    chan_up_bias,
    chan_down,
    chan_down_bias,
):
    S, L, D, F = o.s, o.l, o.d, o.f
    matrices = [live_images, patches, cotangent, token_up, token_down.T, chan_up, chan_down]
    vectors = [first_gain, first_shift, second_gain, second_shift, chan_down_bias, token_up_bias, token_down_bias]
    results = block_call(o, matrices, vectors + [chan_up_bias])
    any_spec = pl.BlockSpec(memory_space=pl.ANY)
    shapes = [
        (patches.shape, BF), (patches.shape, BF), ((L,), F32), ((L,), F32), ((S, L), F32), ((L,), F32),
        ((S, L), F32), ((S,), F32), ((L,), F32), ((L,), F32), ((D, F), F32), ((F,), F32), ((F, L), F32),
        ((L,), F32),
    ]
    outs = pl.pallas_call(
        functools.partial(unpack, o),
        out_shape=[jax.ShapeDtypeStruct(shape, kind) for shape, kind in shapes],
        in_specs=[any_spec] * len(results),
        out_specs=[any_spec] * len(shapes),
        scratch_shapes=[pltpu.VMEM(result.shape, BF) for result in results]
        + [pltpu.VMEM(shape, kind) for shape, kind in shapes[2:]]
        + [pltpu.SemaphoreType.DMA((len(results),)), pltpu.SemaphoreType.DMA((len(shapes),))],
        compiler_params=pltpu.CompilerParams(vmem_limit_bytes=63 * 2**20),
        name="unpack",
    )(*results)
    return tuple(out.T if n == 6 else out for n, out in enumerate(outs))


def solution(mesh):
    in_specs = (
        P(("dp", "hid"), None, "chan"),
        P(("dp", "hid"), None, "chan"),
        P(("dp", "hid")),
        P("chan"),
        P("chan"),
        P(),
        P(),
        P(),
        P(),
        P("chan"),
        P("chan"),
        P(None, "hid"),
        P("hid"),
        P("hid", "chan"),
        P("chan"),
    )
    out_specs = (
        P(("dp", "hid"), None, "chan"),
        P(("dp", "hid"), None, "chan"),
        P("chan"),
        P("chan"),
        P(),
        P(),
        P(),
        P(),
        P("chan"),
        P("chan"),
        P(None, "hid"),
        P("hid"),
        P("hid", "chan"),
        P("chan"),
    )

    def whole(*args):
        shape = dict(mesh.shape)
        patches, token_up, chan_up = args[0].shape, args[5].shape, args[11].shape
        local = (patches[0] // (shape["dp"] * shape["hid"]), patches[1], patches[2] // shape["chan"])
        o = Sizes(shape, local, (chan_up[0], chan_up[1] // shape["hid"]), token_up)
        mapped = jax.shard_map(
            functools.partial(body, o), mesh=mesh, in_specs=in_specs, out_specs=out_specs, check_vma=False
        )
        return mapped(*args)

    return whole
```

```python
import functools

import jax
import jax.numpy as jnp
from jax import lax
from jax.experimental import pallas as pl
from jax.experimental.pallas import tpu as pltpu
from jax.sharding import PartitionSpec as P

EPS = 1e-06
BF = jnp.bfloat16
F32 = jnp.float32
MESH = pl.DeviceIdType.MESH
TANH_A = 0.7978845608028654
TANH_B = TANH_A * 0.044715


def nn(left, right):
    return lax.dot_general(left, right, (((1,), (0,)), ((), ())), preferred_element_type=F32)


def nt(left, right):
    return lax.dot_general(left, right, (((1,), (1,)), ((), ())), preferred_element_type=F32)


def tn(left, right):
    return lax.dot_general(left, right, (((0,), (0,)), ((), ())), preferred_element_type=F32)


def gelu_pair(v):
    square = v * v
    tanh = jnp.tanh(v * (TANH_A + TANH_B * square))
    half = 0.5 + 0.5 * tanh
    value = v * half
    slope = half + value * (1.0 - tanh) * (TANH_A + 3.0 * TANH_B * square)
    return value, slope


def pad_to(count, unit):
    return -(-count // unit) * unit


WAYS = {
    (0, 0): ("yxz", "nr"),
    (0, 1): ("xyz", "gr"),
    (1, 0): ("myxz", "nr"),
    (1, 1): ("xyz", "gr"),
    (2, 0): ("mzxy", "nr"),
    (2, 1): ("xyz", "gr"),
}
PLAN = {
    ("O", 0, 0): ((0, 0),),
    ("M", 0, 0): ((0, 1),),
    ("M", 1, 1): ((1, 0),),
    ("M", 2, 0): ((2, 0),),
    ("M", 2, 1): ((0, 0), (0, 0)),
    ("O", 1): ((2, 0),),
    ("O", 1, 1): ((0, 1),),
    ("O", 2, 1): ((2, 0), (1, 1), (0, 0), (1, 0)),
    ("rows",): ((2, 0),),
    ("residual",): ((1, 0), (0, 0)),
    ("outputs 0",): ((0, 1),),
    ("outputs",): ((0, 0), (2, 0)),
    ("own", 0): ((1, 0), (1, 1), (2, 1), (0, 0)),
    ("own", 2): ((2, 0), (1, 0), (0, 0), (0, 1), (1, 0), (1, 1), (2, 0)),
    ("token other",): (
        (2, 1), (1, 0), (1, 1), "small", "mixed", (2, 1), "small", (2, 0), (1, 1), (0, 1), (2, 1), "small",
        (0, 0), (1, 1), (1, 0), (2, 1),
    ),
    ("norm",): ("small", (2, 0), (0, 1), (2, 1), (1, 0), (1, 1), (0, 1), "small", (2, 1), (2, 0)),
}


class Sizes:
    def __init__(self, mesh_shape, patches, chan_up, token_up):
        self.dp = mesh_shape["dp"]
        self.hid = mesh_shape["hid"]
        self.xs = self.hid // 2
        self.images, self.s, self.l = patches
        self.ps = pad_to(self.s + 1, 16)
        self.wide = pad_to(self.ps, 128)
        self.d = 2 * self.l
        self.own = self.images // 2
        self.f = chan_up[1]
        self.ds = token_up[1]
        self.levels = self.dp.bit_length() - 1
        third = self.f // 3
        self.fetches = ((0, third), (third, 2 * third)) if self.f % 768 == 0 else ((0, self.f),)
        self.parts = tuple((n, third) for n in range(0, self.f, third)) if self.f % 768 == 0 else self.fetches
        self.units = [(part, kind) for part in range(len(self.parts)) for kind in range(2)]
        self.ways = {unit: ("xyz", "n") for unit in self.units}
        self.plan = {("O",) + unit: (unit,) for unit in self.units}
        if (self.xs, len(self.parts), self.levels) == (2, 3, 2):
            self.ways, self.plan = WAYS, PLAN
        self.chan_first = [unit for unit in self.units if self.ways[unit][0] in ("yxz", "myxz")]
        self.dp_first = [unit for unit in self.units if self.ways[unit][0] in ("zxy", "mzxy")]
        self.loads = 16
        self.plane = 2 * self.hid
        self.blocks = -(-self.f // self.l)
        self.vec_wide = max(self.f, self.l)
        groups = 3 + self.hid * self.blocks
        self.vec_row = 2 * self.ps
        self.small = pad_to(self.vec_row + 8 * groups, 64 * self.xs)
        self.groups = (self.small - self.vec_row) // 8
        self.piece = self.small // (4 * self.xs)
        assert self.own >= 3 and mesh_shape["chan"] == 2 and self.hid % 2 == 0 and self.images % 2 == 0 and self.images <= 8
        assert 1 << self.levels == self.dp and self.f % self.l == 0 and self.ds == self.l


def kernel(o, *refs):
    names = iter(refs)

    def get(count):
        return [next(names) for _ in range(count)]

    P_ = len(o.parts)
    live_hbm, patches_ref, cot_ref, tup_hbm, tdn_hbm, chan_up_ref, chan_down_ref = get(7)
    vector_hbm = get(8)
    mixed_out, grad_out, small_hbm = get(3)
    up_hbm, dn_hbm = get(P_), get(P_)
    vector_v = get(8)
    live_ref, tup_ref, tdn_ref, vec_ref, small_out = get(5)
    fin_up, fin_dn = get(P_), get(P_)
    pat, cot, cot_in, stats, stats_in, means, means2, up_s, ut_s, dn_s, dt_s, tdb_s = get(12)
    tin, th, tslope, msend, mrecv, rows_m, rows_n, inv2, vec_in = get(9)
    xs_all, gs_all, w_up, w_dn, w_b, hid_s, pg_s, out_own, ng_own, stage, ng_in, out_in = get(12)
    blow, gacc, vecs, small_send, small_c, small_p, small_in, small_z = get(8)
    (gm,) = get(1)
    gb, rx, yb, ry = get(P_), get(P_), get(P_), get(P_)
    zb, rz = dict(zip(o.units, get(2 * P_))), dict(zip(o.units, get(2 * P_)))
    ryo = {unit: next(names) for unit in o.chan_first}
    rzo = {unit: next(names) for unit in o.dp_first}
    loc_sem, send_sem, recv_sem = get(3)

    z = lax.axis_index("dp")
    y = lax.axis_index("chan")
    h = lax.axis_index("hid")
    c = h % 2
    x = h // 2
    S, PS, L, OWN, IM, X, F, N = o.s, o.ps, o.l, o.own, o.images, o.xs, o.f, o.dp
    width = float(o.d)
    here = y * o.hid + h
    bit = z % 2

    def dev(zz=None, yy=None, xx=None, cc=None):
        zz = z if zz is None else zz
        yy = y if yy is None else yy
        xx = x if xx is None else xx
        cc = c if cc is None else cc
        return (zz, yy, xx * 2 + cc)

    partner = dev(yy=1 - y)
    sibling = dev(cc=1 - c)
    z_pair = dev(zz=z + 1 - 2 * bit)
    counter = [0]

    def take(count=1):
        base = counter[0]
        counter[0] += count
        return base

    def remote(src, dst, device, index=None):
        index = take() if index is None else index
        return pltpu.make_async_remote_copy(
            src_ref=src, dst_ref=dst, send_sem=send_sem.at[index], recv_sem=recv_sem.at[index],
            device_id=device, device_id_type=MESH,
        )

    def send(src, dst, device):
        copy = remote(src, dst, device)
        copy.start()
        return copy

    barrier = pltpu.get_barrier_semaphore()
    for step in range(1, o.plane):
        there = (here + step) % o.plane
        pl.semaphore_signal(barrier, inc=1, device_id=(z, there // o.hid, there % o.hid), device_id_type=MESH)
    for step in range(1, N):
        pl.semaphore_signal(barrier, inc=1, device_id=((z + step) % N, y, h), device_id_type=MESH)

    loads = []

    def load(src, dst):
        copy = pltpu.make_async_copy(src, dst, loc_sem.at[len(loads)])
        loads.append(copy)
        copy.start()
        return copy

    stores = []

    def store(src, dst):
        copy = pltpu.make_async_copy(src, dst, loc_sem.at[o.loads + len(stores)])
        copy.start()
        stores.append(copy)

    load_vectors = [load(src, dst) for src, dst in zip(vector_hbm, vector_v)]
    load_live = load(live_hbm, live_ref)
    load_token = [load(tup_hbm, tup_ref), load(tdn_hbm, tdn_ref)]
    load_pat = load(patches_ref, pat)
    load_cot = load(cot_ref.at[pl.ds(y * OWN, OWN)], cot)
    load_up0 = load(chan_up_ref.at[pl.ds(pl.multiple_of(y * L, L), L)], w_up.at[0, pl.ds(0, L)])
    load_up1 = load(chan_up_ref.at[pl.ds(pl.multiple_of((1 - y) * L, L), L)], w_up.at[0, pl.ds(L, L)])
    load_dn = load(chan_down_ref, w_dn.at[0, :, pl.ds(0, L)])

    pad = PS - S
    pad_row = lax.broadcasted_iota(jnp.int32, (pad, L), 0)
    one_row = jnp.where(pad_row == 0, 1.0, 0.0).astype(BF)
    for j in range(IM):
        tin[j, S:PS, :] = one_row
    for i in range(OWN):
        xs_all[c, i, S:PS, :] = jnp.zeros((pad, o.d), BF)
        gs_all[c, i, S:PS, :] = jnp.zeros((pad, o.d), BF)
        rows_n[i, S:PS, :] = jnp.zeros((pad, o.d), F32)
        rows_m[i, S:PS, :] = jnp.zeros((pad, o.d), BF)
        inv2[i, S:PS, :] = jnp.zeros((pad, 1), F32)
    vecs[...] = jnp.zeros(vecs.shape, F32)
    gacc[...] = jnp.zeros(gacc.shape, F32)
    vec_ref[...] = jnp.zeros(vec_ref.shape, F32)
    for n, copy in enumerate(load_vectors):
        copy.wait()
        count = vector_v[n].shape[0]
        vec_ref[n:n + 1, :count] = vector_v[n][...].astype(F32).reshape(1, count)
    for copy in load_token:
        copy.wait()
    w_b[0, 0:1, :] = vec_ref[7:8, :]
    up_bias, down_bias_row = vec_ref[5:6, :L], vec_ref[6:7, :L]
    last = jnp.zeros((o.wide - S - 1, L), F32)
    up_full = jnp.concatenate([tup_ref[...].astype(F32), up_bias, last], 0)
    up_s[...] = up_full[:PS].astype(BF)
    ut_s[...] = up_full.T[:, :PS].astype(BF)
    dn_full = jnp.concatenate([tdn_ref[...].astype(F32), jnp.zeros((o.wide - S, L), F32)], 0)
    dn_s[...] = dn_full.T[:, :PS].astype(BF)
    dt_s[...] = dn_full[:PS].astype(BF)
    tdb_s[...] = jnp.concatenate([down_bias_row, jnp.zeros((127, L), F32)], 0).T[:PS]

    lane = lax.broadcasted_iota(jnp.int32, (S, 128), 1)
    load_pat.wait()

    def note(table, j, first, second):
        table = jnp.where(lane == j, first, table)
        return jnp.where(lane == j + 8, second, table)

    def across(table):
        rest = jnp.zeros((o.wide - S, 128), F32)
        return jnp.concatenate([table, rest], 0).T[:16]

    def along(table):
        return jnp.concatenate([table, jnp.zeros((112, o.wide), F32)], 0).T

    def sums_of(j, table):
        v = pat[j].astype(F32)
        return note(table, j, jnp.sum(v, -1, keepdims=True), jnp.sum(v * v, -1, keepdims=True))

    stats[0] = across(lax.fori_loop(0, IM, sums_of, jnp.zeros((S, 128), F32)))

    pl.semaphore_wait(barrier, o.plane - 1 + N - 1)

    copy_stats = send(stats.at[0], stats_in.at[0], partner)
    copy_vec = send(vec_ref, vec_in, partner)
    near = pl.ds(bit * L, L)
    near_from = pl.ds(pl.multiple_of(((y + bit) % 2) * L, L), L)
    copy_b = {step: send(w_b.at[0], w_b.at[step], dev(xx=(x + step) % X)) for step in range(1, X)}
    copy_w = {}
    copy_f = {}

    def weight_rows(part):
        start, size = o.fetches[part]
        return pl.ds(pl.multiple_of(start + bit * (size // 2), 16), size // 2)

    def weight_spans(step, part):
        start, size = o.fetches[part]
        cols, rows_dn = pl.ds(start, size), weight_rows(part)
        rows_own = pl.ds(start, size) if part else rows_dn
        return (
            (chan_up_ref.at[near_from, cols], w_up.at[step, near, cols], y),
            (chan_down_ref.at[rows_own], w_dn.at[step, rows_own, pl.ds(0, L)], y),
            (chan_down_ref.at[rows_dn], w_dn.at[step, rows_dn, pl.ds(L, L)], 1 - y),
        )

    def fetch(part, which):
        for step in range(1, X):
            for n in which if part < len(o.fetches) else ():
                src, dst, yy = weight_spans(step, part)[n]
                if part and n == 2:
                    src, yy = w_dn.at[0, weight_rows(part), pl.ds(L, L)], y
                copy_w[step, part, n] = send(src, dst, dev(xx=(x + step) % X, yy=yy))

    def hand_on(part, which):
        for step in range(1, X):
            for n in which if part < len(o.fetches) else ():
                dst = weight_spans(step, part)[n][1]
                if part and n == 1:
                    copy_f[step, part, n] = copy_w[step, part, n]
                else:
                    copy_w[step, part, n].wait()
                    copy_f[step, part, n] = send(dst, dst, z_pair)

    def want(group, which):
        for step in range(1, X):
            for n in which:
                copy_f[step, group, n].wait()

    quarter = F // 4
    bit2 = (z // 2) % 2
    z_far = dev(zz=z + 2 - 4 * bit2)

    def dn2_span(first, count):
        return pl.ds(pl.multiple_of(first * quarter, 16), count * quarter)

    dn2_mine = dn2_span(bit * 2 + bit2, 1)
    dn2_half = dn2_span(bit * 2, 2)
    copy_dn2 = [send(chan_down_ref.at[dn2_mine], w_dn.at[0, dn2_mine, pl.ds(L, L)], partner)]

    def dn2_on(span, peer):
        copy_dn2[-1].wait()
        ref = w_dn.at[0, span, pl.ds(L, L)]
        copy_dn2.append(send(ref, ref, peer))

    fetch(0, (0,))
    cot_sems = take(OWN)

    def copy_cot(i):
        return remote(cot_ref.at[(1 - y) * OWN + i], cot_in.at[i], partner, cot_sems + i)

    fetch(0, (1, 2))
    copy_cot(0).start()

    copy_stats.wait()
    total = (stats[0] + stats_in[0]) * (1.0 / width)
    mean, square = total[:8], total[8:]
    means[...] = along(jnp.concatenate([mean, lax.rsqrt(square - mean * mean + EPS)], 0))
    fetch(1, (0,))

    def column(table, j):
        return jnp.sum(jnp.where(lane == j, table, 0.0), -1, keepdims=True)

    first_gain = vec_ref[0:1, :L]
    first_shift = vec_ref[1:2, :L]

    def first_norm(j):
        table = means[:S, :]
        inv_one = column(table, j + 8)
        return (pat[j].astype(F32) - column(table, j)) * inv_one, inv_one

    def token_forward(j):
        normed, _ = first_norm(j)
        tin[j, :S, :] = (normed * first_gain + first_shift).astype(BF)
        value, slope = gelu_pair(nn(ut_s[...], tin[j]))
        th[j] = value.astype(BF)
        tslope[j] = slope.astype(BF)
        back = nn(dt_s[...], th[j])
        return pat[j].astype(F32) + back[:S] + tdb_s[:S, 0:1]

    mixed_sems = take(OWN)

    def copy_mixed(i):
        return remote(msend.at[i], mrecv.at[i], partner, mixed_sems + i)

    @pl.loop(0, OWN)
    def _(i):
        msend[i] = token_forward((1 - y) * OWN + i).astype(BF)
        copy_mixed(i).start()

    copy_cot(1).start()
    dn2_on(dn2_mine, z_far)
    hand_on(0, (0,))

    @pl.loop(0, OWN)
    def _(i):
        rows_n[i, :S, :L] = token_forward(y * OWN + i)

    hand_on(0, (1, 2))
    fetch(1, (1,))
    dn2_on(dn2_half, z_pair)
    copy_vec.wait()
    both = [jnp.concatenate([vec_ref[n:n + 1, :L], vec_in[n:n + 1, :L]], axis=1) for n in range(2, 5)]
    second_gain, second_shift, down_bias = both
    row_sems = take(OWN)

    def copy_rows(i):
        return remote(xs_all.at[c, i], xs_all.at[c, i], sibling, row_sems + i)

    def second_norm(i):
        copy_mixed(i).wait()
        rows_n[i, :S, L:] = mrecv[i].astype(F32)
        v = rows_n[i, :S, :]
        mean = jnp.sum(v, -1, keepdims=True) * (1.0 / width)
        spread = jnp.sum(v * v, -1, keepdims=True) * (1.0 / width) - mean * mean
        inv_two = lax.rsqrt(spread + EPS)
        normed = (v - mean) * inv_two
        rows_m[i, :S, :] = v.astype(BF)
        inv2[i, :S, :] = inv_two
        rows_n[i, :S, :] = normed
        xs_all[c, i, :S, :] = (normed * second_gain + second_shift).astype(BF)
        copy_rows(i).start()

    load_cot.wait()
    load_live.wait()
    live = live_ref[0]
    gs_sems = take(OWN)

    def keep_of(j):
        return jnp.where(j < live, 1.0, 0.0).astype(F32)

    def copy_gs(i):
        return remote(gs_all.at[c, i], gs_all.at[c, i], sibling, gs_sems + i)

    def out_grads(i):
        copy_cot(i).wait()
        keep = keep_of(y * OWN + i)
        gs_all[c, i, :S, :L] = (cot[i].astype(F32) * keep).astype(BF)
        gs_all[c, i, :S, L:] = (cot_in[i].astype(F32) * keep).astype(BF)
        copy_gs(i).start()

    rows = OWN * PS

    def inner(step, start, size, i, sums):
        cols, block = pl.ds(start, size), pl.ds(pl.multiple_of(i * PS, 16), PS)
        pre = nn(xs_all[:, i].reshape(2 * PS, o.d), w_up[step, :, cols]) + w_b[step, 0:1, cols]
        value, slope = gelu_pair(pre)
        hid_s[step, :, block, cols] = value.astype(BF).reshape(2, PS, size)
        grad = (nt(gs_all[:, i].reshape(2 * PS, o.d), w_dn[step, cols, :]) * slope).astype(BF)
        pg_s[step, :, block, cols] = grad.reshape(2, PS, size)
        return sums + jnp.sum(grad.astype(F32), 0, keepdims=True)

    def bias_sums(step, start, size, sums):
        group = 3 + ((x + X - step) % X * 2 + c) * o.blocks
        for n in range(start, start + size, 128):
            block, lanes = n // L, n % L
            vecs[group + block, 0:1, lanes:lanes + 128] = sums[:, n - start:n - start + 128]

    def own_hidden(cc, i):
        block = pl.ds(pl.multiple_of(i * PS, 16), PS)
        value, slope = gelu_pair(nn(xs_all[cc, i], w_up[0]) + w_b[0, 0:1, :])
        hid_s[0, cc, block, :] = value.astype(BF)
        for n in range(o.blocks):
            first = ((cc * o.blocks + n) * OWN + i) * PS
            gm[pl.ds(pl.multiple_of(first, 16), PS), :] = slope[:, n * L:(n + 1) * L]

    def own_back(i, sums):
        block = pl.ds(pl.multiple_of(i * PS, 16), PS)
        grad = nt(gs_all[:, i].reshape(2 * PS, o.d), w_dn[0])
        for cc in range(2):
            slopes = []
            for n in range(o.blocks):
                first = ((cc * o.blocks + n) * OWN + i) * PS
                slopes.append(gm[pl.ds(pl.multiple_of(first, 16), PS), :])
            mine = (grad[cc * PS:(cc + 1) * PS] * jnp.concatenate(slopes, 1)).astype(BF)
            pg_s[0, cc, block, :] = mine
            sums = sums + jnp.sum(mine.astype(F32), 0, keepdims=True)
        return sums

    def own_forward(i):
        own_hidden(c, i)
        copy_rows(i).wait()
        own_hidden(1 - c, i)

    def other_slots_first(i):
        for step in range(1, X):
            sums_o[step] = inner(step, start0, size0, i, sums_o[step])

    start0, size0 = o.fetches[0]
    sums_o = [jnp.zeros((1, size0), F32)] * X
    sums_m = jnp.zeros((1, F), F32)
    load_up0.wait()
    load_up1.wait()
    load_dn.wait()
    second_norm(0)
    copy_cot(2).start()
    own_forward(0)
    out_grads(0)
    second_norm(1)
    hand_on(1, (0, 1))
    own_forward(1)
    for i in range(2, OWN):
        second_norm(i)
        own_forward(i)
    want(0, (0, 1, 2))
    for step in range(1, X):
        copy_b[step].wait()
    copy_gs(0).wait()
    other_slots_first(0)
    out_grads(1)
    copy_dn2[-1].wait()
    fetch(1, (2,))
    sums_m = own_back(0, sums_m)
    copy_gs(1).wait()
    other_slots_first(1)
    for i in range(2, OWN):
        out_grads(i)
        sums_m = own_back(i - 1, sums_m)
        copy_gs(i).wait()
        other_slots_first(i)
    for step in range(1, X):
        bias_sums(step, start0, size0, sums_o[step])

    def levels():
        start, count, used = 0, N, 0
        for level in range(o.levels):
            side_bit = (z // (1 << level)) % 2
            peer = dev(zz=z + (1 - 2 * side_bit) * (1 << level))
            count //= 2
            yield start + side_bit * count, start + (1 - side_bit) * count, count, used, peer
            start = start + side_bit * count
            used += count

    def my_segment():
        return list(levels())[-1][0]

    def gm_rows(part, kind, half, span):
        start, size = o.parts[part]
        seg = size // N
        first = 4 * start + (2 * kind + half) * size
        return pl.ds(pl.multiple_of(first + span.start * seg, 8), span.size * seg)

    def gm_get(part, kind, half, span):
        seg = o.parts[part][1] // N
        return gm[gm_rows(part, kind, half, span), :].reshape(span.size, seg, L)

    def gm_set(part, kind, half, span, value):
        gm[gm_rows(part, kind, half, span), :] = value.reshape(-1, L)

    def add(part, kind, half, span, *terms):
        mine = gm_get(part, kind, half, span)
        for term in terms:
            mine = mine + term.astype(F32)
        gm_set(part, kind, half, span, mine)

    everything = pl.ds(0, N)
    low, high = pl.ds(0, N // 2), pl.ds(N // 2, N // 2)

    def finals(part, kind):
        if kind == 0:
            return [fin_up[part].at[0], fin_up[part].at[1]]
        return [fin_dn[part]]

    def reduce_rec(part, kind, halves):
        out, land = zb[part, kind], rz[part, kind]
        for keep_at, send_at, count, used, peer in levels():
            span = pl.ds(used, count)
            copies = []
            for half in range(halves):
                out[half, span] = gm_get(part, kind, half, pl.ds(send_at, count)).astype(BF)
                copies.append(send(out.at[half, span], land.at[half, span], peer))
            yield
            for half in range(halves):
                copies[half].wait()
                add(part, kind, half, pl.ds(keep_at, count), land[half, span])

    def gather_rec(part, kind):
        own = pl.ds(my_segment(), 1)
        done = finals(part, kind)
        early = kind == 0 and o.ways[part, kind][1] == "g"
        done[0][own] = gm_get(part, kind, 0, own).astype(BF)
        if early:
            copy = send(done[0].at[own], done[1].at[own], partner)
            yield
            copy.wait()
        for keep_at, _, count, _, peer in reversed(list(levels())):
            span = pl.ds(keep_at, count)
            copies = [send(ref.at[span], ref.at[span], peer) for ref in done[:1 + early]]
            yield
            for copy in copies:
                copy.wait()
        if kind == 0 and not early:
            copy = send(done[0], done[1], partner)
            yield
            copy.wait()

    def owner(n):
        return dev(xx=(x + X - 1 - n) % X)

    def start_x(part, kind):
        return [send(gb[part].at[n, kind], rx[part].at[n, kind], owner(n)) for n in range(X - 1)]

    def send_y(part, kind, span):
        yb[part][kind, span] = gm_get(part, kind, 1, span).astype(BF)
        return send(yb[part].at[kind, span], ry[part].at[kind, span], partner)

    def wait_all(copies):
        for copy in copies:
            copy.wait()

    def add_x(part, kind, half, span):
        add(part, kind, half, span, *[rx[part][n, kind, half, span] for n in range(X - 1)])

    def chunk_xyz(part, kind):
        copies = start_x(part, kind)
        yield
        wait_all(copies)
        add_x(part, kind, 1, everything)
        copy = send_y(part, kind, everything)
        add_x(part, kind, 0, everything)
        yield
        copy.wait()
        add(part, kind, 0, everything, ry[part][kind])
        yield from reduce_rec(part, kind, 1)
        yield from gather_rec(part, kind)

    def chunk_xzy(part, kind):
        copies = start_x(part, kind)
        yield
        wait_all(copies)
        add_x(part, kind, 1, everything)
        add_x(part, kind, 0, everything)
        yield from reduce_rec(part, kind, 2)
        own = pl.ds(my_segment(), 1)
        copy = send_y(part, kind, own)
        yield
        copy.wait()
        add(part, kind, 0, own, ry[part][kind, own])
        yield from gather_rec(part, kind)

    def start_yo(part, kind):
        return [send(gb[part].at[n, kind, 1], ryo[part, kind].at[n], partner) for n in range(X - 1)]

    def pass_yo(part, kind, copies):
        wait_all(copies)
        for n in range(X - 1):
            mine = gb[part][n, kind, 0].astype(F32) + ryo[part, kind][n].astype(F32)
            gb[part][n, kind, 0] = mine.astype(BF)
        return [send(gb[part].at[n, kind, 0], rx[part].at[n, kind, 0], owner(n)) for n in range(X - 1)]

    def end_yx(part, kind, copies, copy):
        copy.wait()
        wait_all(copies)
        add(part, kind, 0, everything, ry[part][kind], *[rx[part][n, kind, 0] for n in range(X - 1)])
        yield from reduce_rec(part, kind, 1)
        yield from gather_rec(part, kind)

    def chunk_yxz(part, kind):
        copies = start_yo(part, kind)
        yield
        copies = pass_yo(part, kind, copies)
        yield
        copy = send_y(part, kind, everything)
        yield
        yield from end_yx(part, kind, copies, copy)

    def chunk_myxz(part, kind):
        copy = send_y(part, kind, everything)
        yield
        copies = start_yo(part, kind)
        yield
        copies = pass_yo(part, kind, copies)
        yield
        yield from end_yx(part, kind, copies, copy)

    def reduce_others(part, kind):
        land = rzo[part, kind]
        for keep_at, send_at, count, used, peer in levels():
            copies = {}
            span = pl.ds(used, count)
            for n in range(X - 1):
                for half in range(2):
                    src = gb[part].at[n, kind, half, pl.ds(send_at, count)]
                    copies[n, half] = send(src, land.at[n, half, span], peer)
            yield
            for n in range(X - 1):
                for half in range(2):
                    copies[n, half].wait()
                    keep = pl.ds(keep_at, count)
                    mine = gb[part][n, kind, half, keep].astype(F32) + land[n, half, span].astype(F32)
                    gb[part][n, kind, half, keep] = mine.astype(BF)

    def segment_x(part, kind):
        own = pl.ds(my_segment(), 1)
        return [send(gb[part].at[n, kind, :, own], rx[part].at[n, kind, :, own], owner(n)) for n in range(X - 1)]

    def end_zx(part, kind, copies):
        own = pl.ds(my_segment(), 1)
        wait_all(copies)
        add_x(part, kind, 1, own)
        copy = send_y(part, kind, own)
        add_x(part, kind, 0, own)
        yield
        copy.wait()
        add(part, kind, 0, own, ry[part][kind, own])
        yield from gather_rec(part, kind)

    def chunk_zxy(part, kind):
        yield from reduce_others(part, kind)
        copies = segment_x(part, kind)
        yield
        yield from reduce_rec(part, kind, 2)
        yield from end_zx(part, kind, copies)

    def chunk_mzxy(part, kind):
        yield from reduce_rec(part, kind, 2)
        yield from reduce_others(part, kind)
        copies = segment_x(part, kind)
        yield
        yield from end_zx(part, kind, copies)

    chunk = {
        "xyz": chunk_xyz, "xzy": chunk_xzy, "yxz": chunk_yxz, "myxz": chunk_myxz, "zxy": chunk_zxy, "mzxy": chunk_mzxy
    }
    pipes = {unit: chunk[o.ways[unit][0]](*unit) for unit in o.units}

    def step_of(name):
        if name in pipes:
            try:
                next(pipes[name])
            except StopIteration:
                del pipes[name]
                if name == "small":
                    store(small_out, small_hbm)
                elif name != "mixed":
                    part, kind = name
                    store(*((fin_up[part], up_hbm[part]), (fin_dn[part], dn_hbm[part]))[kind])

    def at(*point):
        for name in o.plan.get(point, ()):
            step_of(name)

    def weight_grad(step, part, kind):
        start, size = o.parts[part]
        cols = pl.ds(start, size)
        left, right = (pg_s, xs_all) if kind == 0 else (hid_s, gs_all)
        grad = tn(left[step, :, :, cols].reshape(2 * rows, size), right[...].reshape(2 * rows, o.d))
        grad = grad.reshape(N, size // N, o.d)
        for half in range(2):
            block = grad[:, :, half * L:(half + 1) * L]
            if step:
                gb[part][step - 1, kind, half] = block.astype(BF)
            else:
                gm_set(part, kind, half, everything, block)

    def other_slots(group):
        start, size = o.fetches[group]
        if group:
            want(group, (0, 1, 2))
            for step in range(1, X):
                sums = lax.fori_loop(
                    0, OWN, lambda i, t, step=step: inner(step, start, size, i, t), jnp.zeros((1, size), F32)
                )
                bias_sums(step, start, size, sums)
        at("O", group)
        for part in range(P_):
            if start <= o.parts[part][0] < start + size:
                for kind in range(2):
                    for step in range(1, X):
                        weight_grad(step, part, kind)
                    if part + kind == 0:
                        hand_on(1, (2,))
                    at("O", part, kind)

    other_slots(0)
    sums_m = own_back(OWN - 1, sums_m)
    bias_sums(0, 0, F, sums_m)
    at("M")
    for part in range(P_):
        for kind in range(2):
            weight_grad(0, part, kind)
            at("M", part, kind)
    for group in range(1, len(o.fetches)):
        other_slots(group)
    at("O")

    def row_sums(kind, cc):
        left, right, dot = ((pg_s, w_up, nt), (hid_s, w_dn, nn))[kind]
        total = dot(left[0, cc], right[0])
        for step in range(1, X):
            total = total + dot(left[step, cc], right[step])
        return total

    stage[0] = row_sums(0, 1 - c).astype(BF)
    copy_ng = send(stage.at[0], ng_in, sibling)
    mine = row_sums(0, c)
    ng_own[0] = mine[:, :L]
    ng_own[1] = mine[:, L:]
    at("rows")

    res_sems = take(OWN)

    def copy_res(i):
        return remote(mrecv.at[i], blow.at[y * OWN + i], partner, res_sems + i)

    copy_ng.wait()

    def residual(i, sums):
        block = pl.ds(pl.multiple_of(i * PS, 16), PS)
        ng = jnp.concatenate([ng_own[0, block, :], ng_own[1, block, :]], 1) + ng_in[block, :].astype(F32)
        normed = rows_n[i]
        back = gs_all[c, i].astype(F32)
        sums = (
            sums[0] + jnp.sum(ng * normed, 0, keepdims=True),
            sums[1] + jnp.sum(ng, 0, keepdims=True),
            sums[2] + jnp.sum(back, 0, keepdims=True),
        )
        q = ng * second_gain
        m1 = jnp.sum(q, -1, keepdims=True) * (1.0 / width)
        m2 = jnp.sum(q * normed, -1, keepdims=True) * (1.0 / width)
        res = (back + inv2[i] * (q - m1 - normed * m2)).astype(BF)
        mrecv[i] = res[:S, L:]
        copy_res(i).start()
        blow[y * OWN + i] = res[:S, :L]
        return sums

    zero = jnp.zeros((1, o.d), F32)
    sums = lax.fori_loop(0, OWN, residual, (zero, zero, zero))
    for n in range(3):
        vecs[0, 1 + 2 * n:2 + 2 * n, :] = jnp.where(y == 0, sums[n][:, :L], sums[n][:, L:])
        vecs[0, 2 + 2 * n:3 + 2 * n, :] = jnp.where(y == 0, sums[n][:, L:], sums[n][:, :L])
    at("residual")

    stage[1] = row_sums(1, 1 - c).astype(BF)
    copy_out = send(stage.at[1], out_in, sibling)
    at("outputs 0")
    out_own[...] = row_sums(1, c)

    copy_mo = remote(msend, mixed_out.at[pl.ds(y * OWN, OWN)], partner)

    def output_rows():
        copy_out.wait()

        @pl.loop(0, OWN)
        def _(i):
            block = pl.ds(pl.multiple_of(i * PS, 16), PS)
            branch = out_own[block, :] + out_in[block, :].astype(F32) + down_bias
            result = (keep_of(y * OWN + i) * (rows_m[i].astype(F32) + branch)).astype(BF)
            msend[i] = result[:S, L:]
            cot[i] = result[:S, :L]

        copy_mo.start()
        store(cot, mixed_out.at[pl.ds(y * OWN, OWN)])
        yield

    pipes["mixed"] = output_rows()
    at("outputs")

    ones = jnp.ones((16, L), BF)

    def scaled(j):
        return j // OWN, pl.ds(pl.multiple_of(j % OWN * PS, 16), PS)

    def token_backward(j, carry):
        table, sum_gain, sum_shift, sum_bias = carry
        low_grad = blow[j]
        grad = (nn(dn_s[:, :S], low_grad) * tslope[j].astype(F32)).astype(BF)
        gacc[0] += nt(tin[j], grad)
        gacc[1, :S, :] += nt(low_grad, th[j])
        sum_bias = sum_bias + nt(ones, low_grad)
        back = nn(up_s[...], grad)
        normed, _ = first_norm(j)
        sum_gain = sum_gain + jnp.sum(back[:S] * normed, 0, keepdims=True)
        sum_shift = sum_shift + jnp.sum(back[:S], 0, keepdims=True)
        back = back * first_gain
        ng_own[scaled(j)] = back
        back = back[:S]
        table = note(table, j, jnp.sum(back, -1, keepdims=True), jnp.sum(back * normed, -1, keepdims=True))
        return table, sum_gain, sum_shift, sum_bias

    carry = (jnp.zeros((S, 128), F32), jnp.zeros((1, L), F32), jnp.zeros((1, L), F32), jnp.zeros((16, S), F32))
    for i in range(OWN):
        carry = token_backward(y * OWN + i, carry)
        at("own", i)

    for i in range(OWN):
        copy_res(i).wait()
        carry = token_backward((1 - y) * OWN + i, carry)
        if i < OWN - 1:
            at("other", i)
    table, sum_gain, sum_shift, sum_bias = carry
    stats[1] = across(table)
    copy_stats2 = send(stats.at[1], stats_in.at[1], partner)
    vecs[0, 0:1, :S] = sum_bias[0:1, :]
    vecs[1 + y, 0:1, :] = sum_gain
    vecs[1 + y, 1:2, :] = sum_shift

    half_small = o.small // 2
    spot = y * X + x
    chips = 2 * X

    def chip_peers():
        for step in range(1, chips):
            there = (spot + step) % chips
            yield step, there, dev(yy=there // X, xx=there % X)

    def piece(n):
        return pl.ds(pl.multiple_of(n * o.piece, 16), o.piece)

    def share(cc):
        return pl.ds(pl.multiple_of(cc * half_small, 16), half_small)

    def out_piece(n):
        return pl.ds(pl.multiple_of(c * half_small + n * o.piece, 16), o.piece)

    small_send[0:PS, :] = gacc[0]
    small_send[PS:2 * PS, :] = gacc[1]
    small_send[o.vec_row:, :] = vecs[...].reshape(8 * o.groups, L)

    def reduce_small():
        copy = send(small_send.at[share(1 - c)], small_c, sibling)
        yield
        copy.wait()
        small_p[...] = (small_send[share(c), :] + small_c[...]).astype(BF)
        copies = [send(small_p.at[piece(there)], small_in.at[n - 1], peer) for n, there, peer in chip_peers()]
        yield
        for copy in copies:
            copy.wait()
        mine = small_p[piece(spot), :].astype(F32)
        for n in range(1, chips):
            mine = mine + small_in[n - 1].astype(F32)
        small_z[z] = mine.astype(BF)
        copies = [send(small_z.at[z], small_z.at[z], dev(zz=(z + n) % N)) for n in range(1, N)]
        yield
        for copy in copies:
            copy.wait()
        mine = small_z[0].astype(F32)
        for n in range(1, N):
            mine = mine + small_z[n].astype(F32)
        small_out[out_piece(spot), :] = mine.astype(BF)
        span = small_out.at[out_piece(spot)]
        copies = [send(span, span, peer) for _, _, peer in chip_peers()]
        yield
        for copy in copies:
            copy.wait()
        span = small_out.at[share(c)]
        copy = send(span, span, sibling)
        yield
        copy.wait()

    pipes["small"] = reduce_small()
    step_of("small")
    at("token other")

    copy_stats2.wait()
    means2[...] = along((stats[1] + stats_in[1]) * (1.0 / width))

    @pl.loop(0, IM)
    def _(j):
        normed, inv_one = first_norm(j)
        grad = ng_own[scaled(j)][:S]
        grad = grad - column(means2[:S, :], j) - normed * column(means2[:S, :], j + 8)
        blow[j] = (blow[j].astype(F32) + inv_one * grad).astype(BF)

    store(blow, grad_out)
    at("norm")

    while pipes:
        for name in list(pipes):
            step_of(name)

    copy_mo.wait()
    for copy in stores:
        copy.wait()


def block_call(o, matrices, vectors):
    I, S, PS, L, OWN, D, X, N, F = o.images, o.s, o.ps, o.l, o.own, o.d, o.xs, o.dp, o.f
    any_spec = pl.BlockSpec(memory_space=pl.ANY)
    rows = OWN * PS
    groups = len(o.fetches)
    copies = 2 + 4 + 5 * OWN + (X - 1) * (1 + 3 * groups + 3 + 2 * (groups - 1)) + 3 + 4 * X + N - 1
    for unit in o.units:
        way, order = o.ways[unit]
        early = unit[1] == 0 and order == "g"
        copies += o.levels * (1 + early) + (unit[1] == 0) + 1 + o.levels
        if way in ("zxy", "mzxy", "xzy"):
            copies += o.levels
        copies += (X - 1) * {"xyz": 1, "xzy": 1, "yxz": 2, "myxz": 2}.get(way, 2 * o.levels + 1)
    segs = [size // N for _, size in o.parts]
    outs = [
        jax.ShapeDtypeStruct((I, S, L), BF),
        jax.ShapeDtypeStruct((I, S, L), BF),
        jax.ShapeDtypeStruct((o.small, L), BF),
    ]
    outs += [jax.ShapeDtypeStruct((2, N, seg, L), BF) for seg in segs]
    outs += [jax.ShapeDtypeStruct((N, seg, L), BF) for seg in segs]
    scratch = [(vector.shape, BF) for vector in vectors]
    scratch += [None, ((S, L), BF), ((S, L), BF), ((8, o.vec_wide), F32), ((o.small, L), BF)]
    scratch += [((2, N, seg, L), BF) for seg in segs] + [((N, seg, L), BF) for seg in segs]
    scratch += [
        ((I, S, L), BF), ((OWN, S, L), BF), ((OWN, S, L), BF),
        ((2, 16, o.wide), F32), ((2, 16, o.wide), F32),
        ((o.wide, 128), F32), ((o.wide, 128), F32),
        ((PS, L), BF), ((L, PS), BF), ((L, PS), BF), ((PS, L), BF), ((PS, 128), F32),
        ((I, PS, L), BF), ((I, o.ds, L), BF), ((I, o.ds, L), BF),
        ((OWN, S, L), BF), ((OWN, S, L), BF),
        ((OWN, PS, D), BF), ((OWN, PS, D), F32), ((OWN, PS, 1), F32), ((8, o.vec_wide), F32),
        ((2, OWN, PS, D), BF), ((2, OWN, PS, D), BF),
        ((X, D, F), BF), ((X, F, D), BF), ((X, 8, o.vec_wide), F32),
        ((X, 2, rows, F), BF), ((X, 2, rows, F), BF),
        ((rows, D), F32), ((2, rows, L), F32), ((2, rows, D), BF),
        ((rows, D), BF), ((rows, D), BF),
        ((I, S, L), BF), ((2, PS, L), F32), ((o.groups, 8, L), F32),
        ((o.small, L), F32), ((o.small // 2, L), F32), ((o.small // 2, L), BF),
        ((2 * X - 1, o.piece, L), BF), ((N, o.piece, L), BF),
    ]
    blocks = [(N, seg, L) for seg in segs]
    scratch += [((4 * F, L), F32)]
    scratch += [((X - 1, 2, 2) + block, BF) for block in blocks] * 2
    scratch += [((2,) + block, BF) for block in blocks] * 2
    for _ in range(2):
        for unit in o.units:
            halves = 1 if o.ways[unit][0] in ("xyz", "yxz", "myxz") else 2
            scratch.append(((halves,) + blocks[unit[0]], BF))
    scratch += [((X - 1,) + blocks[unit[0]], BF) for unit in o.chan_first]
    scratch += [((X - 1, 2) + blocks[unit[0]], BF) for unit in o.dp_first]
    return pl.pallas_call(
        functools.partial(kernel, o),
        out_shape=outs,
        in_specs=[any_spec] * (len(matrices) + len(vectors)),
        out_specs=[any_spec] * len(outs),
        scratch_shapes=[pltpu.VMEM(*entry) if entry else pltpu.SMEM((1,), jnp.int32) for entry in scratch]
        + [pltpu.SemaphoreType.DMA((o.loads + 3 + len(o.units),)), pltpu.SemaphoreType.DMA((copies,)), pltpu.SemaphoreType.DMA((copies,))],
        compiler_params=pltpu.CompilerParams(
            collective_id=1, has_side_effects=True, vmem_limit_bytes=63 * 2**20
        ),
        name="mixer_block",
    )(*matrices, *vectors)


def unpack(o, *refs):
    P_ = len(o.parts)
    names = iter(refs)

    def get(count):
        return [next(names) for _ in range(count)]

    inputs, outputs = get(3 + 2 * P_), get(14)
    inputs_v, outputs_v = get(3 + 2 * P_), get(12)
    in_sem, out_sem = get(2)
    S, PS, L = o.s, o.ps, o.l
    y = lax.axis_index("chan")
    h = lax.axis_index("hid")
    loads = [pltpu.make_async_copy(src, dst, in_sem.at[n]) for n, (src, dst) in enumerate(zip(inputs, inputs_v))]
    outputs_v = inputs_v[:2] + outputs_v
    stores = [pltpu.make_async_copy(src, dst, out_sem.at[n]) for n, (src, dst) in enumerate(zip(outputs_v, outputs))]
    for load in loads[3:] + loads[:3]:
        load.start()
    small_in = inputs_v[2]
    fin_up, fin_dn = inputs_v[3:3 + P_], inputs_v[3 + P_:]
    _, _, fg, fs, tu, tub, td, tdb, sg, ss, cu, cub, cd, cdb = outputs_v
    for part, (start, size) in enumerate(o.parts):
        loads[3 + part].wait()
        for half in range(2):
            block = fin_up[part][half].astype(F32).reshape(size, L).T
            cu[pl.ds(pl.multiple_of((y + half) % 2 * L, L), L), start:start + size] = block
    stores[10].start()
    for part, (start, size) in enumerate(o.parts):
        loads[3 + P_ + part].wait()
        cd[start:start + size, :] = fin_dn[part][...].astype(F32).reshape(size, L)
    stores[12].start()
    for n in range(2):
        loads[n].wait()
        stores[n].start()
    loads[2].wait()
    small = small_in[...].astype(F32)
    tu[...] = small[:S]
    tub[...] = small[S:S + 1].reshape(L)
    td[...] = small[PS:PS + S]
    groups = small[o.vec_row:].reshape(o.groups, 8, L)
    tdb[...] = groups[0, 0:1, :S].reshape(S)
    for n, ref in enumerate((sg, ss, cdb)):
        ref[...] = jnp.where(y == 0, groups[0, 1 + 2 * n:2 + 2 * n], groups[0, 2 + 2 * n:3 + 2 * n]).reshape(L)
    for n, ref in enumerate((fg, fs)):
        ref[...] = jnp.where(y == 0, groups[1, n:n + 1], groups[2, n:n + 1]).reshape(L)
    totals = []
    for n in range(o.blocks):
        total = jnp.zeros((1, L), F32)
        for k in range(o.hid):
            total = jnp.where(h == k, groups[3 + k * o.blocks + n, 0:1], total)
        totals.append(total)
    cub[...] = jnp.concatenate(totals, 1).reshape(o.f)
    for n in (2, 3, 4, 5, 6, 7, 8, 9, 11, 13):
        stores[n].start()
    for copy in stores:
        copy.wait()


def body(
    o,
    patches,
    cotangent,
    live_images,
    first_gain,
    first_shift,
    token_up,
    token_up_bias,
    token_down,
    token_down_bias,
    second_gain,
    second_shift,
    chan_up,
    chan_up_bias,
    chan_down,
    chan_down_bias,
):
    S, L, D, F = o.s, o.l, o.d, o.f
    matrices = [live_images, patches, cotangent, token_up, token_down.T, chan_up, chan_down]
    vectors = [first_gain, first_shift, second_gain, second_shift, chan_down_bias, token_up_bias, token_down_bias]
    results = block_call(o, matrices, vectors + [chan_up_bias])
    any_spec = pl.BlockSpec(memory_space=pl.ANY)
    shapes = [
        (patches.shape, BF), (patches.shape, BF), ((L,), F32), ((L,), F32), ((S, L), F32), ((L,), F32),
        ((S, L), F32), ((S,), F32), ((L,), F32), ((L,), F32), ((D, F), F32), ((F,), F32), ((F, L), F32),
        ((L,), F32),
    ]
    outs = pl.pallas_call(
        functools.partial(unpack, o),
        out_shape=[jax.ShapeDtypeStruct(shape, kind) for shape, kind in shapes],
        in_specs=[any_spec] * len(results),
        out_specs=[any_spec] * len(shapes),
        scratch_shapes=[pltpu.VMEM(result.shape, BF) for result in results]
        + [pltpu.VMEM(shape, kind) for shape, kind in shapes[2:]]
        + [pltpu.SemaphoreType.DMA((len(results),)), pltpu.SemaphoreType.DMA((len(shapes),))],
        compiler_params=pltpu.CompilerParams(vmem_limit_bytes=63 * 2**20),
        name="unpack",
    )(*results)
    return tuple(out.T if n == 6 else out for n, out in enumerate(outs))


def solution(mesh):
    in_specs = (
        P(("dp", "hid"), None, "chan"),
        P(("dp", "hid"), None, "chan"),
        P(("dp", "hid")),
        P("chan"),
        P("chan"),
        P(),
        P(),
        P(),
        P(),
        P("chan"),
        P("chan"),
        P(None, "hid"),
        P("hid"),
        P("hid", "chan"),
        P("chan"),
    )
    out_specs = (
        P(("dp", "hid"), None, "chan"),
        P(("dp", "hid"), None, "chan"),
        P("chan"),
        P("chan"),
        P(),
        P(),
        P(),
        P(),
        P("chan"),
        P("chan"),
        P(None, "hid"),
        P("hid"),
        P("hid", "chan"),
        P("chan"),
    )

    def whole(*args):
        shape = dict(mesh.shape)
        patches, token_up, chan_up = args[0].shape, args[5].shape, args[11].shape
        local = (patches[0] // (shape["dp"] * shape["hid"]), patches[1], patches[2] // shape["chan"])
        o = Sizes(shape, local, (chan_up[0], chan_up[1] // shape["hid"]), token_up)
        mapped = jax.shard_map(
            functools.partial(body, o), mesh=mesh, in_specs=in_specs, out_specs=out_specs, check_vma=False
        )
        return mapped(*args)

    return whole
```

```python
import functools

import jax
import jax.numpy as jnp
from jax import lax
from jax.experimental import pallas as pl
from jax.experimental.pallas import tpu as pltpu
from jax.sharding import PartitionSpec as P

EPS = 1e-06
BF = jnp.bfloat16
F32 = jnp.float32
MESH = pl.DeviceIdType.MESH
TANH_A = 0.7978845608028654
TANH_B = TANH_A * 0.044715


def nn(left, right):
    return lax.dot_general(left, right, (((1,), (0,)), ((), ())), preferred_element_type=F32)


def nt(left, right):
    return lax.dot_general(left, right, (((1,), (1,)), ((), ())), preferred_element_type=F32)


def tn(left, right):
    return lax.dot_general(left, right, (((0,), (0,)), ((), ())), preferred_element_type=F32)


def gelu_pair(v):
    square = v * v
    tanh = jnp.tanh(v * (TANH_A + TANH_B * square))
    half = 0.5 + 0.5 * tanh
    value = v * half
    slope = half + value * (1.0 - tanh) * (TANH_A + 3.0 * TANH_B * square)
    return value, slope


def pad_to(count, unit):
    return -(-count // unit) * unit


WAYS = {
    (0, 0): ("yxz", "g"),
    (0, 1): ("xyz", "g"),
    (1, 0): ("myxz", "n"),
    (1, 1): ("xyz", "g"),
    (2, 0): ("mzxy", "n"),
    (2, 1): ("xyz", "g"),
}
PLAN = {
    ("O", 0, 1): ((0, 0), (0, 1)),
    ("M", 2, 0): ((2, 0), (1, 0)),
    ("O", 1): ((0, 0), (0, 0), (2, 0)),
    ("O", 1, 0): ((0, 1),),
    ("O", 2, 1): ((1, 1), (2, 0), (0, 0), (1, 0)),
    ("rows",): ((0, 1), (2, 0)),
    ("residual",): ((1, 0),),
    ("outputs 0",): ((0, 0), (2, 1), (0, 1)),
    ("outputs",): ((1, 0), (2, 0), (0, 0), (1, 1)),
    ("own", 0): ((0, 1), (0, 0), (0, 1)),
    ("own", 2): ((1, 0), (2, 1)),
    ("other", 0): ((1, 1),),
    ("token other",): (
        (1, 0), (2, 0), "small", (2, 1), (1, 1), "mixed", (2, 0), (1, 0), (2, 1), "small", (1, 1), (2, 1),
        (1, 0), (2, 0), (0, 0),
    ),
    ("norm",): ("small", (2, 1), (1, 1), (0, 1), (2, 0), (2, 1), "small", (2, 0), (1, 0)),
    ("end",): ("small", (0, 0), (1, 1)),
}


class Sizes:
    def __init__(self, mesh_shape, patches, chan_up, token_up):
        self.dp = mesh_shape["dp"]
        self.hid = mesh_shape["hid"]
        self.xs = self.hid // 2
        self.images, self.s, self.l = patches
        self.ps = pad_to(self.s + 1, 16)
        self.wide = pad_to(self.ps, 128)
        self.d = 2 * self.l
        self.own = self.images // 2
        self.f = chan_up[1]
        self.ds = token_up[1]
        self.levels = self.dp.bit_length() - 1
        third = self.f // 3
        self.fetches = ((0, third), (third, 2 * third)) if self.f % 768 == 0 else ((0, self.f),)
        self.parts = tuple((n, third) for n in range(0, self.f, third)) if self.f % 768 == 0 else self.fetches
        self.units = [(part, kind) for part in range(len(self.parts)) for kind in range(2)]
        self.ways = {unit: ("xyz", "n") for unit in self.units}
        self.plan = {("O",) + unit: (unit,) for unit in self.units}
        if (self.xs, len(self.parts), self.levels) == (2, 3, 2):
            self.ways, self.plan = WAYS, PLAN
        self.chan_first = [unit for unit in self.units if self.ways[unit][0] in ("yxz", "myxz")]
        self.dp_first = [unit for unit in self.units if self.ways[unit][0] in ("zxy", "mzxy")]
        self.loads = 16
        self.plane = 2 * self.hid
        self.blocks = -(-self.f // self.l)
        self.vec_wide = max(self.f, self.l)
        groups = 3 + self.hid * self.blocks
        self.vec_row = 2 * self.ps
        self.small = pad_to(self.vec_row + 8 * groups, 64 * self.xs)
        self.groups = (self.small - self.vec_row) // 8
        self.piece = self.small // (4 * self.xs)
        assert self.own >= 3 and mesh_shape["chan"] == 2 and self.hid % 2 == 0 and self.images % 2 == 0 and self.images <= 8
        assert 1 << self.levels == self.dp and self.f % self.l == 0 and self.ds == self.l


def kernel(o, *refs):
    names = iter(refs)

    def get(count):
        return [next(names) for _ in range(count)]

    P_ = len(o.parts)
    live_hbm, patches_ref, cot_ref, tup_hbm, tdn_hbm, chan_up_ref, chan_down_ref = get(7)
    vector_hbm = get(8)
    mixed_out, grad_out, small_hbm = get(3)
    up_hbm, dn_hbm = get(P_), get(P_)
    vector_v = get(8)
    live_ref, tup_ref, tdn_ref, vec_ref, small_out = get(5)
    fin_up, fin_dn = get(P_), get(P_)
    pat, cot, cot_in, stats, stats_in, means, means2, up_s, ut_s, dn_s, dt_s, tdb_s = get(12)
    tin, th, tslope, msend, mrecv, rows_m, rows_n, inv2, vec_in = get(9)
    xs_all, gs_all, w_up, w_dn, w_b, hid_s, pg_s, out_own, ng_own, stage, ng_in, out_in = get(12)
    blow, gacc, vecs, small_send, small_c, small_p, small_in, small_z = get(8)
    (gm,) = get(1)
    gb, rx, yb, ry = get(P_), get(P_), get(P_), get(P_)
    zb, rz = dict(zip(o.units, get(2 * P_))), dict(zip(o.units, get(2 * P_)))
    ryo = {unit: next(names) for unit in o.chan_first}
    rzo = {unit: next(names) for unit in o.dp_first}
    loc_sem, send_sem, recv_sem = get(3)

    z = lax.axis_index("dp")
    y = lax.axis_index("chan")
    h = lax.axis_index("hid")
    c = h % 2
    x = h // 2
    S, PS, L, OWN, IM, X, F, N = o.s, o.ps, o.l, o.own, o.images, o.xs, o.f, o.dp
    width = float(o.d)
    here = y * o.hid + h
    bit = z % 2

    def dev(zz=None, yy=None, xx=None, cc=None):
        zz = z if zz is None else zz
        yy = y if yy is None else yy
        xx = x if xx is None else xx
        cc = c if cc is None else cc
        return (zz, yy, xx * 2 + cc)

    partner = dev(yy=1 - y)
    sibling = dev(cc=1 - c)
    z_pair = dev(zz=z + 1 - 2 * bit)
    counter = [0]

    def take(count=1):
        base = counter[0]
        counter[0] += count
        return base

    def remote(src, dst, device, index=None):
        index = take() if index is None else index
        return pltpu.make_async_remote_copy(
            src_ref=src, dst_ref=dst, send_sem=send_sem.at[index], recv_sem=recv_sem.at[index],
            device_id=device, device_id_type=MESH,
        )

    def send(src, dst, device):
        copy = remote(src, dst, device)
        copy.start()
        return copy

    barrier = pltpu.get_barrier_semaphore()
    for step in range(1, o.plane):
        there = (here + step) % o.plane
        pl.semaphore_signal(barrier, inc=1, device_id=(z, there // o.hid, there % o.hid), device_id_type=MESH)
    for step in range(1, N):
        pl.semaphore_signal(barrier, inc=1, device_id=((z + step) % N, y, h), device_id_type=MESH)

    loads = []

    def load(src, dst):
        copy = pltpu.make_async_copy(src, dst, loc_sem.at[len(loads)])
        loads.append(copy)
        copy.start()
        return copy

    stores = []

    def store(src, dst):
        copy = pltpu.make_async_copy(src, dst, loc_sem.at[o.loads + len(stores)])
        copy.start()
        stores.append(copy)

    load_vectors = [load(src, dst) for src, dst in zip(vector_hbm, vector_v)]
    load_live = load(live_hbm, live_ref)
    load_token = [load(tup_hbm, tup_ref), load(tdn_hbm, tdn_ref)]
    load_pat = load(patches_ref, pat)
    load_cot = load(cot_ref.at[pl.ds(y * OWN, OWN)], cot)
    load_up0 = load(chan_up_ref.at[pl.ds(pl.multiple_of(y * L, L), L)], w_up.at[0, pl.ds(0, L)])
    load_up1 = load(chan_up_ref.at[pl.ds(pl.multiple_of((1 - y) * L, L), L)], w_up.at[0, pl.ds(L, L)])
    load_dn = load(chan_down_ref, w_dn.at[0, :, pl.ds(0, L)])

    pad = PS - S
    pad_row = lax.broadcasted_iota(jnp.int32, (pad, L), 0)
    one_row = jnp.where(pad_row == 0, 1.0, 0.0).astype(BF)
    for j in range(IM):
        tin[j, S:PS, :] = one_row
    for i in range(OWN):
        xs_all[c, i, S:PS, :] = jnp.zeros((pad, o.d), BF)
        gs_all[c, i, S:PS, :] = jnp.zeros((pad, o.d), BF)
        rows_n[i, S:PS, :] = jnp.zeros((pad, o.d), F32)
        rows_m[i, S:PS, :] = jnp.zeros((pad, o.d), BF)
        inv2[i, S:PS, :] = jnp.zeros((pad, 1), F32)
    vecs[...] = jnp.zeros(vecs.shape, F32)
    gacc[...] = jnp.zeros(gacc.shape, F32)
    vec_ref[...] = jnp.zeros(vec_ref.shape, F32)
    for n, copy in enumerate(load_vectors):
        copy.wait()
        count = vector_v[n].shape[0]
        vec_ref[n:n + 1, :count] = vector_v[n][...].astype(F32).reshape(1, count)
    for copy in load_token:
        copy.wait()
    w_b[0, 0:1, :] = vec_ref[7:8, :]
    up_bias, down_bias_row = vec_ref[5:6, :L], vec_ref[6:7, :L]
    last = jnp.zeros((o.wide - S - 1, L), F32)
    up_full = jnp.concatenate([tup_ref[...].astype(F32), up_bias, last], 0)
    up_s[...] = up_full[:PS].astype(BF)
    ut_s[...] = up_full.T[:, :PS].astype(BF)
    dn_full = jnp.concatenate([tdn_ref[...].astype(F32), jnp.zeros((o.wide - S, L), F32)], 0)
    dn_s[...] = dn_full.T[:, :PS].astype(BF)
    dt_s[...] = dn_full[:PS].astype(BF)
    tdb_s[...] = jnp.concatenate([down_bias_row, jnp.zeros((127, L), F32)], 0).T[:PS]

    lane = lax.broadcasted_iota(jnp.int32, (S, 128), 1)
    load_pat.wait()

    def note(table, j, first, second):
        table = jnp.where(lane == j, first, table)
        return jnp.where(lane == j + 8, second, table)

    def across(table):
        rest = jnp.zeros((o.wide - S, 128), F32)
        return jnp.concatenate([table, rest], 0).T[:16]

    def along(table):
        return jnp.concatenate([table, jnp.zeros((112, o.wide), F32)], 0).T

    def sums_of(j, table):
        v = pat[j].astype(F32)
        return note(table, j, jnp.sum(v, -1, keepdims=True), jnp.sum(v * v, -1, keepdims=True))

    stats[0] = across(lax.fori_loop(0, IM, sums_of, jnp.zeros((S, 128), F32)))

    pl.semaphore_wait(barrier, o.plane - 1 + N - 1)

    copy_stats = send(stats.at[0], stats_in.at[0], partner)
    copy_vec = send(vec_ref, vec_in, partner)
    near = pl.ds(bit * L, L)
    near_from = pl.ds(pl.multiple_of(((y + bit) % 2) * L, L), L)
    copy_b = {step: send(w_b.at[0], w_b.at[step], dev(xx=(x + step) % X)) for step in range(1, X)}
    copy_w = {}
    copy_f = {}

    def weight_rows(part):
        start, size = o.fetches[part]
        return pl.ds(pl.multiple_of(start + bit * (size // 2), 16), size // 2)

    def weight_spans(step, part):
        start, size = o.fetches[part]
        cols, rows_dn = pl.ds(start, size), weight_rows(part)
        rows_own = pl.ds(start, size) if part else rows_dn
        return (
            (chan_up_ref.at[near_from, cols], w_up.at[step, near, cols], y),
            (chan_down_ref.at[rows_own], w_dn.at[step, rows_own, pl.ds(0, L)], y),
            (chan_down_ref.at[rows_dn], w_dn.at[step, rows_dn, pl.ds(L, L)], 1 - y),
        )

    def fetch(part, which):
        for step in range(1, X):
            for n in which if part < len(o.fetches) else ():
                src, dst, yy = weight_spans(step, part)[n]
                if part and n == 2:
                    src, yy = w_dn.at[0, weight_rows(part), pl.ds(L, L)], y
                copy_w[step, part, n] = send(src, dst, dev(xx=(x + step) % X, yy=yy))

    def hand_on(part, which):
        for step in range(1, X):
            for n in which if part < len(o.fetches) else ():
                dst = weight_spans(step, part)[n][1]
                if part and n == 1:
                    copy_f[step, part, n] = copy_w[step, part, n]
                else:
                    copy_w[step, part, n].wait()
                    copy_f[step, part, n] = send(dst, dst, z_pair)

    def want(group, which):
        for step in range(1, X):
            for n in which:
                copy_f[step, group, n].wait()

    quarter = F // 4
    bit2 = (z // 2) % 2
    z_far = dev(zz=z + 2 - 4 * bit2)

    def dn2_span(first, count):
        return pl.ds(pl.multiple_of(first * quarter, 16), count * quarter)

    dn2_mine = dn2_span(bit * 2 + bit2, 1)
    dn2_half = dn2_span(bit * 2, 2)
    copy_dn2 = [send(chan_down_ref.at[dn2_mine], w_dn.at[0, dn2_mine, pl.ds(L, L)], partner)]

    def dn2_on(span, peer):
        copy_dn2[-1].wait()
        ref = w_dn.at[0, span, pl.ds(L, L)]
        copy_dn2.append(send(ref, ref, peer))

    fetch(0, (0,))
    cot_sems = take(OWN)

    def copy_cot(i):
        return remote(cot_ref.at[(1 - y) * OWN + i], cot_in.at[i], partner, cot_sems + i)

    fetch(0, (1, 2))
    copy_cot(0).start()

    copy_stats.wait()
    total = (stats[0] + stats_in[0]) * (1.0 / width)
    mean, square = total[:8], total[8:]
    means[...] = along(jnp.concatenate([mean, lax.rsqrt(square - mean * mean + EPS)], 0))
    fetch(1, (0,))

    def column(table, j):
        return jnp.sum(jnp.where(lane == j, table, 0.0), -1, keepdims=True)

    first_gain = vec_ref[0:1, :L]
    first_shift = vec_ref[1:2, :L]

    def first_norm(j):
        table = means[:S, :]
        inv_one = column(table, j + 8)
        return (pat[j].astype(F32) - column(table, j)) * inv_one, inv_one

    def token_forward(j):
        normed, _ = first_norm(j)
        tin[j, :S, :] = (normed * first_gain + first_shift).astype(BF)
        value, slope = gelu_pair(nn(ut_s[...], tin[j]))
        th[j] = value.astype(BF)
        tslope[j] = slope.astype(BF)
        back = nn(dt_s[...], th[j])
        return pat[j].astype(F32) + back[:S] + tdb_s[:S, 0:1]

    mixed_sems = take(OWN)

    def copy_mixed(i):
        return remote(msend.at[i], mrecv.at[i], partner, mixed_sems + i)

    @pl.loop(0, OWN)
    def _(i):
        msend[i] = token_forward((1 - y) * OWN + i).astype(BF)
        copy_mixed(i).start()

    copy_cot(1).start()
    dn2_on(dn2_mine, z_far)
    hand_on(0, (0,))

    @pl.loop(0, OWN)
    def _(i):
        rows_n[i, :S, :L] = token_forward(y * OWN + i)

    hand_on(0, (1, 2))
    fetch(1, (1,))
    dn2_on(dn2_half, z_pair)
    copy_vec.wait()
    both = [jnp.concatenate([vec_ref[n:n + 1, :L], vec_in[n:n + 1, :L]], axis=1) for n in range(2, 5)]
    second_gain, second_shift, down_bias = both
    row_sems = take(OWN)

    def copy_rows(i):
        return remote(xs_all.at[c, i], xs_all.at[c, i], sibling, row_sems + i)

    def second_norm(i):
        copy_mixed(i).wait()
        rows_n[i, :S, L:] = mrecv[i].astype(F32)
        v = rows_n[i, :S, :]
        mean = jnp.sum(v, -1, keepdims=True) * (1.0 / width)
        spread = jnp.sum(v * v, -1, keepdims=True) * (1.0 / width) - mean * mean
        inv_two = lax.rsqrt(spread + EPS)
        normed = (v - mean) * inv_two
        rows_m[i, :S, :] = v.astype(BF)
        inv2[i, :S, :] = inv_two
        rows_n[i, :S, :] = normed
        xs_all[c, i, :S, :] = (normed * second_gain + second_shift).astype(BF)
        copy_rows(i).start()

    load_cot.wait()
    load_live.wait()
    live = live_ref[0]
    gs_sems = take(OWN)

    def keep_of(j):
        return jnp.where(j < live, 1.0, 0.0).astype(F32)

    def copy_gs(i):
        return remote(gs_all.at[c, i], gs_all.at[c, i], sibling, gs_sems + i)

    def out_grads(i):
        copy_cot(i).wait()
        keep = keep_of(y * OWN + i)
        gs_all[c, i, :S, :L] = (cot[i].astype(F32) * keep).astype(BF)
        gs_all[c, i, :S, L:] = (cot_in[i].astype(F32) * keep).astype(BF)
        copy_gs(i).start()

    rows = OWN * PS

    def inner(step, start, size, i, sums):
        cols, block = pl.ds(start, size), pl.ds(pl.multiple_of(i * PS, 16), PS)
        pre = nn(xs_all[:, i].reshape(2 * PS, o.d), w_up[step, :, cols]) + w_b[step, 0:1, cols]
        value, slope = gelu_pair(pre)
        hid_s[step, :, block, cols] = value.astype(BF).reshape(2, PS, size)
        grad = (nt(gs_all[:, i].reshape(2 * PS, o.d), w_dn[step, cols, :]) * slope).astype(BF)
        pg_s[step, :, block, cols] = grad.reshape(2, PS, size)
        return sums + jnp.sum(grad.astype(F32), 0, keepdims=True)

    def bias_sums(step, start, size, sums):
        group = 3 + ((x + X - step) % X * 2 + c) * o.blocks
        for n in range(start, start + size, 128):
            block, lanes = n // L, n % L
            vecs[group + block, 0:1, lanes:lanes + 128] = sums[:, n - start:n - start + 128]

    def own_hidden(cc, i):
        block = pl.ds(pl.multiple_of(i * PS, 16), PS)
        value, slope = gelu_pair(nn(xs_all[cc, i], w_up[0]) + w_b[0, 0:1, :])
        hid_s[0, cc, block, :] = value.astype(BF)
        for n in range(o.blocks):
            first = ((cc * o.blocks + n) * OWN + i) * PS
            gm[pl.ds(pl.multiple_of(first, 16), PS), :] = slope[:, n * L:(n + 1) * L]

    def own_back(i, sums):
        block = pl.ds(pl.multiple_of(i * PS, 16), PS)
        grad = nt(gs_all[:, i].reshape(2 * PS, o.d), w_dn[0])
        for cc in range(2):
            slopes = []
            for n in range(o.blocks):
                first = ((cc * o.blocks + n) * OWN + i) * PS
                slopes.append(gm[pl.ds(pl.multiple_of(first, 16), PS), :])
            mine = (grad[cc * PS:(cc + 1) * PS] * jnp.concatenate(slopes, 1)).astype(BF)
            pg_s[0, cc, block, :] = mine
            sums = sums + jnp.sum(mine.astype(F32), 0, keepdims=True)
        return sums

    def own_forward(i):
        own_hidden(c, i)
        copy_rows(i).wait()
        own_hidden(1 - c, i)

    def other_slots_first(i):
        for step in range(1, X):
            sums_o[step] = inner(step, start0, size0, i, sums_o[step])

    start0, size0 = o.fetches[0]
    sums_o = [jnp.zeros((1, size0), F32)] * X
    sums_m = jnp.zeros((1, F), F32)
    load_up0.wait()
    load_up1.wait()
    load_dn.wait()
    second_norm(0)
    copy_cot(2).start()
    own_forward(0)
    out_grads(0)
    second_norm(1)
    hand_on(1, (0, 1))
    own_forward(1)
    for i in range(2, OWN):
        second_norm(i)
        own_forward(i)
    want(0, (0, 1, 2))
    for step in range(1, X):
        copy_b[step].wait()
    copy_gs(0).wait()
    other_slots_first(0)
    out_grads(1)
    copy_dn2[-1].wait()
    fetch(1, (2,))
    sums_m = own_back(0, sums_m)
    copy_gs(1).wait()
    other_slots_first(1)
    for i in range(2, OWN):
        out_grads(i)
        sums_m = own_back(i - 1, sums_m)
        copy_gs(i).wait()
        other_slots_first(i)
    for step in range(1, X):
        bias_sums(step, start0, size0, sums_o[step])

    def levels():
        start, count, used = 0, N, 0
        for level in range(o.levels):
            side_bit = (z // (1 << level)) % 2
            peer = dev(zz=z + (1 - 2 * side_bit) * (1 << level))
            count //= 2
            yield start + side_bit * count, start + (1 - side_bit) * count, count, used, peer
            start = start + side_bit * count
            used += count

    def my_segment():
        return list(levels())[-1][0]

    def gm_rows(part, kind, half, span):
        start, size = o.parts[part]
        seg = size // N
        first = 4 * start + (2 * kind + half) * size
        return pl.ds(pl.multiple_of(first + span.start * seg, 8), span.size * seg)

    def gm_get(part, kind, half, span):
        seg = o.parts[part][1] // N
        return gm[gm_rows(part, kind, half, span), :].reshape(span.size, seg, L)

    def gm_set(part, kind, half, span, value):
        gm[gm_rows(part, kind, half, span), :] = value.reshape(-1, L)

    def add(part, kind, half, span, *terms):
        mine = gm_get(part, kind, half, span)
        for term in terms:
            mine = mine + term.astype(F32)
        gm_set(part, kind, half, span, mine)

    everything = pl.ds(0, N)
    low, high = pl.ds(0, N // 2), pl.ds(N // 2, N // 2)

    def finals(part, kind):
        if kind == 0:
            return [fin_up[part].at[0], fin_up[part].at[1]]
        return [fin_dn[part]]

    def reduce_rec(part, kind, halves):
        out, land = zb[part, kind], rz[part, kind]
        for keep_at, send_at, count, used, peer in levels():
            span = pl.ds(used, count)
            copies = []
            for half in range(halves):
                out[half, span] = gm_get(part, kind, half, pl.ds(send_at, count)).astype(BF)
                copies.append(send(out.at[half, span], land.at[half, span], peer))
            yield
            for half in range(halves):
                copies[half].wait()
                add(part, kind, half, pl.ds(keep_at, count), land[half, span])

    def gather_rec(part, kind):
        own = pl.ds(my_segment(), 1)
        done = finals(part, kind)
        early = kind == 0 and o.ways[part, kind][1] == "g"
        done[0][own] = gm_get(part, kind, 0, own).astype(BF)
        if early:
            copy = send(done[0].at[own], done[1].at[own], partner)
            yield
            copy.wait()
        for keep_at, _, count, _, peer in reversed(list(levels())):
            span = pl.ds(keep_at, count)
            copies = [send(ref.at[span], ref.at[span], peer) for ref in done[:1 + early]]
            yield
            for copy in copies:
                copy.wait()
        if kind == 0 and not early:
            copy = send(done[0], done[1], partner)
            yield
            copy.wait()

    def owner(n):
        return dev(xx=(x + X - 1 - n) % X)

    def start_x(part, kind):
        return [send(gb[part].at[n, kind], rx[part].at[n, kind], owner(n)) for n in range(X - 1)]

    def send_y(part, kind, span):
        yb[part][kind, span] = gm_get(part, kind, 1, span).astype(BF)
        return send(yb[part].at[kind, span], ry[part].at[kind, span], partner)

    def wait_all(copies):
        for copy in copies:
            copy.wait()

    def add_x(part, kind, half, span):
        add(part, kind, half, span, *[rx[part][n, kind, half, span] for n in range(X - 1)])

    def chunk_xyz(part, kind):
        copies = start_x(part, kind)
        yield
        wait_all(copies)
        add_x(part, kind, 1, everything)
        copy = send_y(part, kind, everything)
        add_x(part, kind, 0, everything)
        yield
        copy.wait()
        add(part, kind, 0, everything, ry[part][kind])
        yield from reduce_rec(part, kind, 1)
        yield from gather_rec(part, kind)

    def chunk_xzy(part, kind):
        copies = start_x(part, kind)
        yield
        wait_all(copies)
        add_x(part, kind, 1, everything)
        add_x(part, kind, 0, everything)
        yield from reduce_rec(part, kind, 2)
        own = pl.ds(my_segment(), 1)
        copy = send_y(part, kind, own)
        yield
        copy.wait()
        add(part, kind, 0, own, ry[part][kind, own])
        yield from gather_rec(part, kind)

    def start_yo(part, kind):
        return [send(gb[part].at[n, kind, 1], ryo[part, kind].at[n], partner) for n in range(X - 1)]

    def pass_yo(part, kind, copies):
        wait_all(copies)
        for n in range(X - 1):
            mine = gb[part][n, kind, 0].astype(F32) + ryo[part, kind][n].astype(F32)
            gb[part][n, kind, 0] = mine.astype(BF)
        return [send(gb[part].at[n, kind, 0], rx[part].at[n, kind, 0], owner(n)) for n in range(X - 1)]

    def end_yx(part, kind, copies, copy):
        copy.wait()
        wait_all(copies)
        add(part, kind, 0, everything, ry[part][kind], *[rx[part][n, kind, 0] for n in range(X - 1)])
        yield from reduce_rec(part, kind, 1)
        yield from gather_rec(part, kind)

    def chunk_yxz(part, kind):
        copies = start_yo(part, kind)
        yield
        copies = pass_yo(part, kind, copies)
        yield
        copy = send_y(part, kind, everything)
        yield
        yield from end_yx(part, kind, copies, copy)

    def chunk_myxz(part, kind):
        copy = send_y(part, kind, everything)
        yield
        copies = start_yo(part, kind)
        yield
        copies = pass_yo(part, kind, copies)
        yield
        yield from end_yx(part, kind, copies, copy)

    def reduce_others(part, kind):
        land = rzo[part, kind]
        for keep_at, send_at, count, used, peer in levels():
            copies = {}
            span = pl.ds(used, count)
            for n in range(X - 1):
                for half in range(2):
                    src = gb[part].at[n, kind, half, pl.ds(send_at, count)]
                    copies[n, half] = send(src, land.at[n, half, span], peer)
            yield
            for n in range(X - 1):
                for half in range(2):
                    copies[n, half].wait()
                    keep = pl.ds(keep_at, count)
                    mine = gb[part][n, kind, half, keep].astype(F32) + land[n, half, span].astype(F32)
                    gb[part][n, kind, half, keep] = mine.astype(BF)

    def segment_x(part, kind):
        own = pl.ds(my_segment(), 1)
        return [send(gb[part].at[n, kind, :, own], rx[part].at[n, kind, :, own], owner(n)) for n in range(X - 1)]

    def end_zx(part, kind, copies):
        own = pl.ds(my_segment(), 1)
        wait_all(copies)
        add_x(part, kind, 1, own)
        copy = send_y(part, kind, own)
        add_x(part, kind, 0, own)
        yield
        copy.wait()
        add(part, kind, 0, own, ry[part][kind, own])
        yield from gather_rec(part, kind)

    def chunk_zxy(part, kind):
        yield from reduce_others(part, kind)
        copies = segment_x(part, kind)
        yield
        yield from reduce_rec(part, kind, 2)
        yield from end_zx(part, kind, copies)

    def chunk_mzxy(part, kind):
        yield from reduce_rec(part, kind, 2)
        yield from reduce_others(part, kind)
        copies = segment_x(part, kind)
        yield
        yield from end_zx(part, kind, copies)

    chunk = {
        "xyz": chunk_xyz, "xzy": chunk_xzy, "yxz": chunk_yxz, "myxz": chunk_myxz, "zxy": chunk_zxy, "mzxy": chunk_mzxy
    }
    pipes = {unit: chunk[o.ways[unit][0]](*unit) for unit in o.units}

    def step_of(name):
        if name in pipes:
            try:
                next(pipes[name])
            except StopIteration:
                del pipes[name]
                if name == "small":
                    store(small_out, small_hbm)
                elif name != "mixed":
                    part, kind = name
                    store(*((fin_up[part], up_hbm[part]), (fin_dn[part], dn_hbm[part]))[kind])

    def at(*point):
        for name in o.plan.get(point, ()):
            step_of(name)

    def weight_grad(step, part, kind):
        start, size = o.parts[part]
        cols = pl.ds(start, size)
        left, right = (pg_s, xs_all) if kind == 0 else (hid_s, gs_all)
        grad = tn(left[step, :, :, cols].reshape(2 * rows, size), right[...].reshape(2 * rows, o.d))
        grad = grad.reshape(N, size // N, o.d)
        for half in range(2):
            block = grad[:, :, half * L:(half + 1) * L]
            if step:
                gb[part][step - 1, kind, half] = block.astype(BF)
            else:
                gm_set(part, kind, half, everything, block)

    def other_slots(group):
        start, size = o.fetches[group]
        if group:
            want(group, (0, 1, 2))
            for step in range(1, X):
                sums = lax.fori_loop(
                    0, OWN, lambda i, t, step=step: inner(step, start, size, i, t), jnp.zeros((1, size), F32)
                )
                bias_sums(step, start, size, sums)
        at("O", group)
        for part in range(P_):
            if start <= o.parts[part][0] < start + size:
                for kind in range(2):
                    for step in range(1, X):
                        weight_grad(step, part, kind)
                    if part + kind == 0:
                        hand_on(1, (2,))
                    at("O", part, kind)

    other_slots(0)
    sums_m = own_back(OWN - 1, sums_m)
    bias_sums(0, 0, F, sums_m)
    at("M")
    for part in range(P_):
        for kind in range(2):
            weight_grad(0, part, kind)
            at("M", part, kind)
    for group in range(1, len(o.fetches)):
        other_slots(group)
    at("O")

    def row_sums(kind, cc):
        left, right, dot = ((pg_s, w_up, nt), (hid_s, w_dn, nn))[kind]
        total = dot(left[0, cc], right[0])
        for step in range(1, X):
            total = total + dot(left[step, cc], right[step])
        return total

    stage[0] = row_sums(0, 1 - c).astype(BF)
    copy_ng = send(stage.at[0], ng_in, sibling)
    mine = row_sums(0, c)
    ng_own[0] = mine[:, :L]
    ng_own[1] = mine[:, L:]
    at("rows")

    res_sems = take(OWN)

    def copy_res(i):
        return remote(mrecv.at[i], blow.at[y * OWN + i], partner, res_sems + i)

    copy_ng.wait()

    def residual(i, sums):
        block = pl.ds(pl.multiple_of(i * PS, 16), PS)
        ng = jnp.concatenate([ng_own[0, block, :], ng_own[1, block, :]], 1) + ng_in[block, :].astype(F32)
        normed = rows_n[i]
        back = gs_all[c, i].astype(F32)
        sums = (
            sums[0] + jnp.sum(ng * normed, 0, keepdims=True),
            sums[1] + jnp.sum(ng, 0, keepdims=True),
            sums[2] + jnp.sum(back, 0, keepdims=True),
        )
        q = ng * second_gain
        m1 = jnp.sum(q, -1, keepdims=True) * (1.0 / width)
        m2 = jnp.sum(q * normed, -1, keepdims=True) * (1.0 / width)
        res = (back + inv2[i] * (q - m1 - normed * m2)).astype(BF)
        mrecv[i] = res[:S, L:]
        copy_res(i).start()
        blow[y * OWN + i] = res[:S, :L]
        return sums

    zero = jnp.zeros((1, o.d), F32)
    sums = lax.fori_loop(0, OWN, residual, (zero, zero, zero))
    for n in range(3):
        vecs[0, 1 + 2 * n:2 + 2 * n, :] = jnp.where(y == 0, sums[n][:, :L], sums[n][:, L:])
        vecs[0, 2 + 2 * n:3 + 2 * n, :] = jnp.where(y == 0, sums[n][:, L:], sums[n][:, :L])
    at("residual")

    stage[1] = row_sums(1, 1 - c).astype(BF)
    copy_out = send(stage.at[1], out_in, sibling)
    at("outputs 0")
    out_own[...] = row_sums(1, c)

    copy_mo = remote(msend, mixed_out.at[pl.ds(y * OWN, OWN)], partner)

    def output_rows():
        copy_out.wait()

        @pl.loop(0, OWN)
        def _(i):
            block = pl.ds(pl.multiple_of(i * PS, 16), PS)
            branch = out_own[block, :] + out_in[block, :].astype(F32) + down_bias
            result = (keep_of(y * OWN + i) * (rows_m[i].astype(F32) + branch)).astype(BF)
            msend[i] = result[:S, L:]
            cot[i] = result[:S, :L]

        copy_mo.start()
        store(cot, mixed_out.at[pl.ds(y * OWN, OWN)])
        yield

    pipes["mixed"] = output_rows()
    at("outputs")

    ones = jnp.ones((16, L), BF)

    def scaled(j):
        return j // OWN, pl.ds(pl.multiple_of(j % OWN * PS, 16), PS)

    def token_backward(j, carry):
        table, sum_gain, sum_shift, sum_bias = carry
        low_grad = blow[j]
        grad = (nn(dn_s[:, :S], low_grad) * tslope[j].astype(F32)).astype(BF)
        gacc[0] += nt(tin[j], grad)
        gacc[1, :S, :] += nt(low_grad, th[j])
        sum_bias = sum_bias + nt(ones, low_grad)
        back = nn(up_s[...], grad)
        normed, _ = first_norm(j)
        sum_gain = sum_gain + jnp.sum(back[:S] * normed, 0, keepdims=True)
        sum_shift = sum_shift + jnp.sum(back[:S], 0, keepdims=True)
        back = back * first_gain
        ng_own[scaled(j)] = back
        back = back[:S]
        table = note(table, j, jnp.sum(back, -1, keepdims=True), jnp.sum(back * normed, -1, keepdims=True))
        return table, sum_gain, sum_shift, sum_bias

    carry = (jnp.zeros((S, 128), F32), jnp.zeros((1, L), F32), jnp.zeros((1, L), F32), jnp.zeros((16, S), F32))
    for i in range(OWN):
        carry = token_backward(y * OWN + i, carry)
        at("own", i)

    for i in range(OWN):
        copy_res(i).wait()
        carry = token_backward((1 - y) * OWN + i, carry)
        if i < OWN - 1:
            at("other", i)
    table, sum_gain, sum_shift, sum_bias = carry
    stats[1] = across(table)
    copy_stats2 = send(stats.at[1], stats_in.at[1], partner)
    vecs[0, 0:1, :S] = sum_bias[0:1, :]
    vecs[1 + y, 0:1, :] = sum_gain
    vecs[1 + y, 1:2, :] = sum_shift

    half_small = o.small // 2
    spot = y * X + x
    chips = 2 * X

    def chip_peers():
        for step in range(1, chips):
            there = (spot + step) % chips
            yield step, there, dev(yy=there // X, xx=there % X)

    def piece(n):
        return pl.ds(pl.multiple_of(n * o.piece, 16), o.piece)

    def share(cc):
        return pl.ds(pl.multiple_of(cc * half_small, 16), half_small)

    def out_piece(n):
        return pl.ds(pl.multiple_of(c * half_small + n * o.piece, 16), o.piece)

    small_send[0:PS, :] = gacc[0]
    small_send[PS:2 * PS, :] = gacc[1]
    small_send[o.vec_row:, :] = vecs[...].reshape(8 * o.groups, L)

    def reduce_small():
        copy = send(small_send.at[share(1 - c)], small_c, sibling)
        yield
        copy.wait()
        small_p[...] = (small_send[share(c), :] + small_c[...]).astype(BF)
        copies = [send(small_p.at[piece(there)], small_in.at[n - 1], peer) for n, there, peer in chip_peers()]
        yield
        for copy in copies:
            copy.wait()
        mine = small_p[piece(spot), :].astype(F32)
        for n in range(1, chips):
            mine = mine + small_in[n - 1].astype(F32)
        small_z[z] = mine.astype(BF)
        copies = [send(small_z.at[z], small_z.at[z], dev(zz=(z + n) % N)) for n in range(1, N)]
        yield
        for copy in copies:
            copy.wait()
        mine = small_z[0].astype(F32)
        for n in range(1, N):
            mine = mine + small_z[n].astype(F32)
        small_out[out_piece(spot), :] = mine.astype(BF)
        span = small_out.at[out_piece(spot)]
        copies = [send(span, span, peer) for _, _, peer in chip_peers()]
        yield
        for copy in copies:
            copy.wait()
        span = small_out.at[share(c)]
        copy = send(span, span, sibling)
        yield
        copy.wait()

    pipes["small"] = reduce_small()
    step_of("small")
    at("token other")

    copy_stats2.wait()
    means2[...] = along((stats[1] + stats_in[1]) * (1.0 / width))

    @pl.loop(0, IM)
    def _(j):
        normed, inv_one = first_norm(j)
        grad = ng_own[scaled(j)][:S]
        grad = grad - column(means2[:S, :], j) - normed * column(means2[:S, :], j + 8)
        blow[j] = (blow[j].astype(F32) + inv_one * grad).astype(BF)

    store(blow, grad_out)
    at("norm")

    while pipes:
        for name in list(pipes):
            step_of(name)

    copy_mo.wait()
    for copy in stores:
        copy.wait()


def block_call(o, matrices, vectors):
    I, S, PS, L, OWN, D, X, N, F = o.images, o.s, o.ps, o.l, o.own, o.d, o.xs, o.dp, o.f
    any_spec = pl.BlockSpec(memory_space=pl.ANY)
    rows = OWN * PS
    groups = len(o.fetches)
    copies = 2 + 4 + 5 * OWN + (X - 1) * (1 + 3 * groups + 3 + 2 * (groups - 1)) + 3 + 4 * X + N - 1
    for unit in o.units:
        way, order = o.ways[unit]
        early = unit[1] == 0 and order == "g"
        copies += o.levels * (1 + early) + (unit[1] == 0) + 1 + o.levels
        if way in ("zxy", "mzxy", "xzy"):
            copies += o.levels
        copies += (X - 1) * {"xyz": 1, "xzy": 1, "yxz": 2, "myxz": 2}.get(way, 2 * o.levels + 1)
    segs = [size // N for _, size in o.parts]
    outs = [
        jax.ShapeDtypeStruct((I, S, L), BF),
        jax.ShapeDtypeStruct((I, S, L), BF),
        jax.ShapeDtypeStruct((o.small, L), BF),
    ]
    outs += [jax.ShapeDtypeStruct((2, N, seg, L), BF) for seg in segs]
    outs += [jax.ShapeDtypeStruct((N, seg, L), BF) for seg in segs]
    scratch = [(vector.shape, BF) for vector in vectors]
    scratch += [None, ((S, L), BF), ((S, L), BF), ((8, o.vec_wide), F32), ((o.small, L), BF)]
    scratch += [((2, N, seg, L), BF) for seg in segs] + [((N, seg, L), BF) for seg in segs]
    scratch += [
        ((I, S, L), BF), ((OWN, S, L), BF), ((OWN, S, L), BF),
        ((2, 16, o.wide), F32), ((2, 16, o.wide), F32),
        ((o.wide, 128), F32), ((o.wide, 128), F32),
        ((PS, L), BF), ((L, PS), BF), ((L, PS), BF), ((PS, L), BF), ((PS, 128), F32),
        ((I, PS, L), BF), ((I, o.ds, L), BF), ((I, o.ds, L), BF),
        ((OWN, S, L), BF), ((OWN, S, L), BF),
        ((OWN, PS, D), BF), ((OWN, PS, D), F32), ((OWN, PS, 1), F32), ((8, o.vec_wide), F32),
        ((2, OWN, PS, D), BF), ((2, OWN, PS, D), BF),
        ((X, D, F), BF), ((X, F, D), BF), ((X, 8, o.vec_wide), F32),
        ((X, 2, rows, F), BF), ((X, 2, rows, F), BF),
        ((rows, D), F32), ((2, rows, L), F32), ((2, rows, D), BF),
        ((rows, D), BF), ((rows, D), BF),
        ((I, S, L), BF), ((2, PS, L), F32), ((o.groups, 8, L), F32),
        ((o.small, L), F32), ((o.small // 2, L), F32), ((o.small // 2, L), BF),
        ((2 * X - 1, o.piece, L), BF), ((N, o.piece, L), BF),
    ]
    blocks = [(N, seg, L) for seg in segs]
    scratch += [((4 * F, L), F32)]
    scratch += [((X - 1, 2, 2) + block, BF) for block in blocks] * 2
    scratch += [((2,) + block, BF) for block in blocks] * 2
    for _ in range(2):
        for unit in o.units:
            halves = 1 if o.ways[unit][0] in ("xyz", "yxz", "myxz") else 2
            scratch.append(((halves,) + blocks[unit[0]], BF))
    scratch += [((X - 1,) + blocks[unit[0]], BF) for unit in o.chan_first]
    scratch += [((X - 1, 2) + blocks[unit[0]], BF) for unit in o.dp_first]
    return pl.pallas_call(
        functools.partial(kernel, o),
        out_shape=outs,
        in_specs=[any_spec] * (len(matrices) + len(vectors)),
        out_specs=[any_spec] * len(outs),
        scratch_shapes=[pltpu.VMEM(*entry) if entry else pltpu.SMEM((1,), jnp.int32) for entry in scratch]
        + [pltpu.SemaphoreType.DMA((o.loads + 3 + len(o.units),)), pltpu.SemaphoreType.DMA((copies,)), pltpu.SemaphoreType.DMA((copies,))],
        compiler_params=pltpu.CompilerParams(
            collective_id=1, has_side_effects=True, vmem_limit_bytes=63 * 2**20
        ),
        name="mixer_block",
    )(*matrices, *vectors)


def unpack(o, *refs):
    P_ = len(o.parts)
    names = iter(refs)

    def get(count):
        return [next(names) for _ in range(count)]

    inputs, outputs = get(3 + 2 * P_), get(14)
    inputs_v, outputs_v = get(3 + 2 * P_), get(12)
    in_sem, out_sem = get(2)
    S, PS, L = o.s, o.ps, o.l
    y = lax.axis_index("chan")
    h = lax.axis_index("hid")
    loads = [pltpu.make_async_copy(src, dst, in_sem.at[n]) for n, (src, dst) in enumerate(zip(inputs, inputs_v))]
    outputs_v = inputs_v[:2] + outputs_v
    stores = [pltpu.make_async_copy(src, dst, out_sem.at[n]) for n, (src, dst) in enumerate(zip(outputs_v, outputs))]
    for load in loads[3:] + loads[:3]:
        load.start()
    small_in = inputs_v[2]
    fin_up, fin_dn = inputs_v[3:3 + P_], inputs_v[3 + P_:]
    _, _, fg, fs, tu, tub, td, tdb, sg, ss, cu, cub, cd, cdb = outputs_v
    for part, (start, size) in enumerate(o.parts):
        loads[3 + part].wait()
        for half in range(2):
            block = fin_up[part][half].astype(F32).reshape(size, L).T
            cu[pl.ds(pl.multiple_of((y + half) % 2 * L, L), L), start:start + size] = block
    stores[10].start()
    for part, (start, size) in enumerate(o.parts):
        loads[3 + P_ + part].wait()
        cd[start:start + size, :] = fin_dn[part][...].astype(F32).reshape(size, L)
    stores[12].start()
    for n in range(2):
        loads[n].wait()
        stores[n].start()
    loads[2].wait()
    small = small_in[...].astype(F32)
    tu[...] = small[:S]
    tub[...] = small[S:S + 1].reshape(L)
    td[...] = small[PS:PS + S]
    groups = small[o.vec_row:].reshape(o.groups, 8, L)
    tdb[...] = groups[0, 0:1, :S].reshape(S)
    for n, ref in enumerate((sg, ss, cdb)):
        ref[...] = jnp.where(y == 0, groups[0, 1 + 2 * n:2 + 2 * n], groups[0, 2 + 2 * n:3 + 2 * n]).reshape(L)
    for n, ref in enumerate((fg, fs)):
        ref[...] = jnp.where(y == 0, groups[1, n:n + 1], groups[2, n:n + 1]).reshape(L)
    totals = []
    for n in range(o.blocks):
        total = jnp.zeros((1, L), F32)
        for k in range(o.hid):
            total = jnp.where(h == k, groups[3 + k * o.blocks + n, 0:1], total)
        totals.append(total)
    cub[...] = jnp.concatenate(totals, 1).reshape(o.f)
    for n in (2, 3, 4, 5, 6, 7, 8, 9, 11, 13):
        stores[n].start()
    for copy in stores:
        copy.wait()


def body(
    o,
    patches,
    cotangent,
    live_images,
    first_gain,
    first_shift,
    token_up,
    token_up_bias,
    token_down,
    token_down_bias,
    second_gain,
    second_shift,
    chan_up,
    chan_up_bias,
    chan_down,
    chan_down_bias,
):
    S, L, D, F = o.s, o.l, o.d, o.f
    matrices = [live_images, patches, cotangent, token_up, token_down.T, chan_up, chan_down]
    vectors = [first_gain, first_shift, second_gain, second_shift, chan_down_bias, token_up_bias, token_down_bias]
    results = block_call(o, matrices, vectors + [chan_up_bias])
    any_spec = pl.BlockSpec(memory_space=pl.ANY)
    shapes = [
        (patches.shape, BF), (patches.shape, BF), ((L,), F32), ((L,), F32), ((S, L), F32), ((L,), F32),
        ((S, L), F32), ((S,), F32), ((L,), F32), ((L,), F32), ((D, F), F32), ((F,), F32), ((F, L), F32),
        ((L,), F32),
    ]
    outs = pl.pallas_call(
        functools.partial(unpack, o),
        out_shape=[jax.ShapeDtypeStruct(shape, kind) for shape, kind in shapes],
        in_specs=[any_spec] * len(results),
        out_specs=[any_spec] * len(shapes),
        scratch_shapes=[pltpu.VMEM(result.shape, BF) for result in results]
        + [pltpu.VMEM(shape, kind) for shape, kind in shapes[2:]]
        + [pltpu.SemaphoreType.DMA((len(results),)), pltpu.SemaphoreType.DMA((len(shapes),))],
        compiler_params=pltpu.CompilerParams(vmem_limit_bytes=63 * 2**20),
        name="unpack",
    )(*results)
    return tuple(out.T if n == 6 else out for n, out in enumerate(outs))


def solution(mesh):
    in_specs = (
        P(("dp", "hid"), None, "chan"),
        P(("dp", "hid"), None, "chan"),
        P(("dp", "hid")),
        P("chan"),
        P("chan"),
        P(),
        P(),
        P(),
        P(),
        P("chan"),
        P("chan"),
        P(None, "hid"),
        P("hid"),
        P("hid", "chan"),
        P("chan"),
    )
    out_specs = (
        P(("dp", "hid"), None, "chan"),
        P(("dp", "hid"), None, "chan"),
        P("chan"),
        P("chan"),
        P(),
        P(),
        P(),
        P(),
        P("chan"),
        P("chan"),
        P(None, "hid"),
        P("hid"),
        P("hid", "chan"),
        P("chan"),
    )

    def whole(*args):
        shape = dict(mesh.shape)
        patches, token_up, chan_up = args[0].shape, args[5].shape, args[11].shape
        local = (patches[0] // (shape["dp"] * shape["hid"]), patches[1], patches[2] // shape["chan"])
        o = Sizes(shape, local, (chan_up[0], chan_up[1] // shape["hid"]), token_up)
        mapped = jax.shard_map(
            functools.partial(body, o), mesh=mesh, in_specs=in_specs, out_specs=out_specs, check_vma=False
        )
        return mapped(*args)

    return whole
```
